256 devices in a mesh: loss: 32 (over y, z_hi, core), dp: 8 (over z_lo, x).
Axes of the slice: x: 4, y: 4, z: 8 (z_hi: 4, z_lo: 2; z = z_hi * 2 + z_lo), core: 2. Of those that a mesh axis runs over, the one named last changes fastest.
Arguments:
- picture_pooled_features: bfloat16 [8, 4096, 1152], P('dp', 'loss'), may hold values from -6 to 6
- sentence_pooled_features: bfloat16 [8, 4096, 1152], P('dp', 'loss'), may hold values from -6 to 6
- description_keys: int32 [8, 4096], P('dp', 'loss'), may hold values from 0 to 8191
- picture_projection_weights: bfloat16 [1152, 1152], replicated, may hold values from -0.1875 to 0.1875
- sentence_projection_weights: bfloat16 [1152, 1152], replicated, may hold values from -0.1875 to 0.1875
- learned_inverse_heat_exponent: float32 [1], replicated, may hold values from 1.5 to 2.3
- learned_shift_amount: float32 [1], replicated, may hold values from -3 to -1
Outputs:
- grad_w_img: float32 [1152, 1152], P('loss', 'dp')
- grad_w_txt: float32 [1152, 1152], P('loss', 'dp')
- statistics: float32 [3], replicated
The draws below stay inside these ranges and needn't reach their ends.
All inputs are finite; a program needn't handle non-finite values.
Results may differ from the reference program's by a relative error of at most 0.0048.
Values may be sent and summed in bfloat16 or wider, within the bound.
No kernel may reach another device: no remote copies, remote signals or barrier semaphores. Data moves between devices by JAX's collectives and lax.ppermute only.
A program may use at most 128 MiB of HBM per device.

```python
import math
import jax
import jax.numpy as jnp
import numpy as np
from jax import lax

D = 1152
PAIRS_DEV = 128
PAIRS = 4096
N_LOSS = 32
N_DP = 8


def with_ends(entries, key, smallest, top_value):
    shape = entries.shape
    place = [jax.random.randint(jax.random.fold_in(key, axis), (), 0, shape[axis]) for axis in range(len(shape))]
    entries = entries.at[tuple(place)].set(smallest)
    longest = shape.index(max(shape))
    place[longest] = (place[longest] + 1) % shape[longest]
    return entries.at[tuple(place)].set(top_value)


def steps_of(own_key, extent, pieces, smallest, high):
    def one(dim, parts):
        heights = jax.random.uniform(jax.random.fold_in(jax.random.fold_in(own_key, 6), dim), (parts,), jnp.float32, smallest / len(pieces), high / len(pieces))
        return jnp.repeat(jnp.exp(heights), extent[dim] // parts).reshape((-1,) + (1,) * (len(extent) - dim - 1))

    factor_of = one(*pieces[0])
    for cut in pieces[1:]:
        factor_of = factor_of * one(*cut)
    return factor_of


def rank_bounds(amount, slope):
    weights = [(1 << 20) // math.isqrt(grade ** slope) + 1 for grade in range(1, amount + 1)]
    deviation = 1 + sum(weights) // (1 << 30)
    return np.cumsum(np.array([max(1, weight // deviation) for weight in weights]))


def skewed_ids(key, dims, number_of, lean):
    table = rank_bounds(number_of, lean)
    lot = jax.random.randint(jax.random.fold_in(key, 1), dims, 0, int(table[number_of - 1]))
    grade = jnp.searchsorted(jnp.asarray(table, jnp.int32), lot, side="right")
    return jax.random.permutation(jax.random.fold_in(key, 2), number_of)[grade].astype(jnp.int32)


def scatter_about(own_key, extent, deviation, limit, shards=(), kind=jnp.bfloat16):
    result = deviation * jax.random.normal(own_key, extent, jnp.float32)
    if shards:
        result = result * steps_of(own_key, extent, shards, -0.22, 0.18)
    return jnp.clip(result, -limit, limit).astype(kind)


def setup_inputs(seed: int = 0) -> dict:
    splits = jax.random.split(jax.random.key(seed), 8)
    return {
        "picture_pooled_features": scatter_about(splits[0], (N_DP, PAIRS, D), 1.0, 6.0, ((0, 8), (1, 32))),
        "sentence_pooled_features": scatter_about(splits[1], (N_DP, PAIRS, D), 1.0, 6.0, ((0, 8), (1, 32))),
        "description_keys": with_ends(skewed_ids(splits[2], (N_DP, PAIRS), 8192, 2), jax.random.fold_in(splits[2], 3), 0, 8191).astype(jnp.int32),
        "picture_projection_weights": scatter_about(splits[3], (D, D), D ** -0.5, 0.1875),
        "sentence_projection_weights": scatter_about(splits[4], (D, D), D ** -0.5, 0.1875),
        "learned_inverse_heat_exponent": jnp.clip(jax.random.uniform(splits[5], (1,), jnp.float32, 1.5, 2.3), 1.5, 2.3),
        "learned_shift_amount": jnp.clip(jax.random.uniform(splits[6], (1,), jnp.float32, -3.0, -1.0), -3.0, -1.0),
    }


epsilon = 1e-06

def project_rows(features, weight):
    projected = jnp.dot(features, weight, preferred_element_type=jnp.float32)
    lengths = jnp.sqrt(lax.optimization_barrier(jnp.sum(projected * projected, axis=1, keepdims=True)) + epsilon)
    return (projected / lengths, lengths)

def peer_block_routine(picture_vector_entries, sentence_vector_entries, picture_description_keys, sentence_description_keys, heat_multiplier, start_position):
    similarity_entries = jnp.dot(picture_vector_entries, sentence_vector_entries.T, preferred_element_type=jnp.float32)
    similarity_grid = heat_multiplier * similarity_entries + start_position
    labels = jnp.where(picture_description_keys[:, None] == sentence_description_keys[None, :], 1.0, -1.0).astype(jnp.float32)
    margins = -labels * similarity_grid
    row_count = picture_vector_entries.shape[0]
    objective_accumulated_sum = jnp.sum(jax.nn.softplus(margins)) / row_count
    derivative_collection = -labels * jax.nn.sigmoid(margins) / row_count
    return (objective_accumulated_sum, derivative_collection, jnp.sum(derivative_collection * heat_multiplier * similarity_entries), jnp.sum(derivative_collection))

def reference(picture_pooled_features, sentence_pooled_features, description_keys, picture_projection_weights, sentence_projection_weights, learned_inverse_heat_exponent, learned_shift_amount):
    heat_multiplier = jnp.exp(learned_inverse_heat_exponent[0])
    start_position = learned_shift_amount[0]
    bit_count = N_LOSS.bit_length() - 1

    def replica(inputs):
        img_rows, txt_rows, ids_all = inputs
        img_full, img_len = project_rows(img_rows, picture_projection_weights)
        txt_full, txt_len = project_rows(txt_rows, sentence_projection_weights)
        img_blocks = img_full.astype(jnp.bfloat16).reshape(N_LOSS, PAIRS_DEV, D)
        txt_blocks = txt_full.astype(jnp.bfloat16).reshape(N_LOSS, PAIRS_DEV, D)
        id_blocks = ids_all.reshape(N_LOSS, PAIRS_DEV)

        def one_block(block_index):
            own_picture_vectors = img_blocks[block_index]
            own_sentence_vectors = txt_blocks[block_index]
            own_description_keys = id_blocks[block_index]
            objective_accumulated_sum, derivative_collection, heat_derivative, shift_derivative = peer_block_routine(own_picture_vectors, own_sentence_vectors, own_description_keys, own_description_keys, heat_multiplier, start_position)
            derivative_narrow_float = derivative_collection.astype(jnp.bfloat16)
            picture_derivative = heat_multiplier * jnp.dot(derivative_narrow_float, own_sentence_vectors, preferred_element_type=jnp.float32)
            sentence_derivative = heat_multiplier * jnp.dot(derivative_narrow_float.T, own_picture_vectors, preferred_element_type=jnp.float32)
            for bit_number in range(bit_count):
                partner = jnp.bitwise_xor(block_index, jnp.int32(1 << bit_number)).astype(jnp.int32)
                peer_sentence_vectors = txt_blocks[partner]
                peer_picture_vectors = img_blocks[partner]
                peer_description_keys = id_blocks[partner]
                block_objective_amount, block_derivative_collection, block_heat_derivative, block_shift_derivative = peer_block_routine(own_picture_vectors, peer_sentence_vectors, own_description_keys, peer_description_keys, heat_multiplier, start_position)
                objective_accumulated_sum = objective_accumulated_sum + block_objective_amount
                heat_derivative = heat_derivative + block_heat_derivative
                shift_derivative = shift_derivative + block_shift_derivative
                picture_derivative = picture_derivative + heat_multiplier * jnp.dot(block_derivative_collection.astype(jnp.bfloat16), peer_sentence_vectors, preferred_element_type=jnp.float32)
                discarded_output, reverse_mode_derivatives, discarded_output, discarded_output = peer_block_routine(peer_picture_vectors, own_sentence_vectors, peer_description_keys, own_description_keys, heat_multiplier, start_position)
                objective_piece = (heat_multiplier * jnp.dot(reverse_mode_derivatives.astype(jnp.bfloat16).T, peer_picture_vectors, preferred_element_type=jnp.float32)).astype(jnp.bfloat16)
                sentence_derivative = sentence_derivative + lax.optimization_barrier(objective_piece).astype(jnp.float32)
            return (picture_derivative, sentence_derivative, jnp.stack([objective_accumulated_sum, heat_derivative, shift_derivative]))
        img_grads, txt_grads, running_counts = lax.map(one_block, jnp.arange(N_LOSS, dtype=jnp.int32))
        img_grads = img_grads.reshape(PAIRS_DEV * N_LOSS, D)
        txt_grads = txt_grads.reshape(PAIRS_DEV * N_LOSS, D)
        img_dir = ((img_grads - img_full * lax.optimization_barrier(jnp.sum(img_full * img_grads, axis=1, keepdims=True))) / img_len).astype(jnp.bfloat16)
        txt_dir = ((txt_grads - txt_full * lax.optimization_barrier(jnp.sum(txt_full * txt_grads, axis=1, keepdims=True))) / txt_len).astype(jnp.bfloat16)
        head_img = jnp.dot(img_rows.T, img_dir, preferred_element_type=jnp.float32)
        head_txt = jnp.dot(txt_rows.T, txt_dir, preferred_element_type=jnp.float32)
        return (head_img, head_txt, lax.optimization_barrier(jnp.sum(running_counts, axis=0)))
    heads_img, heads_txt, running_counts = lax.map(replica, (picture_pooled_features, sentence_pooled_features, description_keys))
    grouped = N_LOSS * N_DP
    return (lax.optimization_barrier(jnp.sum(heads_img, axis=0)), lax.optimization_barrier(jnp.sum(heads_txt, axis=0)), lax.optimization_barrier(jnp.sum(running_counts, axis=0)) / grouped)
```

```python
import jax
import jax.numpy as jnp
from jax import lax
from jax.sharding import Mesh, PartitionSpec as P

epsilon = 1e-06
LOSS = ("ly", "lz", "lc")


def exchange(array, axis, apart):
    return lax.ppermute(array, axis, [(i, i ^ apart) for i in range(lax.axis_size(axis))])


def project_rows(features, weight):
    projected = jnp.dot(features, weight, preferred_element_type=jnp.float32)
    lengths = jnp.sqrt(jnp.sum(projected * projected, axis=1, keepdims=True) + epsilon)
    return projected / lengths, lengths


def three_parts(values):
    high = values.astype(jnp.bfloat16)
    rest = values - high.astype(jnp.float32)
    middle = rest.astype(jnp.bfloat16)
    low = (rest - middle.astype(jnp.float32)).astype(jnp.bfloat16)
    return jnp.concatenate([high, middle, low])


def tile_terms(similarity, same, heat, shift, rows):
    logits = heat * similarity + shift
    labels = jnp.where(same, 1.0, -1.0).astype(jnp.float32)
    margins = -labels * logits
    gradient = -labels * jax.nn.sigmoid(margins) / rows
    return margins, gradient


def nt(a, b):
    return lax.dot_general(a, b, (((1,), (1,)), ((), ())), preferred_element_type=jnp.float32)


def tn(a, b):
    return lax.dot_general(a, b, (((0,), (0,)), ((), ())), preferred_element_type=jnp.float32)


def tangent(total, unit, length):
    inner = jnp.sum(unit * total, axis=1, keepdims=True)
    return ((total - unit * inner) / length).astype(jnp.bfloat16)


def body(pictures, sentences, keys, picture_weights, sentence_weights, heat_log, shift_value):
    rows, width = pictures.shape[1:]
    ways = lax.axis_size("dp")
    heat = jnp.exp(heat_log[0])
    shift = shift_value[0]
    own_keys = keys[0]
    own = jnp.concatenate([pictures[0], sentences[0]], axis=0)

    bits = [("lz", 2), ("lz", 1), ("ly", 2), ("ly", 1), ("lc", 1)]
    near_keys = [exchange(own_keys, axis, apart) for axis, apart in bits]
    near = [exchange(own, axis, apart) for axis, apart in bits]
    gathered = lax.all_gather(own, "dp", axis=0)

    img_unit, img_len = project_rows(own[:rows], picture_weights)
    txt_unit, txt_len = project_rows(own[rows:], sentence_weights)
    img_vec = [img_unit.astype(jnp.bfloat16)]
    txt_vec = [txt_unit.astype(jnp.bfloat16)]
    for block in reversed(near):
        img_vec.append(project_rows(block[:rows], picture_weights)[0].astype(jnp.bfloat16))
        txt_vec.append(project_rows(block[rows:], sentence_weights)[0].astype(jnp.bfloat16))
    all_keys = jnp.concatenate([own_keys] + near_keys[::-1])
    all_img = jnp.concatenate(img_vec, axis=0)
    all_txt = jnp.concatenate(txt_vec, axis=0)
    same = own_keys[:, None] == all_keys[None, :]

    similarity = nt(img_vec[0], all_txt)
    margins, gradient = tile_terms(similarity, same, heat, shift, rows)
    numbers = jnp.stack(
        [
            jnp.sum(jax.nn.softplus(margins)) / rows,
            jnp.sum(gradient * heat * similarity),
            jnp.sum(gradient),
        ]
    )
    img_total = heat * jnp.dot(
        gradient.astype(jnp.bfloat16), all_txt, preferred_element_type=jnp.float32
    )
    back_similarity = nt(txt_vec[0], all_img)
    _, back_gradient = tile_terms(back_similarity, same, heat, shift, rows)
    txt_total = heat * jnp.dot(
        back_gradient.astype(jnp.bfloat16), all_img, preferred_element_type=jnp.float32
    )
    img_dir = tangent(img_total, img_unit, img_len)
    txt_dir = tangent(txt_total, txt_unit, txt_len)

    cols = width // ways
    spread = jnp.concatenate(
        [img_dir.T.reshape(ways, cols, rows), txt_dir.T.reshape(ways, cols, rows)], axis=1
    )
    extra = jnp.zeros((16, rows), jnp.bfloat16).at[0, :9].set(three_parts(numbers))
    spread = jnp.concatenate([spread, jnp.broadcast_to(extra, (ways, 16, rows))], axis=1)
    spread = lax.all_to_all(spread, "dp", 0, 0, tiled=True)
    numbers = jnp.sum(
        jnp.sum(spread[:, 2 * cols, :9].astype(jnp.float32), axis=0).reshape(3, 3), axis=0
    )

    def head(features, directions):
        return lax.dot_general(
            features,
            directions,
            (((0, 1), (0, 2)), ((), ())),
            preferred_element_type=jnp.float32,
        )

    heads = jnp.concatenate(
        [
            head(gathered[:, :rows], spread[:, :cols]),
            head(gathered[:, rows:], spread[:, cols : 2 * cols]),
        ],
        axis=1,
    )
    quads = lax.axis_size("ly") * lax.axis_size("lz")
    part = width // (2 * quads)
    heads = heads.reshape(quads, 2, part, 2 * cols)
    core = lax.axis_index("lc")
    kept = jnp.where(core == 0, heads[:, 0], heads[:, 1])
    given = jnp.where(core == 0, heads[:, 1], heads[:, 0]).astype(jnp.bfloat16)
    number_row = jnp.zeros((1, 1, 2 * cols), jnp.bfloat16)
    mine = number_row.at[0, 0, :9].set(three_parts(numbers))
    given = jnp.concatenate([given, jnp.broadcast_to(mine, (quads, 1, 2 * cols))], axis=1)
    taken = exchange(given, "lc", 1).astype(jnp.float32)
    numbers = numbers + jnp.sum(taken[0, part, :9].reshape(3, 3), axis=0)
    both = number_row.at[0, 0, :9].set(three_parts(numbers))
    kept = (kept + taken[:, :part]).astype(jnp.bfloat16)
    kept = jnp.concatenate([kept, jnp.broadcast_to(both, (quads, 1, 2 * cols))], axis=1)
    kept = lax.all_to_all(kept, ("ly", "lz"), 0, 0, tiled=True)
    sums = jnp.sum(kept.astype(jnp.float32), axis=0)
    statistics = jnp.sum(sums[part, :9].reshape(3, 3), axis=0) / (2 * quads * ways)
    return sums[:part, :cols], sums[:part, cols:], statistics


def solution(mesh):
    split = Mesh(mesh.devices.reshape(4, 4, 2, 8), ("ly", "lz", "lc", "dp"))
    return jax.shard_map(
        body,
        mesh=split,
        in_specs=(P("dp", LOSS, None), P("dp", LOSS, None), P("dp", LOSS), P(), P(), P(), P()),
        out_specs=(P(LOSS, "dp"), P(LOSS, "dp"), P()),
        check_vma=False,
    )
```

```python
import functools

import jax
import jax.numpy as jnp
from jax import lax
from jax.experimental import pallas as pl
from jax.experimental.pallas import tpu as pltpu
from jax.sharding import Mesh, PartitionSpec as P

EPSILON = 1e-06
LOSS = ("ly", "lz", "lc")
ROWS = 128
WIDTH = 1152
KEY_ROWS = 16
CHUNK = 36
SLOT = 40
COLS = 144
LANES = 128
TAIL = COLS - LANES
QUADS = 16
F32 = jnp.float32
BF16 = jnp.bfloat16

VMEM = pl.BlockSpec(memory_space=pltpu.VMEM)
SMEM = pl.BlockSpec(memory_space=pltpu.SMEM)


def params():
    return pltpu.CompilerParams(vmem_limit_bytes=40 * 2**20)


def cost(flops, moved):
    return pl.CostEstimate(flops=flops, bytes_accessed=moved, transcendentals=0)


def exchange(array, axis, apart):
    return lax.ppermute(array, axis, [(i, i ^ apart) for i in range(lax.axis_size(axis))])


def after(array, *others):
    return lax.optimization_barrier((array, *others))[0]


def nt(a, b):
    return lax.dot_general(a, b, (((1,), (1,)), ((), ())), preferred_element_type=F32)


def mm(a, b):
    return jnp.dot(a, b, preferred_element_type=F32)


def project_kernel(x_ref, w_ref, key_ref, out_ref, unit_ref, len_ref, acc):
    step = pl.program_id(0)

    @pl.when(step == 0)
    def _():
        acc[...] = jnp.zeros_like(acc)

    acc[...] += mm(x_ref[...], w_ref[...])

    @pl.when(step == pl.num_programs(0) - 1)
    def _():
        u = acc[...]
        length = jnp.sqrt(jnp.sum(u * u, axis=1, keepdims=True) + EPSILON)
        unit = u / length
        unit_ref[...] = unit
        out_ref[:ROWS, :] = unit.astype(BF16)
        out_ref[ROWS:, :] = key_ref[...]
        len_ref[...] = jnp.broadcast_to(length, len_ref.shape)


def project(x, w, keys):
    depth = 384
    return pl.pallas_call(
        project_kernel,
        grid=(WIDTH // depth,),
        in_specs=[
            pl.BlockSpec((ROWS, depth), lambda k: (0, k)),
            pl.BlockSpec((depth, WIDTH), lambda k: (k, 0)),
            pl.BlockSpec((KEY_ROWS, WIDTH), lambda k: (0, 0)),
        ],
        out_specs=[
            pl.BlockSpec((ROWS + KEY_ROWS, WIDTH), lambda k: (0, 0)),
            pl.BlockSpec((ROWS, WIDTH), lambda k: (0, 0)),
            pl.BlockSpec((ROWS, LANES), lambda k: (0, 0)),
        ],
        out_shape=[
            jax.ShapeDtypeStruct((ROWS + KEY_ROWS, WIDTH), BF16),
            jax.ShapeDtypeStruct((ROWS, WIDTH), F32),
            jax.ShapeDtypeStruct((ROWS, LANES), F32),
        ],
        scratch_shapes=[pltpu.VMEM((ROWS, WIDTH), F32)],
        compiler_params=params(),
        cost_estimate=cost(2 * ROWS * WIDTH * WIDTH, 4 * 2**20),
    )(x, w, keys)


def tile_kernel(with_stats, ways, scal, own, unit, length, own_key, *refs):
    blocks, out = refs[:-1], refs[-1]
    heat, shift = scal[0], scal[1]
    mine = own[:ROWS, :]
    key_col = own_key[:, :1]
    total = jnp.zeros((ROWS, WIDTH), F32)
    loss_acc = jnp.zeros((ROWS, ROWS), F32)
    heat_acc = jnp.zeros((ROWS, ROWS), F32)
    grad_acc = jnp.zeros((ROWS, ROWS), F32)
    for block in blocks:
        vec = block[:ROWS, :]
        keys = block[ROWS:, :LANES].astype(F32)
        key_row = keys[0:1] * 128.0 + keys[1:2]
        same = key_col == key_row
        sim = nt(mine, vec)
        logits = heat * sim + shift
        z = jnp.where(same, -logits, logits)
        t = jnp.exp(-jnp.abs(z))
        q = 1.0 / (1.0 + t)
        sig = jnp.where(z >= 0, q, t * q)
        g = jnp.where(same, -sig, sig) * (1.0 / ROWS)
        total += mm(g.astype(BF16), vec)
        if with_stats:
            loss_acc += jnp.maximum(z, 0.0) + jnp.log1p(t)
            heat_acc += g * sim
            grad_acc += g
    total = total * heat
    u = unit[...]
    inner = jnp.sum(u * total, axis=1, keepdims=True)
    du = (total - u * inner) / length[:, :1]
    flipped = du.T.astype(BF16)
    for w in range(ways):
        for h in range(2):
            start = h * ways * COLS + w * COLS
            out[w, h * COLS : (h + 1) * COLS, :] = flipped[start : start + COLS]
    if with_stats:
        def full(x):
            return jnp.sum(jnp.sum(x, axis=1, keepdims=True), axis=0, keepdims=True)

        lane = lax.broadcasted_iota(jnp.int32, (KEY_ROWS, LANES), 1)
        row = lax.broadcasted_iota(jnp.int32, (KEY_ROWS, LANES), 0)
        kind = lane % 3
        value = jnp.where(
            kind == 0,
            full(loss_acc) * (1.0 / ROWS),
            jnp.where(kind == 1, full(heat_acc) * heat, full(grad_acc)),
        )
        value = jnp.where((row == 0) & (lane < 9), value, 0.0)
        high = value.astype(BF16).astype(F32)
        middle = (value - high).astype(BF16).astype(F32)
        low = value - high - middle
        parts = jnp.where(lane < 3, high, jnp.where(lane < 6, middle, low)).astype(BF16)
        for w in range(ways):
            out[w, 2 * COLS :, :] = parts


def tiles(with_stats, ways, scal, own, unit, length, own_key, blocks):
    rows = 2 * COLS + (KEY_ROWS if with_stats else 0)
    return pl.pallas_call(
        functools.partial(tile_kernel, with_stats, ways),
        in_specs=[SMEM] + [VMEM] * (4 + len(blocks)),
        out_specs=VMEM,
        out_shape=jax.ShapeDtypeStruct((ways, rows, ROWS), BF16),
        compiler_params=params(),
        cost_estimate=cost(4 * 6 * ROWS * ROWS * WIDTH, 8 * 2**20),
    )(scal, own, unit, length, own_key, *blocks)


def head_kernel(with_stats, core, feat, spread, kept, given):
    ways = feat.shape[0]
    total = jnp.zeros((2 * COLS, feat.shape[2]), F32)
    for w in range(ways):
        total += mm(spread[w, : 2 * COLS, :], feat[w])
    half = QUADS * SLOT
    kept[...] = jnp.zeros_like(kept)
    given[...] = jnp.zeros_like(given)
    for h in range(2):
        main = total[h * COLS : h * COLS + LANES, :].T
        rest = total[h * COLS + LANES : (h + 1) * COLS, :]
        for side, out in enumerate((kept, given)):
            for m in range(QUADS):
                start = side * half + m * SLOT
                out[2 * m + h, :SLOT, :] = main[start : start + SLOT].astype(BF16)
                out[2 * m + h, 48:, :SLOT] = rest[:, start : start + SLOT].astype(BF16)
    if with_stats:
        parts = jnp.zeros((KEY_ROWS, LANES), F32)
        for w in range(ways):
            parts += spread[w, 2 * COLS :, :].astype(F32)
        lane = lax.broadcasted_iota(jnp.int32, (8, LANES), 1)
        row = lax.broadcasted_iota(jnp.int32, (8, LANES), 0)
        sums = parts[0:1]
        summed = jnp.zeros((8, LANES), F32)
        for k in range(3):
            number = jnp.sum(
                jnp.where((lane[:1] % 3 == k) & (lane[:1] < 9), sums, 0.0), axis=1, keepdims=True
            )
            summed = jnp.where(lane % 3 == k, number, summed)
        value = jnp.where((row == core[0]) & (lane < 9), summed, 0.0)
        high = value.astype(BF16).astype(F32)
        middle = (value - high).astype(BF16).astype(F32)
        low = value - high - middle
        spare = jnp.where(lane < 3, high, jnp.where(lane < 6, middle, low)).astype(BF16)
        for m in range(2 * QUADS):
            kept[m, SLOT:48, :] = spare
            given[m, SLOT:48, :] = spare


def heads(with_stats, core, feat, spread):
    shape = jax.ShapeDtypeStruct((2 * QUADS, 64, LANES), BF16)
    return pl.pallas_call(
        functools.partial(head_kernel, with_stats),
        in_specs=[SMEM, VMEM, VMEM],
        out_specs=[VMEM, VMEM],
        out_shape=[shape, shape],
        compiler_params=params(),
        cost_estimate=cost(2 * feat.shape[0] * ROWS * 2 * COLS * feat.shape[2], 4 * 2**20),
    )(core, feat, spread)


def final_kernel(count, parts, out, stats):
    total = jnp.sum(parts[...].astype(F32), axis=0)
    out[:, :LANES] = total[:CHUNK]
    rest = total[48:, :].T
    out[:, LANES:] = rest[:CHUNK, :]
    lane = lax.broadcasted_iota(jnp.int32, (1, LANES), 1)
    row = total[SLOT : SLOT + 1] + total[SLOT + 1 : SLOT + 2]
    answer = jnp.zeros((1, LANES), F32)
    for k in range(3):
        number = jnp.sum(jnp.where((lane % 3 == k) & (lane < 9), row, 0.0), axis=1, keepdims=True)
        answer = jnp.where(lane == k, number, answer)
    stats[...] = answer * (1.0 / count)


def final(count, parts):
    return pl.pallas_call(
        functools.partial(final_kernel, count),
        in_specs=[VMEM],
        out_specs=[VMEM, VMEM],
        out_shape=[
            jax.ShapeDtypeStruct((CHUNK, COLS), F32),
            jax.ShapeDtypeStruct((1, LANES), F32),
        ],
        compiler_params=params(),
        cost_estimate=cost(2 * QUADS * 64 * LANES, 2**20),
    )(parts)


def body(pictures, sentences, keys, picture_weights, sentence_weights, heat_log, shift_value):
    ways = lax.axis_size("dx")
    core = lax.axis_index("lc")
    scal = jnp.stack([jnp.exp(heat_log[0]), shift_value[0]])
    key = keys[0]
    key_rows = jnp.zeros((KEY_ROWS, WIDTH), BF16)
    key_rows = key_rows.at[0, :ROWS].set((key >> 7).astype(BF16))
    key_rows = key_rows.at[1, :ROWS].set((key & 127).astype(BF16))
    key_col = jnp.broadcast_to(key.astype(F32)[:, None], (ROWS, LANES))

    txt, txt_unit, txt_len = project(sentences[0], sentence_weights, key_rows)
    txt_a = exchange(txt, "lz", 1)
    txt_y2 = exchange(txt, "ly", 2)
    txt_y1 = exchange(txt, "ly", 1)
    txt_c = exchange(txt, "lc", 1)
    txt_b = exchange(txt_a, "lz", 3)

    img, img_unit, img_len = project(pictures[0], picture_weights, key_rows)
    img_a = exchange(after(img, txt_a), "lz", 1)
    img_n = after(img, txt_y1, txt_y2)
    img_y2 = exchange(img_n, "ly", 2)
    img_y1 = exchange(img_n, "ly", 1)
    img_c = exchange(img_n, "lc", 1)
    img_b = exchange(img_a, "lz", 3)

    slot = lax.broadcasted_iota(jnp.int32, (1, 2 * QUADS * SLOT), 1)
    side, place = slot // (QUADS * SLOT), slot % (QUADS * SLOT)
    chunk = 2 * (place // SLOT) + jnp.where(core == 0, side, 1 - side)
    within = place % SLOT
    source = jnp.where(within < CHUNK, chunk * CHUNK + within, -1)
    order = (lax.broadcasted_iota(jnp.int32, (WIDTH, 1), 0) == source).astype(BF16)
    img_feat = lax.all_gather(mm(pictures[0], order).astype(BF16), "dx", axis=0)
    txt_feat = lax.all_gather(mm(sentences[0], order).astype(BF16), "dx", axis=0)

    count = 2 * QUADS * lax.axis_size("dz") * ways
    core_ref = core.astype(jnp.int32)[None]

    def tail(with_stats, own, unit, length, blocks, feat):
        spread = tiles(with_stats, ways, scal, own, unit, length, key_col, blocks)
        spread = lax.all_to_all(spread, "dx", 0, 0, tiled=True)
        kept, given = heads(with_stats, core_ref, feat, spread)
        taken = exchange(given, "lc", 1)
        sums = (kept.astype(F32) + taken.astype(F32)).astype(BF16)
        sums = lax.all_to_all(sums, ("ly", "lz", "dz"), 0, 0, tiled=True)
        return final(count, sums)

    grad_img, stats = tail(
        True, img, img_unit, img_len, [txt, txt_c, txt_y1, txt_y2, txt_a, txt_b], img_feat
    )
    grad_txt, _ = tail(
        False, txt, txt_unit, txt_len, [img, img_c, img_y1, img_y2, img_a, img_b], txt_feat
    )
    return grad_img, grad_txt, stats[0, :3]


def solution(mesh):
    split = Mesh(mesh.devices.reshape(4, 4, 2, 2, 4), ("ly", "lz", "lc", "dz", "dx"))
    dp = ("dz", "dx")
    return jax.shard_map(
        body,
        mesh=split,
        in_specs=(P(dp, LOSS, None), P(dp, LOSS, None), P(dp, LOSS), P(), P(), P(), P()),
        out_specs=(P(LOSS, dp), P(LOSS, dp), P()),
        check_vma=False,
    )
```

```python
import functools

import jax
import jax.numpy as jnp
from jax import lax
from jax.experimental import pallas as pl
from jax.experimental.pallas import tpu as pltpu
from jax.sharding import Mesh, PartitionSpec as P

EPSILON = 1e-06
LOSS = ("ly", "lz", "lc")
ROWS = 128
WIDTH = 1152
KEY_ROWS = 16
CHUNK = 36
SLOT = 40
COLS = 144
LANES = 128
TAIL = COLS - LANES
QUADS = 16
STATS = 112
F32 = jnp.float32
BF16 = jnp.bfloat16

VMEM = pl.BlockSpec(memory_space=pltpu.VMEM)
SMEM = pl.BlockSpec(memory_space=pltpu.SMEM)


def params():
    return pltpu.CompilerParams(vmem_limit_bytes=40 * 2**20)


def cost(flops, moved):
    return pl.CostEstimate(flops=flops, bytes_accessed=moved, transcendentals=0)


def exchange(array, axis, apart):
    return lax.ppermute(array, axis, [(i, i ^ apart) for i in range(lax.axis_size(axis))])


def after(array, *others):
    return lax.optimization_barrier((array, *others))[0]


def nt(a, b):
    return lax.dot_general(a, b, (((1,), (1,)), ((), ())), preferred_element_type=F32)


def mm(a, b):
    return jnp.dot(a, b, preferred_element_type=F32)


def project_kernel(x_ref, w_ref, key_ref, out_ref, unit_ref, len_ref, acc):
    step = pl.program_id(0)

    @pl.when(step == 0)
    def _():
        acc[...] = jnp.zeros_like(acc)

    acc[...] += mm(x_ref[...], w_ref[...])

    @pl.when(step == pl.num_programs(0) - 1)
    def _():
        u = acc[...]
        length = jnp.sqrt(jnp.sum(u * u, axis=1, keepdims=True) + EPSILON)
        unit = u / length
        unit_ref[...] = unit
        out_ref[:ROWS, :] = unit.astype(BF16)
        key = jnp.broadcast_to(key_ref[...], (KEY_ROWS, ROWS))
        row = lax.broadcasted_iota(jnp.int32, (KEY_ROWS, ROWS), 0)
        digits = jnp.where(row == 0, key >> 7, jnp.where(row == 1, key & 127, 0))
        out_ref[ROWS:, :] = jnp.zeros((KEY_ROWS, WIDTH), BF16)
        out_ref[ROWS:, :ROWS] = digits.astype(F32).astype(BF16)
        len_ref[...] = jnp.broadcast_to(length, len_ref.shape)


def project(x, w, keys):
    depth = 384
    return pl.pallas_call(
        project_kernel,
        grid=(WIDTH // depth,),
        in_specs=[
            pl.BlockSpec((ROWS, depth), lambda k: (0, k)),
            pl.BlockSpec((depth, WIDTH), lambda k: (k, 0)),
            pl.BlockSpec((1, ROWS), lambda k: (0, 0)),
        ],
        out_specs=[
            pl.BlockSpec((ROWS + KEY_ROWS, WIDTH), lambda k: (0, 0)),
            pl.BlockSpec((ROWS, WIDTH), lambda k: (0, 0)),
            pl.BlockSpec((ROWS, LANES), lambda k: (0, 0)),
        ],
        out_shape=[
            jax.ShapeDtypeStruct((ROWS + KEY_ROWS, WIDTH), BF16),
            jax.ShapeDtypeStruct((ROWS, WIDTH), F32),
            jax.ShapeDtypeStruct((ROWS, LANES), F32),
        ],
        scratch_shapes=[pltpu.VMEM((ROWS, WIDTH), F32)],
        compiler_params=params(),
        cost_estimate=cost(2 * ROWS * WIDTH * WIDTH, 4 * 2**20),
    )(x, w, keys)


def tile_kernel(with_stats, ways, spot, scal, own, unit, length, own_key, *refs):
    blocks, outs, held = refs[: -ways - 1], refs[-ways - 1 : -1], refs[-1]
    heat, shift = scal[0], scal[1]
    mine = own[:ROWS, :]
    key_col = own_key[:, :1]
    total = jnp.zeros((ROWS, WIDTH), F32)
    loss_acc = jnp.zeros((ROWS, ROWS), F32)
    heat_acc = jnp.zeros((ROWS, ROWS), F32)
    grad_acc = jnp.zeros((ROWS, ROWS), F32)
    for block in blocks:
        vec = block[:ROWS, :]
        keys = block[ROWS:, :LANES].astype(F32)
        key_row = keys[0:1] * 128.0 + keys[1:2]
        same = key_col == key_row
        sim = nt(mine, vec)
        logits = heat * sim + shift
        z = jnp.where(same, -logits, logits)
        t = jnp.exp(-jnp.abs(z))
        q = 1.0 / (1.0 + t)
        sig = jnp.where(z >= 0, q, t * q)
        g = jnp.where(same, -sig, sig) * (1.0 / ROWS)
        total += mm(g.astype(BF16), vec)
        if with_stats:
            loss_acc += jnp.maximum(z, 0.0) + jnp.log1p(t)
            heat_acc += g * sim
            grad_acc += g
    total = total * heat
    u = unit[...]
    inner = jnp.sum(u * total, axis=1, keepdims=True)
    du = (total - u * inner) / length[:, :1]
    held[...] = du.T.astype(BF16).reshape(held.shape)
    for step, out in enumerate(outs):
        w = lax.rem(spot[0] + step, ways)
        for h in range(2):
            out[h * COLS : (h + 1) * COLS, :] = held[h * ways + w]
    if with_stats:
        def full(x):
            return jnp.sum(jnp.sum(x, axis=1, keepdims=True), axis=0, keepdims=True)

        lane = lax.broadcasted_iota(jnp.int32, (KEY_ROWS, LANES), 1)
        row = lax.broadcasted_iota(jnp.int32, (KEY_ROWS, LANES), 0)
        kind = lane % 3
        value = jnp.where(
            kind == 0,
            full(loss_acc) * (1.0 / ROWS),
            jnp.where(kind == 1, full(heat_acc) * heat, full(grad_acc)),
        )
        value = jnp.where((row == 0) & (lane < 9), value, 0.0)
        high = value.astype(BF16).astype(F32)
        middle = (value - high).astype(BF16).astype(F32)
        low = value - high - middle
        parts = jnp.where(lane < 3, high, jnp.where(lane < 6, middle, low)).astype(BF16)
        for out in outs:
            out[2 * COLS :, :] = parts


def tiles(with_stats, ways, spot, scal, own, unit, length, own_key, blocks):
    rows = 2 * COLS + (KEY_ROWS if with_stats else 0)
    return pl.pallas_call(
        functools.partial(tile_kernel, with_stats, ways),
        in_specs=[SMEM] * 2 + [VMEM] * (4 + len(blocks)),
        out_specs=[VMEM] * ways,
        out_shape=[jax.ShapeDtypeStruct((rows, ROWS), BF16)] * ways,
        scratch_shapes=[pltpu.VMEM((2 * ways, COLS, ROWS), BF16)],
        compiler_params=params(),
        cost_estimate=cost(4 * 6 * ROWS * ROWS * WIDTH, 8 * 2**20),
    )(spot, scal, own, unit, length, own_key, *blocks)


def head_kernel(with_stats, spot, feat, *refs):
    spreads, (kept, given, held) = refs[:-3], refs[-3:]
    ways = len(spreads)
    total = jnp.zeros((2 * COLS, feat.shape[1]), F32)
    for step, spread in enumerate(spreads):
        source = lax.rem(spot[0] + ways - step, ways)
        rows = feat[pl.ds(pl.multiple_of(source * ROWS, ROWS), ROWS), :]
        total += mm(spread[: 2 * COLS, :], rows)
    spare = None
    if with_stats:
        parts = jnp.zeros((KEY_ROWS, LANES), F32)
        for spread in spreads:
            parts += spread[2 * COLS :, :].astype(F32)
        lane = lax.broadcasted_iota(jnp.int32, (8, LANES), 1)
        row = lax.broadcasted_iota(jnp.int32, (8, LANES), 0)
        place = lane - STATS
        summed = jnp.zeros((8, LANES), F32)
        for k in range(3):
            number = jnp.sum(
                jnp.where((lane[:1] % 3 == k) & (lane[:1] < 9), parts[0:1], 0.0),
                axis=1,
                keepdims=True,
            )
            summed = jnp.where(place % 3 == k, number, summed)
        value = jnp.where((row == spot[1]) & (place >= 0) & (place < 9), summed, 0.0)
        high = value.astype(BF16).astype(F32)
        middle = (value - high).astype(BF16).astype(F32)
        low = value - high - middle
        spare = jnp.where(place < 3, high, jnp.where(place < 6, middle, low))
    for h in range(2):
        main = total[h * COLS : h * COLS + LANES, :].T
        rest = total[h * COLS + LANES : (h + 1) * COLS, :]
        for m in range(QUADS):
            for side in range(2):
                start = (2 * m + side) * CHUNK
                target = held.at[side, 2 * m + h]
                target[:CHUNK, :] = main[start : start + CHUNK]
                target[CHUNK:SLOT, :] = jnp.zeros((SLOT - CHUNK, LANES), F32)
                target[SLOT:, :] = jnp.zeros((8, LANES), F32) if spare is None else spare
                for k in range(2):
                    target[SLOT:, 64 * k : 64 * k + CHUNK] = rest[
                        8 * k : 8 * k + 8, start : start + CHUNK
                    ]
    kept[...] = held[spot[1]]
    given[...] = held[1 - spot[1]].astype(BF16)


def heads(with_stats, spot, feat, spreads):
    shape = (2 * QUADS, SLOT + 8, LANES)
    return pl.pallas_call(
        functools.partial(head_kernel, with_stats),
        in_specs=[SMEM] + [VMEM] * (1 + len(spreads)),
        out_specs=[VMEM, VMEM],
        out_shape=[jax.ShapeDtypeStruct(shape, F32), jax.ShapeDtypeStruct(shape, BF16)],
        scratch_shapes=[pltpu.VMEM((2, *shape), F32)],
        compiler_params=params(),
        cost_estimate=cost(2 * 4 * ROWS * 2 * COLS * feat.shape[1], 4 * 2**20),
    )(spot, feat, *spreads)


def final_kernel(count, parts, out, stats):
    total = jnp.sum(parts[...].astype(F32), axis=0)
    out[:, :LANES] = total[:CHUNK]
    rest = total[SLOT:, :].T
    out[:, LANES : LANES + 8] = rest[:CHUNK]
    out[:, LANES + 8 :] = rest[64 : 64 + CHUNK]
    lane = lax.broadcasted_iota(jnp.int32, (1, LANES), 1)
    place = lane - STATS
    row = total[SLOT : SLOT + 1] + total[SLOT + 1 : SLOT + 2]
    answer = jnp.zeros((1, LANES), F32)
    for k in range(3):
        number = jnp.sum(
            jnp.where((place % 3 == k) & (place >= 0) & (place < 9), row, 0.0),
            axis=1,
            keepdims=True,
        )
        answer = jnp.where(lane == k, number, answer)
    stats[...] = answer * (1.0 / count)


def final(count, parts):
    return pl.pallas_call(
        functools.partial(final_kernel, count),
        in_specs=[VMEM],
        out_specs=[VMEM, VMEM],
        out_shape=[
            jax.ShapeDtypeStruct((CHUNK, COLS), F32),
            jax.ShapeDtypeStruct((1, LANES), F32),
        ],
        compiler_params=params(),
        cost_estimate=cost(2 * QUADS * 48 * LANES, 2**20),
    )(parts)


def body(pictures, sentences, keys, picture_weights, sentence_weights, heat_log, shift_value):
    ways = lax.axis_size("dx")
    core = lax.axis_index("lc")
    spot = jnp.stack([lax.axis_index("dx"), core]).astype(jnp.int32)
    scal = jnp.stack([jnp.exp(heat_log[0]), shift_value[0]])
    key_col = jnp.broadcast_to(keys[0].astype(F32)[:, None], (ROWS, LANES))

    txt, txt_unit, txt_len = project(sentences[0], sentence_weights, keys)
    txt_a = exchange(txt, "lz", 1)
    txt_y2 = exchange(txt, "ly", 2)
    txt_y1 = exchange(txt, "ly", 1)
    txt_c = exchange(txt, "lc", 1)
    txt_b = exchange(txt_a, "lz", 3)

    img_feat = lax.all_gather(pictures[0], "dx", axis=0, tiled=True)
    txt_feat = lax.all_gather(sentences[0], "dx", axis=0, tiled=True)
    img, img_unit, img_len = project(after(pictures[0], txt_c), picture_weights, keys)

    img_a = exchange(after(img, txt_a), "lz", 1)
    img_n = after(img, txt_y1, txt_y2)
    img_y2 = exchange(img_n, "ly", 2)
    img_y1 = exchange(img_n, "ly", 1)
    img_c = exchange(img_n, "lc", 1)
    img_b = exchange(img_a, "lz", 3)

    count = 2 * QUADS * lax.axis_size("dz") * ways

    def turn(array, step):
        return lax.ppermute(array, "dx", [(i, (i + step) % ways) for i in range(ways)])

    def columns(with_stats, own, unit, length, blocks):
        outs = tiles(with_stats, ways, spot, scal, own, unit, length, key_col, blocks)
        return [outs[0]] + [turn(out, step) for step, out in enumerate(outs) if step]

    def share(with_stats, feat, spreads):
        kept, given = heads(with_stats, spot, feat, spreads)
        taken = exchange(given, "lc", 1)
        return (kept + taken.astype(F32)).astype(BF16)

    def collect(sums):
        return final(count, lax.all_to_all(sums, ("ly", "lz", "dz"), 0, 0, tiled=True))

    img_blocks = list(
        lax.optimization_barrier(
            (txt, txt_c, txt_y1, txt_y2, txt_a, txt_b, img_a, img_c, img_y1, img_y2)
        )
    )[:6]
    img_cols = columns(True, img, img_unit, img_len, img_blocks)
    img_feat = after(img_feat, img_b)
    img_sums = share(True, img_feat, img_cols)
    txt_cols = columns(
        False, txt, txt_unit, txt_len, [img, img_c, img_y1, img_y2, img_a, img_b]
    )
    txt_sums = share(False, txt_feat, txt_cols)
    grad_img, stats = collect(img_sums)
    grad_txt, _ = collect(txt_sums)
    return grad_img, grad_txt, stats[0, :3]


def solution(mesh):
    split = Mesh(mesh.devices.reshape(4, 4, 2, 2, 4), ("ly", "lz", "lc", "dz", "dx"))
    dp = ("dz", "dx")
    return jax.shard_map(
        body,
        mesh=split,
        in_specs=(P(dp, LOSS, None), P(dp, LOSS, None), P(dp, LOSS), P(), P(), P(), P()),
        out_specs=(P(LOSS, dp), P(LOSS, dp), P()),
        check_vma=False,
    )
```

```python
import functools

import jax
import jax.numpy as jnp
from jax import lax
from jax.experimental import pallas as pl
from jax.experimental.pallas import tpu as pltpu
from jax.sharding import Mesh, PartitionSpec as P

EPSILON = 1e-06
LOSS = ("ly", "lz", "lc")
ROWS = 128
WIDTH = 1152
KEY_ROWS = 16
CHUNK = 36
SLOT = 40
COLS = 144
LANES = 128
TAIL = COLS - LANES
QUADS = 16
STATS = 112
DEPTH = 384
PIECES = WIDTH // DEPTH
F32 = jnp.float32
BF16 = jnp.bfloat16

VMEM = pl.BlockSpec(memory_space=pltpu.VMEM)
SMEM = pl.BlockSpec(memory_space=pltpu.SMEM)


def params(megabytes):
    return pltpu.CompilerParams(vmem_limit_bytes=megabytes * 2**20)


def cost(flops, moved):
    return pl.CostEstimate(flops=flops, bytes_accessed=moved, transcendentals=0)


def exchange(array, axis, apart):
    return lax.ppermute(array, axis, [(i, i ^ apart) for i in range(lax.axis_size(axis))])


def after(array, *others):
    return lax.optimization_barrier((array, *others))[0]


def nt(a, b):
    return lax.dot_general(a, b, (((1,), (1,)), ((), ())), preferred_element_type=F32)


def mm(a, b):
    return jnp.dot(a, b, preferred_element_type=F32)


def project_kernel(x_hbm, w_hbm, key_hbm, out_ref, x, w, key, sems):
    copies = [
        pltpu.make_async_copy(x_hbm, x, sems.at[0]),
        pltpu.make_async_copy(key_hbm, key, sems.at[1]),
    ]
    for k in range(PIECES):
        span = pl.ds(k * DEPTH, DEPTH)
        copies.append(pltpu.make_async_copy(w_hbm.at[span], w.at[span], sems.at[2 + k]))
    for copy in copies:
        copy.start()
    copies[0].wait()
    u = jnp.zeros((ROWS, WIDTH), F32)
    for k in range(PIECES):
        copies[2 + k].wait()
        span = slice(k * DEPTH, (k + 1) * DEPTH)
        u += mm(x[:, span], w[span])
    out_ref[:ROWS, :] = (u / lengths(u)).astype(BF16)
    copies[1].wait()
    digit = jnp.broadcast_to(key[...], (KEY_ROWS, ROWS))
    row = lax.broadcasted_iota(jnp.int32, (KEY_ROWS, ROWS), 0)
    digit = jnp.where(row == 0, digit >> 7, jnp.where(row == 1, digit & 127, 0))
    out_ref[ROWS:, :] = jnp.zeros((KEY_ROWS, WIDTH), BF16)
    out_ref[ROWS:, :ROWS] = digit.astype(F32).astype(BF16)


def lengths(u):
    return jnp.sqrt(jnp.sum(u * u, axis=1, keepdims=True) + EPSILON)


def project(x, w, keys):
    return pl.pallas_call(
        project_kernel,
        in_specs=[pl.BlockSpec(memory_space=pltpu.HBM)] * 3,
        out_specs=VMEM,
        out_shape=jax.ShapeDtypeStruct((ROWS + KEY_ROWS, WIDTH), BF16),
        scratch_shapes=[
            pltpu.VMEM((ROWS, WIDTH), BF16),
            pltpu.VMEM((WIDTH, WIDTH), BF16),
            pltpu.VMEM((1, ROWS), jnp.int32),
            pltpu.SemaphoreType.DMA((2 + PIECES,)),
        ],
        compiler_params=params(56),
        cost_estimate=cost(2 * ROWS * WIDTH * WIDTH, 4 * 2**20),
    )(x, w, keys)


def add_tiles(with_stats, scal, mine, key_col, blocks, total, sums):
    heat, shift = scal[0], scal[1]
    for block in blocks:
        vec = block[:ROWS, :]
        keys = block[ROWS:, :LANES].astype(F32)
        same = key_col == keys[0:1] * 128.0 + keys[1:2]
        sim = nt(mine, vec)
        logits = heat * sim + shift
        z = jnp.where(same, -logits, logits)
        t = jnp.exp(-jnp.abs(z))
        q = 1.0 / (1.0 + t)
        sig = jnp.where(z >= 0, q, t * q)
        g = jnp.where(same, -sig, sig) * (1.0 / ROWS)
        total += mm(g.astype(BF16), vec)
        if with_stats:
            new = (jnp.maximum(z, 0.0) + jnp.log1p(t), g * sim, g)
            sums = [old + add for old, add in zip(sums, new)]
    return total, sums


def early_kernel(with_stats, scal, x, w, key, own, *refs):
    blocks, (total_ref, unit_ref, len_ref, key_ref, sum_ref) = refs[:-5], refs[-5:]
    u = mm(x[...], w[...])
    length = lengths(u)
    unit_ref[...] = u / length
    len_ref[...] = jnp.broadcast_to(length, len_ref.shape)
    key_col = jnp.broadcast_to(key[...].astype(F32), (ROWS, ROWS)).T
    key_ref[...] = key_col
    zero = jnp.zeros((ROWS, ROWS), F32)
    total, sums = add_tiles(
        with_stats,
        scal,
        own[:ROWS, :],
        key_col,
        blocks,
        jnp.zeros((ROWS, WIDTH), F32),
        [zero] * 3,
    )
    total_ref[...] = total
    for k in range(3):
        sum_ref[k] = sums[k]


def early(with_stats, scal, x, w, keys, own, blocks):
    shapes = [(ROWS, WIDTH), (ROWS, WIDTH), (ROWS, LANES), (ROWS, ROWS), (3, ROWS, ROWS)]
    return pl.pallas_call(
        functools.partial(early_kernel, with_stats),
        in_specs=[SMEM] + [VMEM] * (4 + len(blocks)),
        out_specs=[VMEM] * len(shapes),
        out_shape=[jax.ShapeDtypeStruct(shape, F32) for shape in shapes],
        compiler_params=params(56),
        cost_estimate=cost(4 * 5 * ROWS * ROWS * WIDTH, 8 * 2**20),
    )(scal, x, w, keys, own, *blocks)


def late_kernel(with_stats, ways, count, spot, scal, own, total_ref, unit, length, key, acc, *refs):
    blocks, outs, held = refs[:count], refs[count:-1], refs[-1]
    heat = scal[0]
    total, sums = add_tiles(
        with_stats,
        scal,
        own[:ROWS, :],
        key[...],
        blocks,
        total_ref[...],
        [acc[k] for k in range(3)],
    )
    total = total * heat
    u = unit[...]
    inner = jnp.sum(u * total, axis=1, keepdims=True)
    du = (total - u * inner) / length[:, :1]
    held[...] = du.T.astype(BF16).reshape(held.shape)
    if with_stats:
        def full(x):
            return jnp.sum(jnp.sum(x, axis=1, keepdims=True), axis=0, keepdims=True)

        lane = lax.broadcasted_iota(jnp.int32, (KEY_ROWS, LANES), 1)
        row = lax.broadcasted_iota(jnp.int32, (KEY_ROWS, LANES), 0)
        kind = lane % 3
        value = jnp.where(
            kind == 0,
            full(sums[0]) * (1.0 / ROWS),
            jnp.where(kind == 1, full(sums[1]) * heat, full(sums[2])),
        )
        value = jnp.where((row == 0) & (lane < 9), value, 0.0)
        high = value.astype(BF16).astype(F32)
        middle = (value - high).astype(BF16).astype(F32)
        low = value - high - middle
        parts = jnp.where(lane < 3, high, jnp.where(lane < 6, middle, low)).astype(BF16)
        out = outs[0]
        for w in range(ways):
            for h in range(2):
                out[w, h * COLS : (h + 1) * COLS, :] = held[h * ways + w]
            out[w, 2 * COLS :, :] = parts
    else:
        for step, out in enumerate(outs):
            w = lax.rem(spot[0] + step, ways)
            for h in range(2):
                out[h * COLS : (h + 1) * COLS, :] = held[h * ways + w]


def late(with_stats, ways, spot, scal, own, partial, blocks):
    if with_stats:
        shapes = [(ways, 2 * COLS + KEY_ROWS, ROWS)]
    else:
        shapes = [(2 * COLS, ROWS)] * ways
    return pl.pallas_call(
        functools.partial(late_kernel, with_stats, ways, len(blocks)),
        in_specs=[SMEM] * 2 + [VMEM] * (6 + len(blocks)),
        out_specs=[VMEM] * len(shapes),
        out_shape=[jax.ShapeDtypeStruct(shape, BF16) for shape in shapes],
        scratch_shapes=[pltpu.VMEM((2 * ways, COLS, ROWS), BF16)],
        compiler_params=params(56),
        cost_estimate=cost(4 * 2 * ROWS * ROWS * WIDTH, 4 * 2**20),
    )(spot, scal, own, *partial, *blocks)


def head_kernel(with_stats, spot, feat, *refs):
    spreads, (kept, given, held) = refs[:-3], refs[-3:]
    if with_stats:
        spreads = [spreads[0].at[w] for w in range(spreads[0].shape[0])]
    ways = len(spreads)
    total = jnp.zeros((2 * COLS, feat.shape[1]), F32)
    for step, spread in enumerate(spreads):
        source = step if with_stats else lax.rem(spot[0] + ways - step, ways)
        start = source * ROWS if with_stats else pl.multiple_of(source * ROWS, ROWS)
        rows = feat[pl.ds(start, ROWS), :]
        total += mm(spread[: 2 * COLS, :], rows)
    spare = None
    if with_stats:
        parts = jnp.zeros((KEY_ROWS, LANES), F32)
        for spread in spreads:
            parts += spread[2 * COLS :, :].astype(F32)
        lane = lax.broadcasted_iota(jnp.int32, (8, LANES), 1)
        row = lax.broadcasted_iota(jnp.int32, (8, LANES), 0)
        place = lane - STATS
        summed = jnp.zeros((8, LANES), F32)
        for k in range(3):
            number = jnp.sum(
                jnp.where((lane[:1] % 3 == k) & (lane[:1] < 9), parts[0:1], 0.0),
                axis=1,
                keepdims=True,
            )
            summed = jnp.where(place % 3 == k, number, summed)
        value = jnp.where((row == spot[1]) & (place >= 0) & (place < 9), summed, 0.0)
        high = value.astype(BF16).astype(F32)
        middle = (value - high).astype(BF16).astype(F32)
        low = value - high - middle
        spare = jnp.where(place < 3, high, jnp.where(place < 6, middle, low))
    for h in range(2):
        main = total[h * COLS : h * COLS + LANES, :].T
        rest = total[h * COLS + LANES : (h + 1) * COLS, :]
        for m in range(QUADS):
            for side in range(2):
                start = (2 * m + side) * CHUNK
                target = held.at[side, 2 * m + h]
                target[:CHUNK, :] = main[start : start + CHUNK]
                target[CHUNK:SLOT, :] = jnp.zeros((SLOT - CHUNK, LANES), F32)
                target[SLOT:, :] = jnp.zeros((8, LANES), F32) if spare is None else spare
                for k in range(2):
                    target[SLOT:, 64 * k : 64 * k + CHUNK] = rest[
                        8 * k : 8 * k + 8, start : start + CHUNK
                    ]
    kept[...] = held[spot[1]]
    given[...] = held[1 - spot[1]].astype(BF16)


def heads(with_stats, spot, feat, spreads):
    shape = (2 * QUADS, SLOT + 8, LANES)
    return pl.pallas_call(
        functools.partial(head_kernel, with_stats),
        in_specs=[SMEM] + [VMEM] * (1 + len(spreads)),
        out_specs=[VMEM, VMEM],
        out_shape=[jax.ShapeDtypeStruct(shape, F32), jax.ShapeDtypeStruct(shape, BF16)],
        scratch_shapes=[pltpu.VMEM((2, *shape), F32)],
        compiler_params=params(24),
        cost_estimate=cost(2 * 4 * ROWS * 2 * COLS * feat.shape[1], 4 * 2**20),
    )(spot, feat, *spreads)


def final_kernel(count, parts, out, stats):
    total = jnp.sum(parts[...].astype(F32), axis=0)
    out[:, :LANES] = total[:CHUNK]
    rest = total[SLOT:, :].T
    out[:, LANES : LANES + 8] = rest[:CHUNK]
    out[:, LANES + 8 :] = rest[64 : 64 + CHUNK]
    lane = lax.broadcasted_iota(jnp.int32, (1, LANES), 1)
    place = lane - STATS
    row = total[SLOT : SLOT + 1] + total[SLOT + 1 : SLOT + 2]
    answer = jnp.zeros((1, LANES), F32)
    for k in range(3):
        number = jnp.sum(
            jnp.where((place % 3 == k) & (place >= 0) & (place < 9), row, 0.0),
            axis=1,
            keepdims=True,
        )
        answer = jnp.where(lane == k, number, answer)
    stats[...] = answer * (1.0 / count)


def final(count, parts):
    return pl.pallas_call(
        functools.partial(final_kernel, count),
        in_specs=[VMEM],
        out_specs=[VMEM, VMEM],
        out_shape=[
            jax.ShapeDtypeStruct((CHUNK, COLS), F32),
            jax.ShapeDtypeStruct((1, LANES), F32),
        ],
        compiler_params=params(8),
        cost_estimate=cost(2 * QUADS * 48 * LANES, 2**20),
    )(parts)


def body(pictures, sentences, keys, picture_weights, sentence_weights, heat_log, shift_value):
    ways = lax.axis_size("dx")
    spot = jnp.stack([lax.axis_index("dx"), lax.axis_index("lc")]).astype(jnp.int32)
    scal = jnp.stack([jnp.exp(heat_log[0]), shift_value[0]])
    img_feat = lax.all_gather(pictures[0], "dx", axis=0, tiled=True)
    txt_feat = lax.all_gather(sentences[0], "dx", axis=0, tiled=True)

    txt = project(sentences[0], sentence_weights, keys)
    txt_a = exchange(txt, "lz", 1)
    txt_y2 = exchange(txt, "ly", 2)
    txt_y1 = exchange(txt, "ly", 1)
    txt_c = exchange(txt, "lc", 1)
    img = project(after(pictures[0], txt_c), picture_weights, keys)
    txt_b = exchange(after(txt_a, txt_y1, txt_y2), "lz", 3)

    img_a = exchange(after(img, txt_a), "lz", 1)
    img_c = exchange(img, "lc", 1)
    img_b = exchange(img_a, "lz", 3)
    img_n = after(img, img_a)
    img_y2 = exchange(img_n, "ly", 2)
    img_y1 = exchange(img_n, "ly", 1)

    count = 2 * QUADS * lax.axis_size("dz") * ways

    def turn(array, step):
        return lax.ppermute(array, "dx", [(i, (i + step) % ways) for i in range(ways)])

    def share(with_stats, feat, spreads):
        kept, given = heads(with_stats, spot, feat, spreads)
        taken = exchange(given, "lc", 1)
        return (kept + taken.astype(F32)).astype(BF16)

    def collect(sums):
        return final(count, lax.all_to_all(sums, ("ly", "lz", "dz"), 0, 0, tiled=True))

    img_part = early(
        True, scal, pictures[0], picture_weights, keys, img, [txt, txt_c, txt_y1, txt_y2, txt_a]
    )
    last, img_feat = lax.optimization_barrier((txt_b, img_feat, img_a, img_c))[:2]
    img_outs = late(True, ways, spot, scal, img, img_part, [last])[0]
    img_cols = lax.all_to_all(img_outs, "dx", 0, 0, tiled=True)
    txt_part = early(
        False, scal, sentences[0], sentence_weights, keys, txt, [img, img_c, img_a]
    )
    img_feat = after(img_feat, img_b, img_y1, img_y2, *txt_part)
    img_sums = share(True, img_feat, [img_cols])
    lasts = list(lax.optimization_barrier((img_y1, img_y2, img_b, img_cols))[:3])
    outs = late(False, ways, spot, scal, txt, txt_part, lasts)
    *outs, txt_feat = lax.optimization_barrier((*outs, txt_feat))
    txt_cols = [outs[0]] + [turn(out, step) for step, out in enumerate(outs) if step]
    txt_sums = share(False, txt_feat, txt_cols)
    grad_img, stats = collect(img_sums)
    grad_txt, _ = collect(txt_sums)
    return grad_img, grad_txt, stats[0, :3]


def solution(mesh):
    split = Mesh(mesh.devices.reshape(4, 4, 2, 2, 4), ("ly", "lz", "lc", "dz", "dx"))
    dp = ("dz", "dx")
    return jax.shard_map(
        body,
        mesh=split,
        in_specs=(P(dp, LOSS, None), P(dp, LOSS, None), P(dp, LOSS), P(), P(), P(), P()),
        out_specs=(P(LOSS, dp), P(LOSS, dp), P()),
        check_vma=False,
    )
```

```python
import functools

import jax
import jax.numpy as jnp
from jax import lax
from jax.experimental import pallas as pl
from jax.experimental.pallas import tpu as pltpu
from jax.sharding import Mesh, PartitionSpec as P

EPSILON = 1e-06
LOSS = ("ly", "lz", "lc")
ROWS = 128
WIDTH = 1152
KEY_ROWS = 16
CHUNK = 36
SLOT = 40
COLS = 144
LANES = 128
TAIL = COLS - LANES
QUADS = 16
STATS = 112
DEPTH = 384
PIECES = WIDTH // DEPTH
F32 = jnp.float32
BF16 = jnp.bfloat16

VMEM = pl.BlockSpec(memory_space=pltpu.VMEM)
SMEM = pl.BlockSpec(memory_space=pltpu.SMEM)


def params(megabytes):
    return pltpu.CompilerParams(vmem_limit_bytes=megabytes * 2**20)


def cost(flops, moved):
    return pl.CostEstimate(flops=flops, bytes_accessed=moved, transcendentals=0)


def exchange(array, axis, apart):
    return lax.ppermute(array, axis, [(i, i ^ apart) for i in range(lax.axis_size(axis))])


def after(array, *others):
    return lax.optimization_barrier((array, *others))[0]


def nt(a, b):
    return lax.dot_general(a, b, (((1,), (1,)), ((), ())), preferred_element_type=F32)


def mm(a, b):
    return jnp.dot(a, b, preferred_element_type=F32)


def project_kernel(x_hbm, w_hbm, key_hbm, out_ref, x, w, key, sems):
    copies = [
        pltpu.make_async_copy(x_hbm, x, sems.at[0]),
        pltpu.make_async_copy(key_hbm, key, sems.at[1]),
    ]
    for k in range(PIECES):
        span = pl.ds(k * DEPTH, DEPTH)
        copies.append(pltpu.make_async_copy(w_hbm.at[span], w.at[span], sems.at[2 + k]))
    for copy in copies:
        copy.start()
    copies[0].wait()
    u = jnp.zeros((ROWS, WIDTH), F32)
    for k in range(PIECES):
        copies[2 + k].wait()
        span = slice(k * DEPTH, (k + 1) * DEPTH)
        u += mm(x[:, span], w[span])
    out_ref[:ROWS, :] = (u / lengths(u)).astype(BF16)
    copies[1].wait()
    digit = jnp.broadcast_to(key[...], (KEY_ROWS, ROWS))
    row = lax.broadcasted_iota(jnp.int32, (KEY_ROWS, ROWS), 0)
    digit = jnp.where(row == 0, digit >> 7, jnp.where(row == 1, digit & 127, 0))
    out_ref[ROWS:, :] = jnp.zeros((KEY_ROWS, WIDTH), BF16)
    out_ref[ROWS:, :ROWS] = digit.astype(F32).astype(BF16)


def lengths(u):
    return jnp.sqrt(jnp.sum(u * u, axis=1, keepdims=True) + EPSILON)


def project(x, w, keys):
    return pl.pallas_call(
        project_kernel,
        in_specs=[pl.BlockSpec(memory_space=pltpu.HBM)] * 3,
        out_specs=VMEM,
        out_shape=jax.ShapeDtypeStruct((ROWS + KEY_ROWS, WIDTH), BF16),
        scratch_shapes=[
            pltpu.VMEM((ROWS, WIDTH), BF16),
            pltpu.VMEM((WIDTH, WIDTH), BF16),
            pltpu.VMEM((1, ROWS), jnp.int32),
            pltpu.SemaphoreType.DMA((2 + PIECES,)),
        ],
        compiler_params=params(56),
        cost_estimate=cost(2 * ROWS * WIDTH * WIDTH, 4 * 2**20),
    )(x, w, keys)


def add_tiles(with_stats, scal, mine, key_col, blocks, total, sums):
    heat, shift = scal[0], scal[1]
    for block in blocks:
        vec = block[:ROWS, :]
        keys = block[ROWS:, :LANES].astype(F32)
        same = key_col == keys[0:1] * 128.0 + keys[1:2]
        sim = nt(mine, vec)
        logits = heat * sim + shift
        z = jnp.where(same, -logits, logits)
        t = jnp.exp(-jnp.abs(z))
        q = 1.0 / (1.0 + t)
        sig = jnp.where(z >= 0, q, t * q)
        g = jnp.where(same, -sig, sig) * (1.0 / ROWS)
        total += mm(g.astype(BF16), vec)
        if with_stats:
            new = (jnp.maximum(z, 0.0) + jnp.log1p(t), g * sim, g)
            sums = [old + add for old, add in zip(sums, new)]
    return total, sums


def early_kernel(with_stats, scal, x, w, key, own, *refs):
    blocks, (total_ref, unit_ref, len_ref, key_ref, sum_ref) = refs[:-5], refs[-5:]
    u = mm(x[...], w[...])
    length = lengths(u)
    unit_ref[...] = u / length
    len_ref[...] = jnp.broadcast_to(length, len_ref.shape)
    key_col = jnp.broadcast_to(key[...].astype(F32), (ROWS, ROWS)).T
    key_ref[...] = key_col
    zero = jnp.zeros((ROWS, ROWS), F32)
    total, sums = add_tiles(
        with_stats,
        scal,
        own[:ROWS, :],
        key_col,
        blocks,
        jnp.zeros((ROWS, WIDTH), F32),
        [zero] * 3,
    )
    total_ref[...] = total
    for k in range(3):
        sum_ref[k] = sums[k]


def early(with_stats, scal, x, w, keys, own, blocks):
    shapes = [(ROWS, WIDTH), (ROWS, WIDTH), (ROWS, LANES), (ROWS, ROWS), (3, ROWS, ROWS)]
    return pl.pallas_call(
        functools.partial(early_kernel, with_stats),
        in_specs=[SMEM] + [VMEM] * (4 + len(blocks)),
        out_specs=[VMEM] * len(shapes),
        out_shape=[jax.ShapeDtypeStruct(shape, F32) for shape in shapes],
        compiler_params=params(56),
        cost_estimate=cost(4 * 5 * ROWS * ROWS * WIDTH, 8 * 2**20),
    )(scal, x, w, keys, own, *blocks)


def late_kernel(with_stats, ways, count, spot, scal, own, total_ref, unit, length, key, acc, *refs):
    blocks, outs, held = refs[:count], refs[count:-1], refs[-1]
    heat = scal[0]
    total, sums = add_tiles(
        with_stats,
        scal,
        own[:ROWS, :],
        key[...],
        blocks,
        total_ref[...],
        [acc[k] for k in range(3)],
    )
    total = total * heat
    u = unit[...]
    inner = jnp.sum(u * total, axis=1, keepdims=True)
    du = (total - u * inner) / length[:, :1]
    held[...] = du.T.astype(BF16).reshape(held.shape)
    if with_stats:
        def full(x):
            return jnp.sum(jnp.sum(x, axis=1, keepdims=True), axis=0, keepdims=True)

        lane = lax.broadcasted_iota(jnp.int32, (KEY_ROWS, LANES), 1)
        row = lax.broadcasted_iota(jnp.int32, (KEY_ROWS, LANES), 0)
        kind = lane % 3
        value = jnp.where(
            kind == 0,
            full(sums[0]) * (1.0 / ROWS),
            jnp.where(kind == 1, full(sums[1]) * heat, full(sums[2])),
        )
        value = jnp.where((row == 0) & (lane < 9), value, 0.0)
        high = value.astype(BF16).astype(F32)
        middle = (value - high).astype(BF16).astype(F32)
        low = value - high - middle
        parts = jnp.where(lane < 3, high, jnp.where(lane < 6, middle, low)).astype(BF16)
        out = outs[0]
        for w in range(ways):
            for h in range(2):
                out[w, h * COLS : (h + 1) * COLS, :] = held[h * ways + w]
            out[w, 2 * COLS :, :] = parts
    else:
        for step, out in enumerate(outs):
            w = lax.rem(spot[0] + step, ways)
            for h in range(2):
                out[h * COLS : (h + 1) * COLS, :] = held[h * ways + w]


def late(with_stats, ways, spot, scal, own, partial, blocks):
    if with_stats:
        shapes = [(ways, 2 * COLS + KEY_ROWS, ROWS)]
    else:
        shapes = [(2 * COLS, ROWS)] * ways
    return pl.pallas_call(
        functools.partial(late_kernel, with_stats, ways, len(blocks)),
        in_specs=[SMEM] * 2 + [VMEM] * (6 + len(blocks)),
        out_specs=[VMEM] * len(shapes),
        out_shape=[jax.ShapeDtypeStruct(shape, BF16) for shape in shapes],
        scratch_shapes=[pltpu.VMEM((2 * ways, COLS, ROWS), BF16)],
        compiler_params=params(56),
        cost_estimate=cost(4 * 2 * ROWS * ROWS * WIDTH, 4 * 2**20),
    )(spot, scal, own, *partial, *blocks)


def head_kernel(with_stats, spot, feat, *refs):
    spreads, (kept, given, held) = refs[:-3], refs[-3:]
    if with_stats:
        spreads = [spreads[0].at[w] for w in range(spreads[0].shape[0])]
    ways = len(spreads)
    total = jnp.zeros((2 * COLS, feat.shape[1]), F32)
    for step, spread in enumerate(spreads):
        source = step if with_stats else lax.rem(spot[0] + ways - step, ways)
        start = source * ROWS if with_stats else pl.multiple_of(source * ROWS, ROWS)
        rows = feat[pl.ds(start, ROWS), :]
        total += mm(spread[: 2 * COLS, :], rows)
    spare = None
    if with_stats:
        parts = jnp.zeros((KEY_ROWS, LANES), F32)
        for spread in spreads:
            parts += spread[2 * COLS :, :].astype(F32)
        lane = lax.broadcasted_iota(jnp.int32, (8, LANES), 1)
        row = lax.broadcasted_iota(jnp.int32, (8, LANES), 0)
        place = lane - STATS
        summed = jnp.zeros((8, LANES), F32)
        for k in range(3):
            number = jnp.sum(
                jnp.where((lane[:1] % 3 == k) & (lane[:1] < 9), parts[0:1], 0.0),
                axis=1,
                keepdims=True,
            )
            summed = jnp.where(place % 3 == k, number, summed)
        value = jnp.where((row == spot[1]) & (place >= 0) & (place < 9), summed, 0.0)
        high = value.astype(BF16).astype(F32)
        middle = (value - high).astype(BF16).astype(F32)
        low = value - high - middle
        spare = jnp.where(place < 3, high, jnp.where(place < 6, middle, low))
    for h in range(2):
        main = total[h * COLS : h * COLS + LANES, :].T
        rest = total[h * COLS + LANES : (h + 1) * COLS, :]
        for m in range(QUADS):
            for side in range(2):
                start = (2 * m + side) * CHUNK
                target = held.at[side, 2 * m + h]
                target[:CHUNK, :] = main[start : start + CHUNK]
                target[CHUNK:SLOT, :] = jnp.zeros((SLOT - CHUNK, LANES), F32)
                target[SLOT:, :] = jnp.zeros((8, LANES), F32) if spare is None else spare
                for k in range(2):
                    target[SLOT:, 64 * k : 64 * k + CHUNK] = rest[
                        8 * k : 8 * k + 8, start : start + CHUNK
                    ]
    kept[...] = held[spot[1]]
    given[...] = held[1 - spot[1]].astype(BF16)


def heads(with_stats, spot, feat, spreads):
    shape = (2 * QUADS, SLOT + 8, LANES)
    return pl.pallas_call(
        functools.partial(head_kernel, with_stats),
        in_specs=[SMEM] + [VMEM] * (1 + len(spreads)),
        out_specs=[VMEM, VMEM],
        out_shape=[jax.ShapeDtypeStruct(shape, F32), jax.ShapeDtypeStruct(shape, BF16)],
        scratch_shapes=[pltpu.VMEM((2, *shape), F32)],
        compiler_params=params(24),
        cost_estimate=cost(2 * 4 * ROWS * 2 * COLS * feat.shape[1], 4 * 2**20),
    )(spot, feat, *spreads)


def final_kernel(count, parts, out, stats):
    total = jnp.sum(parts[...].astype(F32), axis=0)
    out[:, :LANES] = total[:CHUNK]
    rest = total[SLOT:, :].T
    out[:, LANES : LANES + 8] = rest[:CHUNK]
    out[:, LANES + 8 :] = rest[64 : 64 + CHUNK]
    lane = lax.broadcasted_iota(jnp.int32, (1, LANES), 1)
    place = lane - STATS
    row = total[SLOT : SLOT + 1] + total[SLOT + 1 : SLOT + 2]
    answer = jnp.zeros((1, LANES), F32)
    for k in range(3):
        number = jnp.sum(
            jnp.where((place % 3 == k) & (place >= 0) & (place < 9), row, 0.0),
            axis=1,
            keepdims=True,
        )
        answer = jnp.where(lane == k, number, answer)
    stats[...] = answer * (1.0 / count)


def final(count, parts):
    return pl.pallas_call(
        functools.partial(final_kernel, count),
        in_specs=[VMEM],
        out_specs=[VMEM, VMEM],
        out_shape=[
            jax.ShapeDtypeStruct((CHUNK, COLS), F32),
            jax.ShapeDtypeStruct((1, LANES), F32),
        ],
        compiler_params=params(8),
        cost_estimate=cost(2 * QUADS * 48 * LANES, 2**20),
    )(parts)


def body(pictures, sentences, keys, picture_weights, sentence_weights, heat_log, shift_value):
    ways = lax.axis_size("dx")
    spot = jnp.stack([lax.axis_index("dx"), lax.axis_index("lc")]).astype(jnp.int32)
    scal = jnp.stack([jnp.exp(heat_log[0]), shift_value[0]])
    txt = project(sentences[0], sentence_weights, keys)
    txt_a = exchange(txt, "lz", 1)
    txt_b = exchange(txt, "lz", 2)
    txt_y2 = exchange(txt, "ly", 2)
    txt_y1 = exchange(txt, "ly", 1)
    txt_c = exchange(txt, "lc", 1)
    img_feat = lax.all_gather(after(pictures[0], txt), "dx", axis=0, tiled=True)
    txt_feat = lax.all_gather(after(sentences[0], txt), "dx", axis=0, tiled=True)

    img = project(after(pictures[0], txt_c), picture_weights, keys)
    img_a = exchange(img, "lz", 1)
    img_c = exchange(img, "lc", 1)
    img_n = after(img, txt_y1, txt_y2)
    img_y2 = exchange(img_n, "ly", 2)
    img_y1 = exchange(img_n, "ly", 1)
    img_b = exchange(img_a, "lz", 3)

    count = 2 * QUADS * lax.axis_size("dz") * ways

    def turn(array, step):
        return lax.ppermute(array, "dx", [(i, (i + step) % ways) for i in range(ways)])

    def share(with_stats, feat, spreads, *others):
        kept, given = heads(with_stats, spot, feat, spreads)
        taken = after(exchange(given, "lc", 1), *others)
        return (kept + taken.astype(F32)).astype(BF16)

    def collect(sums):
        return final(count, lax.all_to_all(sums, ("ly", "lz", "dz"), 0, 0, tiled=True))

    img_part = early(
        True, scal, pictures[0], picture_weights, keys, img, [txt, txt_c, txt_y1, txt_y2, txt_a]
    )
    last = after(txt_b, img_feat, img_a, img_c, img_y1, img_y2)
    img_outs = late(True, ways, spot, scal, img, img_part, [last])[0]
    img_cols = lax.all_to_all(img_outs, "dx", 0, 0, tiled=True)
    txt_part = early(
        False, scal, sentences[0], sentence_weights, keys, txt, [img, img_c, img_y1, img_y2, img_a]
    )
    img_sums = share(True, after(img_feat, img_b, *txt_part), [img_cols])
    last = after(img_b, img_cols)
    outs = late(False, ways, spot, scal, txt, txt_part, [last])
    *outs, txt_feat = lax.optimization_barrier((*outs, txt_feat))
    txt_cols = [outs[0]] + [turn(out, step) for step, out in enumerate(outs) if step]
    txt_sums = share(False, txt_feat, txt_cols)
    grad_img, stats = collect(img_sums)
    grad_txt, _ = collect(txt_sums)
    return grad_img, grad_txt, stats[0, :3]


def solution(mesh):
    split = Mesh(mesh.devices.reshape(4, 4, 2, 2, 4), ("ly", "lz", "lc", "dz", "dx"))
    dp = ("dz", "dx")
    return jax.shard_map(
        body,
        mesh=split,
        in_specs=(P(dp, LOSS, None), P(dp, LOSS, None), P(dp, LOSS), P(), P(), P(), P()),
        out_specs=(P(LOSS, dp), P(LOSS, dp), P()),
        check_vma=False,
    )
```

```python
import functools

import jax
import jax.numpy as jnp
from jax import lax
from jax.experimental import pallas as pl
from jax.experimental.pallas import tpu as pltpu
from jax.sharding import Mesh, PartitionSpec as P

EPSILON = 1e-06
LOSS = ("ly", "lz", "lc")
ROWS = 128
WIDTH = 1152
KEY_ROWS = 16
CHUNK = 36
SLOT = 40
COLS = 144
LANES = 128
TAIL = COLS - LANES
QUADS = 16
STATS = 112
DEPTH = 384
PIECES = WIDTH // DEPTH
F32 = jnp.float32
BF16 = jnp.bfloat16

VMEM = pl.BlockSpec(memory_space=pltpu.VMEM)
SMEM = pl.BlockSpec(memory_space=pltpu.SMEM)


def params(megabytes):
    return pltpu.CompilerParams(vmem_limit_bytes=megabytes * 2**20)


def cost(flops, moved):
    return pl.CostEstimate(flops=flops, bytes_accessed=moved, transcendentals=0)


def exchange(array, axis, apart):
    return lax.ppermute(array, axis, [(i, i ^ apart) for i in range(lax.axis_size(axis))])


def after(array, *others):
    return lax.optimization_barrier((array, *others))[0]


def nt(a, b):
    return lax.dot_general(a, b, (((1,), (1,)), ((), ())), preferred_element_type=F32)


def mm(a, b):
    return jnp.dot(a, b, preferred_element_type=F32)


def project_kernel(x_hbm, w_hbm, key_hbm, out_ref, x, w, key, sems):
    copies = [
        pltpu.make_async_copy(x_hbm, x, sems.at[0]),
        pltpu.make_async_copy(key_hbm, key, sems.at[1]),
    ]
    for k in range(PIECES):
        span = pl.ds(k * DEPTH, DEPTH)
        copies.append(pltpu.make_async_copy(w_hbm.at[span], w.at[span], sems.at[2 + k]))
    for copy in copies:
        copy.start()
    copies[0].wait()
    u = jnp.zeros((ROWS, WIDTH), F32)
    for k in range(PIECES):
        copies[2 + k].wait()
        span = slice(k * DEPTH, (k + 1) * DEPTH)
        u += mm(x[:, span], w[span])
    copies[1].wait()
    write_payload(out_ref, u / lengths(u), key[...])


def lengths(u):
    return jnp.sqrt(jnp.sum(u * u, axis=1, keepdims=True) + EPSILON)


def project(x, w, keys):
    return pl.pallas_call(
        project_kernel,
        in_specs=[pl.BlockSpec(memory_space=pltpu.HBM)] * 3,
        out_specs=VMEM,
        out_shape=jax.ShapeDtypeStruct((ROWS + KEY_ROWS, WIDTH), BF16),
        scratch_shapes=[
            pltpu.VMEM((ROWS, WIDTH), BF16),
            pltpu.VMEM((WIDTH, WIDTH), BF16),
            pltpu.VMEM((1, ROWS), jnp.int32),
            pltpu.SemaphoreType.DMA((2 + PIECES,)),
        ],
        compiler_params=params(56),
        cost_estimate=cost(2 * ROWS * WIDTH * WIDTH, 4 * 2**20),
    )(x, w, keys)


def add_tiles(with_stats, scal, mine, key_col, blocks, total, sums):
    heat, shift = scal[0], scal[1]
    for block in blocks:
        vec = block[:ROWS, :]
        keys = block[ROWS:, :LANES].astype(F32)
        same = key_col == keys[0:1] * 128.0 + keys[1:2]
        sim = nt(mine, vec)
        logits = heat * sim + shift
        z = jnp.where(same, -logits, logits)
        t = jnp.exp(-jnp.abs(z))
        q = 1.0 / (1.0 + t)
        sig = jnp.where(z >= 0, q, t * q)
        g = jnp.where(same, -sig, sig) * (1.0 / ROWS)
        total += mm(g.astype(BF16), vec)
        if with_stats:
            new = (jnp.maximum(z, 0.0) + jnp.log1p(t), g * sim, g)
            sums = [old + add for old, add in zip(sums, new)]
    return total, sums


def write_payload(out_ref, unit, key):
    digit = jnp.broadcast_to(key, (KEY_ROWS, ROWS))
    row = lax.broadcasted_iota(jnp.int32, (KEY_ROWS, ROWS), 0)
    digit = jnp.where(row == 0, digit >> 7, jnp.where(row == 1, digit & 127, 0))
    out_ref[:ROWS, :] = unit.astype(BF16)
    out_ref[ROWS:, :] = jnp.zeros((KEY_ROWS, WIDTH), BF16)
    out_ref[ROWS:, :ROWS] = digit.astype(F32).astype(BF16)


def early_kernel(first, scal, x, w_hbm, key, *refs):
    blocks, refs = refs[:-7], refs[-7:]
    total_ref, unit_ref, len_ref, key_ref, sum_ref, w, sem = refs
    own, blocks = (blocks[-1], blocks[:-1]) if first else (blocks[0], blocks[1:])
    copy = pltpu.make_async_copy(w_hbm, w, sem)
    copy.start()
    key_col = jnp.broadcast_to(key[...].astype(F32), (ROWS, ROWS)).T
    key_ref[...] = key_col

    def norm():
        copy.wait()
        u = mm(x[...], w[...])
        length = lengths(u)
        unit_ref[...] = u / length
        len_ref[...] = jnp.broadcast_to(length, len_ref.shape)

    if first:
        norm()
        write_payload(own, unit_ref[...], key[...])
    zero = jnp.zeros((ROWS, ROWS), F32)
    total, sums = add_tiles(
        first,
        scal,
        own[:ROWS, :],
        key_col,
        blocks,
        jnp.zeros((ROWS, WIDTH), F32),
        [zero] * 3,
    )
    total_ref[...] = total
    for k in range(3):
        sum_ref[k] = sums[k]
    if not first:
        norm()


def early(first, scal, x, w, keys, blocks):
    shapes = [(ROWS, WIDTH), (ROWS, WIDTH), (ROWS, LANES), (ROWS, ROWS), (3, ROWS, ROWS)]
    outs = [jax.ShapeDtypeStruct(shape, F32) for shape in shapes]
    if first:
        outs = [jax.ShapeDtypeStruct((ROWS + KEY_ROWS, WIDTH), BF16)] + outs
    hbm = pl.BlockSpec(memory_space=pltpu.HBM)
    return pl.pallas_call(
        functools.partial(early_kernel, first),
        in_specs=[SMEM, VMEM, hbm, VMEM] + [VMEM] * len(blocks),
        out_specs=[VMEM] * len(outs),
        out_shape=outs,
        scratch_shapes=[pltpu.VMEM((WIDTH, WIDTH), BF16), pltpu.SemaphoreType.DMA],
        compiler_params=params(56),
        cost_estimate=cost(4 * 5 * ROWS * ROWS * WIDTH, 8 * 2**20),
    )(scal, x, w, keys, *blocks)


def late_kernel(with_stats, ways, count, spot, scal, own, total_ref, unit, length, key, acc, *refs):
    blocks, outs, held = refs[:count], refs[count:-1], refs[-1]
    heat = scal[0]
    total, sums = add_tiles(
        with_stats,
        scal,
        own[:ROWS, :],
        key[...],
        blocks,
        total_ref[...],
        [acc[k] for k in range(3)],
    )
    total = total * heat
    u = unit[...]
    inner = jnp.sum(u * total, axis=1, keepdims=True)
    du = (total - u * inner) / length[:, :1]
    held[...] = du.T.astype(BF16).reshape(held.shape)
    if with_stats:
        def full(x):
            return jnp.sum(jnp.sum(x, axis=1, keepdims=True), axis=0, keepdims=True)

        lane = lax.broadcasted_iota(jnp.int32, (KEY_ROWS, LANES), 1)
        row = lax.broadcasted_iota(jnp.int32, (KEY_ROWS, LANES), 0)
        kind = lane % 3
        value = jnp.where(
            kind == 0,
            full(sums[0]) * (1.0 / ROWS),
            jnp.where(kind == 1, full(sums[1]) * heat, full(sums[2])),
        )
        value = jnp.where((row == 0) & (lane < 9), value, 0.0)
        high = value.astype(BF16).astype(F32)
        middle = (value - high).astype(BF16).astype(F32)
        low = value - high - middle
        parts = jnp.where(lane < 3, high, jnp.where(lane < 6, middle, low)).astype(BF16)
        out = outs[0]
        for w in range(ways):
            for h in range(2):
                out[w, h * COLS : (h + 1) * COLS, :] = held[h * ways + w]
            out[w, 2 * COLS :, :] = parts
    else:
        for step, out in enumerate(outs):
            w = lax.rem(spot[0] + step, ways)
            for h in range(2):
                out[h * COLS : (h + 1) * COLS, :] = held[h * ways + w]


def late(with_stats, ways, spot, scal, own, partial, blocks):
    if with_stats:
        shapes = [(ways, 2 * COLS + KEY_ROWS, ROWS)]
    else:
        shapes = [(2 * COLS, ROWS)] * ways
    return pl.pallas_call(
        functools.partial(late_kernel, with_stats, ways, len(blocks)),
        in_specs=[SMEM] * 2 + [VMEM] * (6 + len(blocks)),
        out_specs=[VMEM] * len(shapes),
        out_shape=[jax.ShapeDtypeStruct(shape, BF16) for shape in shapes],
        scratch_shapes=[pltpu.VMEM((2 * ways, COLS, ROWS), BF16)],
        compiler_params=params(56),
        cost_estimate=cost(4 * 2 * ROWS * ROWS * WIDTH, 4 * 2**20),
    )(spot, scal, own, *partial, *blocks)


def head_kernel(with_stats, spot, feat, *refs):
    spreads, (kept, given, held) = refs[:-3], refs[-3:]
    if with_stats:
        spreads = [spreads[0].at[w] for w in range(spreads[0].shape[0])]
    ways = len(spreads)
    total = jnp.zeros((2 * COLS, feat.shape[1]), F32)
    for step, spread in enumerate(spreads):
        source = step if with_stats else lax.rem(spot[0] + ways - step, ways)
        start = source * ROWS if with_stats else pl.multiple_of(source * ROWS, ROWS)
        rows = feat[pl.ds(start, ROWS), :]
        total += mm(spread[: 2 * COLS, :], rows)
    spare = None
    if with_stats:
        parts = jnp.zeros((KEY_ROWS, LANES), F32)
        for spread in spreads:
            parts += spread[2 * COLS :, :].astype(F32)
        lane = lax.broadcasted_iota(jnp.int32, (8, LANES), 1)
        row = lax.broadcasted_iota(jnp.int32, (8, LANES), 0)
        place = lane - STATS
        summed = jnp.zeros((8, LANES), F32)
        for k in range(3):
            number = jnp.sum(
                jnp.where((lane[:1] % 3 == k) & (lane[:1] < 9), parts[0:1], 0.0),
                axis=1,
                keepdims=True,
            )
            summed = jnp.where(place % 3 == k, number, summed)
        value = jnp.where((row == spot[1]) & (place >= 0) & (place < 9), summed, 0.0)
        high = value.astype(BF16).astype(F32)
        middle = (value - high).astype(BF16).astype(F32)
        low = value - high - middle
        spare = jnp.where(place < 3, high, jnp.where(place < 6, middle, low))
    for h in range(2):
        main = total[h * COLS : h * COLS + LANES, :].T
        rest = total[h * COLS + LANES : (h + 1) * COLS, :]
        for m in range(QUADS):
            for side in range(2):
                start = (2 * m + side) * CHUNK
                target = held.at[side, 2 * m + h]
                target[:CHUNK, :] = main[start : start + CHUNK]
                target[CHUNK:SLOT, :] = jnp.zeros((SLOT - CHUNK, LANES), F32)
                target[SLOT:, :] = jnp.zeros((8, LANES), F32) if spare is None else spare
                for k in range(2):
                    target[SLOT:, 64 * k : 64 * k + CHUNK] = rest[
                        8 * k : 8 * k + 8, start : start + CHUNK
                    ]
    kept[...] = held[spot[1]]
    given[...] = held[1 - spot[1]].astype(BF16)


def heads(with_stats, spot, feat, spreads):
    shape = (2 * QUADS, SLOT + 8, LANES)
    return pl.pallas_call(
        functools.partial(head_kernel, with_stats),
        in_specs=[SMEM] + [VMEM] * (1 + len(spreads)),
        out_specs=[VMEM, VMEM],
        out_shape=[jax.ShapeDtypeStruct(shape, F32), jax.ShapeDtypeStruct(shape, BF16)],
        scratch_shapes=[pltpu.VMEM((2, *shape), F32)],
        compiler_params=params(24),
        cost_estimate=cost(2 * 4 * ROWS * 2 * COLS * feat.shape[1], 4 * 2**20),
    )(spot, feat, *spreads)


def final_kernel(count, parts, out, stats):
    total = jnp.sum(parts[...].astype(F32), axis=0)
    out[:, :LANES] = total[:CHUNK]
    rest = total[SLOT:, :].T
    out[:, LANES : LANES + 8] = rest[:CHUNK]
    out[:, LANES + 8 :] = rest[64 : 64 + CHUNK]
    lane = lax.broadcasted_iota(jnp.int32, (1, LANES), 1)
    place = lane - STATS
    row = total[SLOT : SLOT + 1] + total[SLOT + 1 : SLOT + 2]
    answer = jnp.zeros((1, LANES), F32)
    for k in range(3):
        number = jnp.sum(
            jnp.where((place % 3 == k) & (place >= 0) & (place < 9), row, 0.0),
            axis=1,
            keepdims=True,
        )
        answer = jnp.where(lane == k, number, answer)
    stats[...] = answer * (1.0 / count)


def final(count, parts):
    return pl.pallas_call(
        functools.partial(final_kernel, count),
        in_specs=[VMEM],
        out_specs=[VMEM, VMEM],
        out_shape=[
            jax.ShapeDtypeStruct((CHUNK, COLS), F32),
            jax.ShapeDtypeStruct((1, LANES), F32),
        ],
        compiler_params=params(8),
        cost_estimate=cost(2 * QUADS * 48 * LANES, 2**20),
    )(parts)


def body(pictures, sentences, keys, picture_weights, sentence_weights, heat_log, shift_value):
    ways = lax.axis_size("dx")
    spot = jnp.stack([lax.axis_index("dx"), lax.axis_index("lc")]).astype(jnp.int32)
    scal = jnp.stack([jnp.exp(heat_log[0]), shift_value[0]])
    txt = project(sentences[0], sentence_weights, keys)
    txt_a = exchange(txt, "lz", 1)
    txt_y2 = exchange(txt, "ly", 2)
    txt_y1 = exchange(txt, "ly", 1)
    txt_c = exchange(txt, "lc", 1)
    img_feat = lax.all_gather(after(pictures[0], txt), "dx", axis=0, tiled=True)
    txt_feat = lax.all_gather(after(sentences[0], txt), "dx", axis=0, tiled=True)

    img, *img_part = early(True, scal, pictures[0], picture_weights, keys, [txt, txt_c])
    txt_b = exchange(after(txt_a, txt_y1, txt_y2), "lz", 3)
    img_a = exchange(after(img, txt_a), "lz", 1)
    img_c = exchange(after(img, txt_a, txt_y1, txt_y2), "lc", 1)
    img_n = after(img, img_c)
    img_y2 = exchange(img_n, "ly", 2)
    img_y1 = exchange(img_n, "ly", 1)
    img_b = exchange(img_a, "lz", 3)

    count = 2 * QUADS * lax.axis_size("dz") * ways

    def turn(array, step):
        return lax.ppermute(array, "dx", [(i, (i + step) % ways) for i in range(ways)])

    def share(with_stats, feat, spreads, *others):
        kept, given = heads(with_stats, spot, feat, spreads)
        taken = after(exchange(given, "lc", 1), *others)
        return (kept + taken.astype(F32)).astype(BF16)

    def collect(sums):
        return final(count, lax.all_to_all(sums, ("ly", "lz", "dz"), 0, 0, tiled=True))

    last = after(txt_b, img_feat, img_a, img_c, img_y1, img_y2)
    img_outs = late(True, ways, spot, scal, img, img_part, [txt_y1, txt_y2, txt_a, last])[0]
    img_cols = lax.all_to_all(img_outs, "dx", 0, 0, tiled=True)
    txt_part = early(
        False, scal, sentences[0], sentence_weights, keys, [txt, img, img_c, img_y1, img_y2, img_a]
    )
    img_sums = share(True, after(img_feat, img_b, *txt_part), [img_cols])
    last = after(img_b, img_sums)
    outs = late(False, ways, spot, scal, txt, txt_part, [last])
    *outs, txt_feat = lax.optimization_barrier((*outs, txt_feat))
    txt_cols = [outs[0]] + [turn(out, step) for step, out in enumerate(outs) if step]
    txt_sums = share(False, txt_feat, txt_cols)
    grad_img, stats = collect(img_sums)
    grad_txt, _ = collect(txt_sums)
    return grad_img, grad_txt, stats[0, :3]


def solution(mesh):
    split = Mesh(mesh.devices.reshape(4, 4, 2, 2, 4), ("ly", "lz", "lc", "dz", "dx"))
    dp = ("dz", "dx")
    return jax.shard_map(
        body,
        mesh=split,
        in_specs=(P(dp, LOSS, None), P(dp, LOSS, None), P(dp, LOSS), P(), P(), P(), P()),
        out_specs=(P(LOSS, dp), P(LOSS, dp), P()),
        check_vma=False,
    )
```

```python
import functools

import jax
import jax.numpy as jnp
from jax import lax
from jax.experimental import pallas as pl
from jax.experimental.pallas import tpu as pltpu
from jax.sharding import Mesh, PartitionSpec as P

EPSILON = 1e-06
LOSS = ("ly", "lz", "lc")
ROWS = 128
WIDTH = 1152
KEY_ROWS = 16
CHUNK = 36
SLOT = 40
COLS = 144
LANES = 128
TAIL = COLS - LANES
QUADS = 16
STATS = 112
DEPTH = 128
PIECES = WIDTH // DEPTH
F32 = jnp.float32
BF16 = jnp.bfloat16

VMEM = pl.BlockSpec(memory_space=pltpu.VMEM)
SMEM = pl.BlockSpec(memory_space=pltpu.SMEM)


def params(megabytes):
    return pltpu.CompilerParams(vmem_limit_bytes=megabytes * 2**20)


def cost(flops, moved):
    return pl.CostEstimate(flops=flops, bytes_accessed=moved, transcendentals=0)


def exchange(array, axis, apart):
    return lax.ppermute(array, axis, [(i, i ^ apart) for i in range(lax.axis_size(axis))])


def after(array, *others):
    return lax.optimization_barrier((array, *others))[0]


def nt(a, b):
    return lax.dot_general(a, b, (((1,), (1,)), ((), ())), preferred_element_type=F32)


def mm(a, b):
    return jnp.dot(a, b, preferred_element_type=F32)


def project_kernel(x_hbm, w_hbm, key_hbm, out_ref, x, w, key, sems):
    copies = [
        pltpu.make_async_copy(x_hbm, x, sems.at[0]),
        pltpu.make_async_copy(key_hbm, key, sems.at[1]),
    ]
    for k in range(PIECES):
        span = pl.ds(k * DEPTH, DEPTH)
        copies.append(pltpu.make_async_copy(w_hbm.at[span], w.at[span], sems.at[2 + k]))
    for copy in copies:
        copy.start()
    copies[0].wait()
    u = jnp.zeros((ROWS, WIDTH), F32)
    for k in range(PIECES):
        copies[2 + k].wait()
        span = slice(k * DEPTH, (k + 1) * DEPTH)
        u += mm(x[:, span], w[span])
    copies[1].wait()
    write_payload(out_ref, u / lengths(u), key[...])


def lengths(u):
    return jnp.sqrt(jnp.sum(u * u, axis=1, keepdims=True) + EPSILON)


def project(x, w, keys):
    return pl.pallas_call(
        project_kernel,
        in_specs=[pl.BlockSpec(memory_space=pltpu.HBM)] * 3,
        out_specs=VMEM,
        out_shape=jax.ShapeDtypeStruct((ROWS + KEY_ROWS, WIDTH), BF16),
        scratch_shapes=[
            pltpu.VMEM((ROWS, WIDTH), BF16),
            pltpu.VMEM((WIDTH, WIDTH), BF16),
            pltpu.VMEM((1, ROWS), jnp.int32),
            pltpu.SemaphoreType.DMA((2 + PIECES,)),
        ],
        compiler_params=params(56),
        cost_estimate=cost(2 * ROWS * WIDTH * WIDTH, 4 * 2**20),
    )(x, w, keys)


def add_tiles(with_stats, scal, mine, key_col, blocks, total, sums):
    heat, shift = scal[0], scal[1]
    for block in blocks:
        vec = block[:ROWS, :]
        keys = block[ROWS:, :LANES].astype(F32)
        same = key_col == keys[0:1] * 128.0 + keys[1:2]
        sim = nt(mine, vec)
        logits = heat * sim + shift
        z = jnp.where(same, -logits, logits)
        t = jnp.exp(-jnp.abs(z))
        q = 1.0 / (1.0 + t)
        sig = jnp.where(z >= 0, q, t * q)
        g = jnp.where(same, -sig, sig) * (1.0 / ROWS)
        total += mm(g.astype(BF16), vec)
        if with_stats:
            new = (jnp.maximum(z, 0.0) + jnp.log1p(t), g * sim, g)
            sums = [old + add for old, add in zip(sums, new)]
    return total, sums


def write_payload(out_ref, unit, key):
    digit = jnp.broadcast_to(key, (KEY_ROWS, ROWS))
    row = lax.broadcasted_iota(jnp.int32, (KEY_ROWS, ROWS), 0)
    digit = jnp.where(row == 0, digit >> 7, jnp.where(row == 1, digit & 127, 0))
    out_ref[:ROWS, :] = unit.astype(BF16)
    out_ref[ROWS:, :] = jnp.zeros((KEY_ROWS, WIDTH), BF16)
    out_ref[ROWS:, :ROWS] = digit.astype(F32).astype(BF16)


def early_kernel(first, scal, spot, x, w_hbm, key, *refs):
    blocks, refs = refs[:-7], refs[-7:]
    total_ref, unit_ref, len_ref, key_ref, sum_ref, w, sem = refs
    own, blocks = (blocks[-1], blocks[:-1]) if first else (blocks[0], blocks[1:])
    copy = pltpu.make_async_copy(w_hbm, w, sem)
    copy.start()
    key_col = jnp.broadcast_to(key[...].astype(F32), (ROWS, ROWS)).T
    key_ref[...] = key_col

    def norm():
        copy.wait()
        u = mm(x[...], w[...])
        length = lengths(u)
        unit_ref[...] = u / length
        len_ref[...] = jnp.broadcast_to(length, len_ref.shape)

    if first:
        norm()
        write_payload(own, unit_ref[...], key[...])
    zero = jnp.zeros((ROWS, ROWS), F32)
    total, sums = add_tiles(
        first,
        scal,
        own[:ROWS, :],
        key_col,
        blocks,
        jnp.zeros((ROWS, WIDTH), F32),
        [zero] * 3,
    )
    total_ref[...] = total
    for k in range(3):
        sum_ref[k] = sums[k]
    if not first:
        norm()


def early(first, scal, spot, x, w, keys, blocks):
    shapes = [(ROWS, WIDTH), (ROWS, WIDTH), (ROWS, LANES), (ROWS, ROWS), (3, ROWS, ROWS)]
    outs = [jax.ShapeDtypeStruct(shape, F32) for shape in shapes]
    if first:
        outs = [jax.ShapeDtypeStruct((ROWS + KEY_ROWS, WIDTH), BF16)] + outs
    hbm = pl.BlockSpec(memory_space=pltpu.HBM)
    return pl.pallas_call(
        functools.partial(early_kernel, first),
        in_specs=[SMEM, SMEM, VMEM, hbm, VMEM] + [VMEM] * len(blocks),
        out_specs=[VMEM] * len(outs),
        out_shape=outs,
        scratch_shapes=[pltpu.VMEM((WIDTH, WIDTH), BF16), pltpu.SemaphoreType.DMA],
        compiler_params=params(56),
        cost_estimate=cost(4 * 5 * ROWS * ROWS * WIDTH, 8 * 2**20),
    )(scal, spot, x, w, keys, *blocks)


def late_kernel(with_stats, ways, count, spot, scal, own, total_ref, unit, length, key, acc, *refs):
    blocks, outs, held = refs[:count], refs[count:-1], refs[-1]
    heat = scal[0]
    total, sums = add_tiles(
        with_stats,
        scal,
        own[:ROWS, :],
        key[...],
        blocks,
        total_ref[...],
        [acc[k] for k in range(3)],
    )
    total = total * heat
    u = unit[...]
    inner = jnp.sum(u * total, axis=1, keepdims=True)
    du = (total - u * inner) / length[:, :1]
    held[...] = du.T.astype(BF16).reshape(held.shape)
    if with_stats:
        def full(x):
            return jnp.sum(jnp.sum(x, axis=1, keepdims=True), axis=0, keepdims=True)

        lane = lax.broadcasted_iota(jnp.int32, (KEY_ROWS, LANES), 1)
        row = lax.broadcasted_iota(jnp.int32, (KEY_ROWS, LANES), 0)
        kind = lane % 3
        value = jnp.where(
            kind == 0,
            full(sums[0]) * (1.0 / ROWS),
            jnp.where(kind == 1, full(sums[1]) * heat, full(sums[2])),
        )
        value = jnp.where((row == 0) & (lane < 9), value, 0.0)
        high = value.astype(BF16).astype(F32)
        middle = (value - high).astype(BF16).astype(F32)
        low = value - high - middle
        parts = jnp.where(lane < 3, high, jnp.where(lane < 6, middle, low)).astype(BF16)
        for out in outs:
            out[2 * COLS :, :] = parts
    for step, out in enumerate(outs):
        w = lax.rem(spot[0] + step, ways)
        for h in range(2):
            out[h * COLS : (h + 1) * COLS, :] = held[h * ways + w]


def late(with_stats, ways, spot, scal, own, partial, blocks):
    shapes = [(2 * COLS + (KEY_ROWS if with_stats else 0), ROWS)] * ways
    return pl.pallas_call(
        functools.partial(late_kernel, with_stats, ways, len(blocks)),
        in_specs=[SMEM] * 2 + [VMEM] * (6 + len(blocks)),
        out_specs=[VMEM] * len(shapes),
        out_shape=[jax.ShapeDtypeStruct(shape, BF16) for shape in shapes],
        scratch_shapes=[pltpu.VMEM((2 * ways, COLS, ROWS), BF16)],
        compiler_params=params(56),
        cost_estimate=cost(4 * 2 * ROWS * ROWS * WIDTH, 4 * 2**20),
    )(spot, scal, own, *partial, *blocks)


def head_kernel(with_stats, spot, feat, *refs):
    spreads, (kept, given, held) = refs[:-3], refs[-3:]
    ways = len(spreads)
    total = jnp.zeros((2 * COLS, feat.shape[1]), F32)
    for step, spread in enumerate(spreads):
        source = lax.rem(spot[0] + ways - step, ways)
        rows = feat[pl.ds(pl.multiple_of(source * ROWS, ROWS), ROWS), :]
        total += mm(spread[: 2 * COLS, :], rows)
    spare = None
    if with_stats:
        parts = jnp.zeros((KEY_ROWS, LANES), F32)
        for spread in spreads:
            parts += spread[2 * COLS :, :].astype(F32)
        lane = lax.broadcasted_iota(jnp.int32, (8, LANES), 1)
        row = lax.broadcasted_iota(jnp.int32, (8, LANES), 0)
        place = lane - STATS
        summed = jnp.zeros((8, LANES), F32)
        for k in range(3):
            number = jnp.sum(
                jnp.where((lane[:1] % 3 == k) & (lane[:1] < 9), parts[0:1], 0.0),
                axis=1,
                keepdims=True,
            )
            summed = jnp.where(place % 3 == k, number, summed)
        value = jnp.where((row == spot[1]) & (place >= 0) & (place < 9), summed, 0.0)
        high = value.astype(BF16).astype(F32)
        middle = (value - high).astype(BF16).astype(F32)
        low = value - high - middle
        spare = jnp.where(place < 3, high, jnp.where(place < 6, middle, low))
    for h in range(2):
        main = total[h * COLS : h * COLS + LANES, :].T
        rest = total[h * COLS + LANES : (h + 1) * COLS, :]
        for m in range(QUADS):
            for side in range(2):
                start = (2 * m + side) * CHUNK
                target = held.at[side, 2 * m + h]
                target[:CHUNK, :] = main[start : start + CHUNK]
                target[CHUNK:SLOT, :] = jnp.zeros((SLOT - CHUNK, LANES), F32)
                target[SLOT:, :] = jnp.zeros((8, LANES), F32) if spare is None else spare
                for k in range(2):
                    target[SLOT:, 64 * k : 64 * k + CHUNK] = rest[
                        8 * k : 8 * k + 8, start : start + CHUNK
                    ]
    kept[...] = held[spot[1]]
    given[...] = held[1 - spot[1]].astype(BF16)


def heads(with_stats, spot, feat, spreads):
    shape = (2 * QUADS, SLOT + 8, LANES)
    return pl.pallas_call(
        functools.partial(head_kernel, with_stats),
        in_specs=[SMEM] + [VMEM] * (1 + len(spreads)),
        out_specs=[VMEM, VMEM],
        out_shape=[jax.ShapeDtypeStruct(shape, F32), jax.ShapeDtypeStruct(shape, BF16)],
        scratch_shapes=[pltpu.VMEM((2, *shape), F32)],
        compiler_params=params(24),
        cost_estimate=cost(2 * 4 * ROWS * 2 * COLS * feat.shape[1], 4 * 2**20),
    )(spot, feat, *spreads)


def final_kernel(count, parts, out, stats):
    total = jnp.sum(parts[...].astype(F32), axis=0)
    out[:, :LANES] = total[:CHUNK]
    rest = total[SLOT:, :].T
    out[:, LANES : LANES + 8] = rest[:CHUNK]
    out[:, LANES + 8 :] = rest[64 : 64 + CHUNK]
    lane = lax.broadcasted_iota(jnp.int32, (1, LANES), 1)
    place = lane - STATS
    row = total[SLOT : SLOT + 1] + total[SLOT + 1 : SLOT + 2]
    answer = jnp.zeros((1, LANES), F32)
    for k in range(3):
        number = jnp.sum(
            jnp.where((place % 3 == k) & (place >= 0) & (place < 9), row, 0.0),
            axis=1,
            keepdims=True,
        )
        answer = jnp.where(lane == k, number, answer)
    stats[...] = answer * (1.0 / count)


def final(count, parts):
    return pl.pallas_call(
        functools.partial(final_kernel, count),
        in_specs=[VMEM],
        out_specs=[VMEM, VMEM],
        out_shape=[
            jax.ShapeDtypeStruct((CHUNK, COLS), F32),
            jax.ShapeDtypeStruct((1, LANES), F32),
        ],
        compiler_params=params(8),
        cost_estimate=cost(2 * QUADS * 48 * LANES, 2**20),
    )(parts)


def body(pictures, sentences, keys, picture_weights, sentence_weights, heat_log, shift_value):
    ways = lax.axis_size("dx")
    spot = jnp.stack([lax.axis_index("dx"), lax.axis_index("lc")]).astype(jnp.int32)
    scal = jnp.stack([jnp.exp(heat_log[0]), shift_value[0]])
    txt = project(sentences[0], sentence_weights, keys)
    txt_a = exchange(txt, "lz", 1)
    txt_y2 = exchange(txt, "ly", 2)
    txt_y1 = exchange(txt, "ly", 1)
    txt_c = exchange(txt, "lc", 1)
    img_feat = lax.all_gather(after(pictures[0], txt), "dx", axis=0, tiled=True)
    txt_feat = lax.all_gather(after(sentences[0], txt), "dx", axis=0, tiled=True)

    img, *img_part = early(True, scal, spot, pictures[0], picture_weights, keys, [txt, txt_c])
    txt_b = exchange(after(txt_a, txt_y1, txt_y2), "lz", 3)
    img_a = exchange(after(img, txt_a), "lz", 1)
    img_c = exchange(after(img, txt_a, txt_y1, txt_y2), "lc", 1)
    img_n = after(img, img_c)
    img_y2 = exchange(img_n, "ly", 2)
    img_y1 = exchange(img_n, "ly", 1)
    img_b = exchange(img_a, "lz", 3)

    count = 2 * QUADS * lax.axis_size("dz") * ways

    def turn(array, step):
        return lax.ppermute(array, "dx", [(i, (i + step) % ways) for i in range(ways)])

    def share(with_stats, feat, spreads, *others):
        kept, given = heads(with_stats, spot, feat, spreads)
        taken = after(exchange(given, "lc", 1), *others)
        return (kept + taken.astype(F32)).astype(BF16)

    def columns(outs):
        return [outs[0]] + [turn(out, step) for step, out in enumerate(outs) if step]

    def collect(sums):
        return lax.all_to_all(sums, ("ly", "lz", "dz"), 0, 0, tiled=True)

    last = after(txt_b, img_feat, img_a, img_c, img_y1, img_y2)
    img_outs = late(True, ways, spot, scal, img, img_part, [txt_y1, txt_y2, txt_a, last])
    img_cols = columns(img_outs)
    txt_part = early(
        False, scal, spot, sentences[0], sentence_weights, keys, [txt, img, img_c, img_y1, img_y2, img_a]
    )
    img_sums = share(True, after(img_feat, img_b, *txt_part), img_cols)
    img_parts = collect(img_sums)
    last = after(img_b, img_sums)
    outs = late(False, ways, spot, scal, txt, txt_part, [last])
    *outs, txt_feat = lax.optimization_barrier((*outs, txt_feat))
    txt_cols = columns(outs)
    txt_parts = collect(share(False, after(txt_feat, img_parts), txt_cols))
    grad_img, stats = final(count, img_parts)
    grad_txt, _ = final(count, txt_parts)
    return grad_img, grad_txt, stats[0, :3]


def solution(mesh):
    split = Mesh(mesh.devices.reshape(4, 4, 2, 2, 4), ("ly", "lz", "lc", "dz", "dx"))
    dp = ("dz", "dx")
    return jax.shard_map(
        body,
        mesh=split,
        in_specs=(P(dp, LOSS, None), P(dp, LOSS, None), P(dp, LOSS), P(), P(), P(), P()),
        out_specs=(P(LOSS, dp), P(LOSS, dp), P()),
        check_vma=False,
    )
```

```python
import functools

import jax
import jax.numpy as jnp
from jax import lax
from jax.experimental import pallas as pl
from jax.experimental.pallas import tpu as pltpu
from jax.sharding import Mesh, PartitionSpec as P

EPSILON = 1e-06
LOSS = ("ly", "lz", "lc")
ROWS = 128
WIDTH = 1152
KEY_ROWS = 16
CHUNK = 36
SLOT = 40
COLS = 144
LANES = 128
TAIL = COLS - LANES
QUADS = 16
STATS = 112
DEPTH = 128
PIECES = WIDTH // DEPTH
SLAB = SLOT + 8
LINE = 4
FAR = 8
F32 = jnp.float32
BF16 = jnp.bfloat16

VMEM = pl.BlockSpec(memory_space=pltpu.VMEM)
SMEM = pl.BlockSpec(memory_space=pltpu.SMEM)


def params(megabytes):
    return pltpu.CompilerParams(vmem_limit_bytes=megabytes * 2**20)


def cost(flops, moved):
    return pl.CostEstimate(flops=flops, bytes_accessed=moved, transcendentals=0)


def exchange(array, axis, apart):
    return lax.ppermute(array, axis, [(i, i ^ apart) for i in range(lax.axis_size(axis))])


def after(array, *others):
    return lax.optimization_barrier((array, *others))[0]


def nt(a, b):
    return lax.dot_general(a, b, (((1,), (1,)), ((), ())), preferred_element_type=F32)


def mm(a, b):
    return jnp.dot(a, b, preferred_element_type=F32)


def project_kernel(x_hbm, w_hbm, key_hbm, out_ref, x, w, key, sems):
    copies = [
        pltpu.make_async_copy(x_hbm, x, sems.at[0]),
        pltpu.make_async_copy(key_hbm, key, sems.at[1]),
    ]
    for k in range(PIECES):
        span = pl.ds(k * DEPTH, DEPTH)
        copies.append(pltpu.make_async_copy(w_hbm.at[span], w.at[span], sems.at[2 + k]))
    for copy in copies:
        copy.start()
    copies[0].wait()
    u = jnp.zeros((ROWS, WIDTH), F32)
    for k in range(PIECES):
        copies[2 + k].wait()
        span = slice(k * DEPTH, (k + 1) * DEPTH)
        u += mm(x[:, span], w[span])
    copies[1].wait()
    write_payload(out_ref, u / lengths(u), key[...])


def lengths(u):
    return jnp.sqrt(jnp.sum(u * u, axis=1, keepdims=True) + EPSILON)


def project(x, w, keys):
    return pl.pallas_call(
        project_kernel,
        in_specs=[pl.BlockSpec(memory_space=pltpu.HBM)] * 3,
        out_specs=VMEM,
        out_shape=jax.ShapeDtypeStruct((ROWS + KEY_ROWS, WIDTH), BF16),
        scratch_shapes=[
            pltpu.VMEM((ROWS, WIDTH), BF16),
            pltpu.VMEM((WIDTH, WIDTH), BF16),
            pltpu.VMEM((1, ROWS), jnp.int32),
            pltpu.SemaphoreType.DMA((2 + PIECES,)),
        ],
        compiler_params=params(56),
        cost_estimate=cost(2 * ROWS * WIDTH * WIDTH, 4 * 2**20),
    )(x, w, keys)


def caption_row(block):
    digits = block[ROWS:, :LANES].astype(F32)
    return digits[0:1] * 128.0 + digits[1:2]


def add_tiles(with_stats, scal, mine, key_col, pairs, total, sums):
    heat, shift = scal[0], scal[1]
    for block, key_row in pairs:
        vec = block[:ROWS, :]
        same = key_col == key_row
        sim = nt(mine, vec)
        logits = heat * sim + shift
        z = jnp.where(same, -logits, logits)
        t = jnp.exp(-jnp.abs(z))
        q = 1.0 / (1.0 + t)
        sig = jnp.where(z >= 0, q, t * q)
        g = jnp.where(same, -sig, sig) * (1.0 / ROWS)
        total += mm(g.astype(BF16), vec)
        if with_stats:
            new = (jnp.maximum(z, 0.0) + jnp.log1p(t), g * sim, g)
            sums = [old + add for old, add in zip(sums, new)]
    return total, sums


def pair_up(blocks, rows_ref):
    pairs = []
    for k, block in enumerate(blocks):
        key_row = caption_row(block)
        rows_ref[k] = jnp.broadcast_to(key_row, (8, LANES))
        pairs.append((block, key_row))
    return pairs


def write_payload(out_ref, unit, key):
    digit = jnp.broadcast_to(key, (KEY_ROWS, ROWS))
    row = lax.broadcasted_iota(jnp.int32, (KEY_ROWS, ROWS), 0)
    digit = jnp.where(row == 0, digit >> 7, jnp.where(row == 1, digit & 127, 0))
    out_ref[:ROWS, :] = unit.astype(BF16)
    out_ref[ROWS:, :] = jnp.zeros((KEY_ROWS, WIDTH), BF16)
    out_ref[ROWS:, :ROWS] = digit.astype(F32).astype(BF16)


def early_kernel(first, scal, spot, x, w_hbm, key, *refs):
    refs, (total_ref, unit_ref, len_ref, key_ref, sum_ref, w, sem) = refs[:-7], refs[-7:]
    copy = pltpu.make_async_copy(w_hbm, w, sem)
    copy.start()
    key_col = jnp.broadcast_to(key[...].astype(F32), (ROWS, ROWS)).T
    key_ref[...] = key_col

    def norm():
        copy.wait()
        u = mm(x[...], w[...])
        length = lengths(u)
        unit_ref[...] = u / length
        len_ref[...] = jnp.broadcast_to(length, len_ref.shape)

    if first:
        blocks, (own, rows_ref) = refs[:-2], refs[-2:]
        norm()
        own[...] = unit_ref[...].astype(BF16)
        pairs = pair_up(blocks, rows_ref)
    else:
        own, near_rows, far_rows, *blocks = refs
        rows = [near_rows[0], near_rows[1], far_rows[0], far_rows[1], far_rows[2]]
        pairs = [(block, row[0:1]) for block, row in zip(blocks, rows)]
    zero = jnp.zeros((ROWS, ROWS), F32)
    total, sums = add_tiles(
        first,
        scal,
        own[:ROWS, :],
        key_col,
        pairs,
        jnp.zeros((ROWS, WIDTH), F32),
        [zero] * 3,
    )
    total_ref[...] = total
    for k in range(3):
        sum_ref[k] = sums[k]
    if not first:
        norm()


def early(first, scal, spot, x, w, keys, blocks):
    shapes = [(ROWS, WIDTH), (ROWS, WIDTH), (ROWS, LANES), (ROWS, ROWS), (3, ROWS, ROWS)]
    outs = [jax.ShapeDtypeStruct(shape, F32) for shape in shapes]
    if first:
        outs = [
            jax.ShapeDtypeStruct((ROWS, WIDTH), BF16),
            jax.ShapeDtypeStruct((len(blocks), 8, LANES), F32),
        ] + outs
    hbm = pl.BlockSpec(memory_space=pltpu.HBM)
    return pl.pallas_call(
        functools.partial(early_kernel, first),
        in_specs=[SMEM, SMEM, VMEM, hbm, VMEM] + [VMEM] * len(blocks),
        out_specs=[VMEM] * len(outs),
        out_shape=outs,
        scratch_shapes=[pltpu.VMEM((WIDTH, WIDTH), BF16), pltpu.SemaphoreType.DMA],
        compiler_params=params(56),
        cost_estimate=cost(4 * 5 * ROWS * ROWS * WIDTH, 8 * 2**20),
    )(scal, spot, x, w, keys, *blocks)


def late_kernel(with_stats, ways, count, spot, scal, own, total_ref, unit, length, key, acc, *refs):
    blocks, outs, held = refs[:count], refs[count:-1], refs[-1]
    heat = scal[0]
    if with_stats:
        *outs, rows_ref = outs
        pairs = pair_up(blocks, rows_ref)
    else:
        rows, block = blocks
        pairs = [(block, rows[3][0:1])]
    total, sums = add_tiles(
        with_stats,
        scal,
        own[:ROWS, :],
        key[...],
        pairs,
        total_ref[...],
        [acc[k] for k in range(3)],
    )
    total = total * heat
    u = unit[...]
    inner = jnp.sum(u * total, axis=1, keepdims=True)
    du = (total - u * inner) / length[:, :1]
    held[...] = du.T.astype(BF16).reshape(held.shape)
    if with_stats:
        def full(x):
            return jnp.sum(jnp.sum(x, axis=1, keepdims=True), axis=0, keepdims=True)

        lane = lax.broadcasted_iota(jnp.int32, (KEY_ROWS, LANES), 1)
        row = lax.broadcasted_iota(jnp.int32, (KEY_ROWS, LANES), 0)
        kind = lane % 3
        value = jnp.where(
            kind == 0,
            full(sums[0]) * (1.0 / ROWS),
            jnp.where(kind == 1, full(sums[1]) * heat, full(sums[2])),
        )
        value = jnp.where((row == 0) & (lane < 9), value, 0.0)
        high = value.astype(BF16).astype(F32)
        middle = (value - high).astype(BF16).astype(F32)
        low = value - high - middle
        parts = jnp.where(lane < 3, high, jnp.where(lane < 6, middle, low)).astype(BF16)
        for out in outs:
            out[2 * COLS :, :] = parts
    for step, out in enumerate(outs):
        w = lax.rem(spot[0] + step, ways)
        for h in range(2):
            out[h * COLS : (h + 1) * COLS, :] = held[h * ways + w]


def late(with_stats, ways, spot, scal, own, partial, blocks):
    rows = 2 * COLS + (KEY_ROWS if with_stats else 0)
    shapes = [jax.ShapeDtypeStruct((rows, ROWS), BF16)] * ways
    if with_stats:
        shapes.append(jax.ShapeDtypeStruct((len(blocks), 8, LANES), F32))
    return pl.pallas_call(
        functools.partial(late_kernel, with_stats, ways, len(blocks)),
        in_specs=[SMEM] * 2 + [VMEM] * (6 + len(blocks)),
        out_specs=[VMEM] * len(shapes),
        out_shape=shapes,
        scratch_shapes=[pltpu.VMEM((2 * ways, COLS, ROWS), BF16)],
        compiler_params=params(56),
        cost_estimate=cost(4 * 2 * ROWS * ROWS * WIDTH, 4 * 2**20),
    )(spot, scal, own, *partial, *blocks)


def head_kernel(with_stats, spot, feat, *refs):
    spreads, (kept, given, held) = refs[:-3], refs[-3:]
    ways = len(spreads)
    total = jnp.zeros((2 * COLS, feat.shape[1]), F32)
    for step, spread in enumerate(spreads):
        source = lax.rem(spot[0] + ways - step, ways)
        rows = feat[pl.ds(pl.multiple_of(source * ROWS, ROWS), ROWS), :]
        total += mm(spread[: 2 * COLS, :], rows)
    spare = None
    if with_stats:
        parts = jnp.zeros((KEY_ROWS, LANES), F32)
        for spread in spreads:
            parts += spread[2 * COLS :, :].astype(F32)
        lane = lax.broadcasted_iota(jnp.int32, (8, LANES), 1)
        row = lax.broadcasted_iota(jnp.int32, (8, LANES), 0)
        place = lane - STATS
        summed = jnp.zeros((8, LANES), F32)
        for k in range(3):
            number = jnp.sum(
                jnp.where((lane[:1] % 3 == k) & (lane[:1] < 9), parts[0:1], 0.0),
                axis=1,
                keepdims=True,
            )
            summed = jnp.where(place % 3 == k, number, summed)
        value = jnp.where((row == spot[1]) & (place >= 0) & (place < 9), summed, 0.0)
        high = value.astype(BF16).astype(F32)
        middle = (value - high).astype(BF16).astype(F32)
        low = value - high - middle
        spare = jnp.where(place < 3, high, jnp.where(place < 6, middle, low))
    for h in range(2):
        main = total[h * COLS : h * COLS + LANES, :].T
        rest = total[h * COLS + LANES : (h + 1) * COLS, :]
        for m in range(QUADS):
            for side in range(2):
                start = (2 * m + side) * CHUNK
                target = held.at[side, 2 * m + h]
                target[:CHUNK, :] = main[start : start + CHUNK]
                target[CHUNK:SLOT, :] = jnp.zeros((SLOT - CHUNK, LANES), F32)
                target[SLOT:, :] = jnp.zeros((8, LANES), F32) if spare is None else spare
                for k in range(2):
                    target[SLOT:, 64 * k : 64 * k + CHUNK] = rest[
                        8 * k : 8 * k + 8, start : start + CHUNK
                    ]
    kept[...] = held[spot[1]]
    given[...] = held[1 - spot[1]].astype(BF16)


def heads(with_stats, spot, feat, spreads):
    shape = (2 * QUADS, SLOT + 8, LANES)
    return pl.pallas_call(
        functools.partial(head_kernel, with_stats),
        in_specs=[SMEM] + [VMEM] * (1 + len(spreads)),
        out_specs=[VMEM, VMEM],
        out_shape=[jax.ShapeDtypeStruct(shape, F32), jax.ShapeDtypeStruct(shape, BF16)],
        scratch_shapes=[pltpu.VMEM((2, *shape), F32)],
        compiler_params=params(24),
        cost_estimate=cost(2 * 4 * ROWS * 2 * COLS * feat.shape[1], 4 * 2**20),
    )(spot, feat, *spreads)


def mix_kernel(spot, kept_img, taken_img, kept_txt, taken_txt, mine, *outs):
    def part(place):
        span = pl.ds(place * FAR, FAR)
        img = kept_img[span] + taken_img[span].astype(F32)
        txt = kept_txt[span] + taken_txt[span].astype(F32)
        return img, txt

    img, txt = part(spot[2])
    mine[:, :SLAB, :] = img
    mine[:, SLAB:, :] = txt
    for step, out in enumerate(outs):
        img, txt = part(lax.rem(spot[2] + step + 1, LINE))
        out[:, :SLAB, :] = img.astype(BF16)
        out[:, SLAB:, :] = txt.astype(BF16)


def mix(spot, *arrays):
    shape = (FAR, 2 * SLAB, LANES)
    return pl.pallas_call(
        mix_kernel,
        in_specs=[SMEM] + [VMEM] * 4,
        out_specs=[VMEM] * LINE,
        out_shape=[jax.ShapeDtypeStruct(shape, F32)]
        + [jax.ShapeDtypeStruct(shape, BF16)] * (LINE - 1),
        compiler_params=params(16),
        cost_estimate=cost(4 * FAR * SLAB * LANES, 2**20),
    )(spot, *arrays)


def fold_kernel(mine, *refs):
    total = mine[...]
    for part in refs[:-1]:
        total += part[...].astype(F32)
    refs[-1][...] = total.astype(BF16)


def fold(mine, parts):
    return pl.pallas_call(
        fold_kernel,
        in_specs=[VMEM] * (1 + len(parts)),
        out_specs=VMEM,
        out_shape=jax.ShapeDtypeStruct(mine.shape, BF16),
        compiler_params=params(16),
        cost_estimate=cost(4 * FAR * SLAB * LANES, 2**20),
    )(mine, *parts)


def final_kernel(count, parts, out_img, out_txt, stats):
    both = jnp.sum(parts[...].astype(F32), axis=0)
    for out, total in ((out_img, both[:SLAB]), (out_txt, both[SLAB:])):
        out[:, :LANES] = total[:CHUNK]
        rest = total[SLOT:, :].T
        out[:, LANES : LANES + 8] = rest[:CHUNK]
        out[:, LANES + 8 :] = rest[64 : 64 + CHUNK]
    place = lax.broadcasted_iota(jnp.int32, (1, LANES), 1) - STATS
    row = both[SLOT : SLOT + 1] + both[SLOT + 1 : SLOT + 2]
    for k in range(3):
        chosen = jnp.where((place % 3 == k) & (place >= 0) & (place < 9), row, 0.0)
        stats[k] = jnp.sum(chosen) * (1.0 / count)


def final(count, parts):
    grad = jax.ShapeDtypeStruct((CHUNK, COLS), F32)
    return pl.pallas_call(
        functools.partial(final_kernel, count),
        in_specs=[VMEM],
        out_specs=[VMEM, VMEM, SMEM],
        out_shape=[grad, grad, jax.ShapeDtypeStruct((3,), F32)],
        compiler_params=params(8),
        cost_estimate=cost(4 * FAR * SLAB * LANES, 2**20),
    )(parts)


def body(pictures, sentences, keys, picture_weights, sentence_weights, heat_log, shift_value):
    ways = lax.axis_size("dx")
    spot = jnp.stack([lax.axis_index(axis) for axis in ("dx", "lc", "ly")]).astype(jnp.int32)
    scal = jnp.stack([jnp.exp(heat_log[0]), shift_value[0]])
    txt = project(sentences[0], sentence_weights, keys)
    txt_a = exchange(txt, "lz", 1)
    txt_y2 = exchange(txt, "ly", 2)
    txt_y1 = exchange(txt, "ly", 1)
    txt_c = exchange(txt, "lc", 1)
    img_feat = lax.all_gather(after(pictures[0], txt), "dx", axis=0, tiled=True)
    txt_feat = lax.all_gather(after(sentences[0], txt), "dx", axis=0, tiled=True)

    img, near_rows, *img_part = early(True, scal, spot, pictures[0], picture_weights, keys, [txt, txt_c])
    txt_b = exchange(after(txt_a, txt_y1, txt_y2), "lz", 3)
    img_a = exchange(after(img, txt_a), "lz", 1)
    img_c = exchange(after(img, txt_a, txt_y1, txt_y2), "lc", 1)
    img_n = after(img, img_c)
    img_y2 = exchange(img_n, "ly", 2)
    img_y1 = exchange(img_n, "ly", 1)
    img_b = exchange(img_a, "lz", 3)

    count = 2 * QUADS * lax.axis_size("dz") * ways

    def turn(array, axis, step):
        size = lax.axis_size(axis)
        return lax.ppermute(array, axis, [(i, (i + step) % size) for i in range(size)])

    def columns(outs):
        return [outs[0]] + [turn(out, "dx", step) for step, out in enumerate(outs) if step]

    last = after(txt_b, img_feat, img_a, img_c, img_y1, img_y2)
    *img_outs, far_rows = late(
        True, ways, spot, scal, img, img_part, [txt_y1, txt_y2, txt_a, last]
    )
    img_cols = columns(img_outs)
    txt_part = early(
        False,
        scal,
        spot,
        sentences[0],
        sentence_weights,
        keys,
        [txt, near_rows, far_rows, img, img_c, img_y1, img_y2, img_a],
    )
    last = after(img_b, *img_cols, *txt_part)
    outs = late(False, ways, spot, scal, txt, txt_part, [far_rows, last])
    txt_cols = columns(outs)
    img_kept, img_given = heads(True, spot, after(img_feat, outs[0]), img_cols)
    img_taken = exchange(img_given, "lc", 1)
    txt_kept, txt_given = heads(False, spot, txt_feat, txt_cols)
    txt_taken = exchange(txt_given, "lc", 1)
    mine, *others = mix(spot, img_kept, img_taken, txt_kept, txt_taken)
    others = [turn(other, "ly", step + 1) for step, other in enumerate(others)]
    sums = lax.all_to_all(fold(mine, others), ("lz", "dz"), 0, 0, tiled=True)
    grad_img, grad_txt, stats = final(count, sums)
    return grad_img, grad_txt, stats


def solution(mesh):
    split = Mesh(mesh.devices.reshape(4, 4, 2, 2, 4), ("ly", "lz", "lc", "dz", "dx"))
    dp = ("dz", "dx")
    return jax.shard_map(
        body,
        mesh=split,
        in_specs=(P(dp, LOSS, None), P(dp, LOSS, None), P(dp, LOSS), P(), P(), P(), P()),
        out_specs=(P(LOSS, dp), P(LOSS, dp), P()),
        check_vma=False,
    )
```

```python
import functools

import jax
import jax.numpy as jnp
from jax import lax
from jax.experimental import pallas as pl
from jax.experimental.pallas import tpu as pltpu
from jax.sharding import Mesh, PartitionSpec as P

EPSILON = 1e-06
LOSS = ("ly", "lz", "lc")
ROWS = 128
WIDTH = 1152
KEY_ROWS = 16
CHUNK = 36
SLOT = 40
COLS = 144
LANES = 128
TAIL = COLS - LANES
QUADS = 16
STATS = 112
DEPTH = 128
PIECES = WIDTH // DEPTH
SLAB = SLOT + 8
F32 = jnp.float32
BF16 = jnp.bfloat16

VMEM = pl.BlockSpec(memory_space=pltpu.VMEM)
SMEM = pl.BlockSpec(memory_space=pltpu.SMEM)


def params(megabytes):
    return pltpu.CompilerParams(vmem_limit_bytes=megabytes * 2**20)


def cost(flops, moved):
    return pl.CostEstimate(flops=flops, bytes_accessed=moved, transcendentals=0)


def exchange(array, axis, apart):
    return lax.ppermute(array, axis, [(i, i ^ apart) for i in range(lax.axis_size(axis))])


def after(array, *others):
    return lax.optimization_barrier((array, *others))[0]


def nt(a, b):
    return lax.dot_general(a, b, (((1,), (1,)), ((), ())), preferred_element_type=F32)


def mm(a, b):
    return jnp.dot(a, b, preferred_element_type=F32)


def project_kernel(x_hbm, w_hbm, key_hbm, out_ref, x, w, key, sems):
    copies = [
        pltpu.make_async_copy(x_hbm, x, sems.at[0]),
        pltpu.make_async_copy(key_hbm, key, sems.at[1]),
    ]
    for k in range(PIECES):
        span = pl.ds(k * DEPTH, DEPTH)
        copies.append(pltpu.make_async_copy(w_hbm.at[span], w.at[span], sems.at[2 + k]))
    for copy in copies:
        copy.start()
    copies[0].wait()
    u = jnp.zeros((ROWS, WIDTH), F32)
    for k in range(PIECES):
        copies[2 + k].wait()
        span = slice(k * DEPTH, (k + 1) * DEPTH)
        u += mm(x[:, span], w[span])
    copies[1].wait()
    write_payload(out_ref, u / lengths(u), key[...])


def lengths(u):
    return jnp.sqrt(jnp.sum(u * u, axis=1, keepdims=True) + EPSILON)


def project(x, w, keys):
    return pl.pallas_call(
        project_kernel,
        in_specs=[pl.BlockSpec(memory_space=pltpu.HBM)] * 3,
        out_specs=VMEM,
        out_shape=jax.ShapeDtypeStruct((ROWS + KEY_ROWS, WIDTH), BF16),
        scratch_shapes=[
            pltpu.VMEM((ROWS, WIDTH), BF16),
            pltpu.VMEM((WIDTH, WIDTH), BF16),
            pltpu.VMEM((1, ROWS), jnp.int32),
            pltpu.SemaphoreType.DMA((2 + PIECES,)),
        ],
        compiler_params=params(56),
        cost_estimate=cost(2 * ROWS * WIDTH * WIDTH, 4 * 2**20),
    )(x, w, keys)


def temperature(heat_log):
    return jnp.exp(jnp.full((1, 1), heat_log[0], F32))


def caption_row(block):
    digits = block[ROWS:, :LANES].astype(F32)
    return digits[0:1] * 128.0 + digits[1:2]


def add_tiles(with_stats, heat, shift, mine, key_col, pairs, total, sums):
    for block, key_row in pairs:
        vec = block[:ROWS, :]
        same = key_col == key_row
        sim = nt(mine, vec)
        logits = heat * sim + shift
        z = jnp.where(same, -logits, logits)
        t = jnp.exp(-jnp.abs(z))
        q = 1.0 / (1.0 + t)
        sig = jnp.where(z >= 0, q, t * q)
        g = jnp.where(same, -sig, sig) * (1.0 / ROWS)
        total += mm(g.astype(BF16), vec)
        if with_stats:
            new = (jnp.maximum(z, 0.0) + jnp.log1p(t), g * sim, g)
            sums = [old + add for old, add in zip(sums, new)]
    return total, sums


def pair_up(blocks, rows_ref):
    pairs = []
    for k, block in enumerate(blocks):
        key_row = caption_row(block)
        rows_ref[k] = jnp.broadcast_to(key_row, (8, LANES))
        pairs.append((block, key_row))
    return pairs


def write_payload(out_ref, unit, key):
    digit = jnp.broadcast_to(key, (KEY_ROWS, ROWS))
    row = lax.broadcasted_iota(jnp.int32, (KEY_ROWS, ROWS), 0)
    digit = jnp.where(row == 0, digit >> 7, jnp.where(row == 1, digit & 127, 0))
    out_ref[:ROWS, :] = unit.astype(BF16)
    out_ref[ROWS:, :] = jnp.zeros((KEY_ROWS, WIDTH), BF16)
    out_ref[ROWS:, :ROWS] = digit.astype(F32).astype(BF16)


def early_kernel(first, heat_log, shift, x, w_hbm, key, *refs):
    refs, (total_ref, unit_ref, len_ref, key_ref, sum_ref, w, sem) = refs[:-7], refs[-7:]
    copy = pltpu.make_async_copy(w_hbm, w, sem)
    copy.start()
    key_col = jnp.broadcast_to(key[...].astype(F32), (ROWS, ROWS)).T
    key_ref[...] = key_col

    def norm():
        copy.wait()
        u = mm(x[...], w[...])
        length = lengths(u)
        unit_ref[...] = u / length
        len_ref[...] = jnp.broadcast_to(length, len_ref.shape)

    if first:
        blocks, (own, rows_ref) = refs[:-2], refs[-2:]
        norm()
        own[...] = unit_ref[...].astype(BF16)
        pairs = pair_up(blocks, rows_ref)
    else:
        own, near_rows, far_rows, *blocks = refs
        rows = [near_rows[0], near_rows[1], far_rows[0], far_rows[1], far_rows[2]]
        pairs = [(block, row[0:1]) for block, row in zip(blocks, rows)]
    zero = jnp.zeros((ROWS, ROWS), F32)
    total, sums = add_tiles(
        first,
        temperature(heat_log),
        shift[0],
        own[:ROWS, :],
        key_col,
        pairs,
        jnp.zeros((ROWS, WIDTH), F32),
        [zero] * 3,
    )
    total_ref[...] = total
    for k in range(3):
        sum_ref[k] = sums[k]
    if not first:
        norm()


def early(first, scal, x, w, keys, blocks):
    shapes = [(ROWS, WIDTH), (ROWS, WIDTH), (ROWS, LANES), (ROWS, ROWS), (3, ROWS, ROWS)]
    outs = [jax.ShapeDtypeStruct(shape, F32) for shape in shapes]
    if first:
        outs = [
            jax.ShapeDtypeStruct((ROWS, WIDTH), BF16),
            jax.ShapeDtypeStruct((len(blocks), 8, LANES), F32),
        ] + outs
    hbm = pl.BlockSpec(memory_space=pltpu.HBM)
    return pl.pallas_call(
        functools.partial(early_kernel, first),
        in_specs=[SMEM, SMEM, VMEM, hbm, VMEM] + [VMEM] * len(blocks),
        out_specs=[VMEM] * len(outs),
        out_shape=outs,
        scratch_shapes=[pltpu.VMEM((WIDTH, WIDTH), BF16), pltpu.SemaphoreType.DMA],
        compiler_params=params(56),
        cost_estimate=cost(4 * 5 * ROWS * ROWS * WIDTH, 8 * 2**20),
    )(*scal, x, w, keys, *blocks)


def late_kernel(with_stats, ways, count, spot, heat_log, shift, own, *refs):
    total_ref, unit, length, key, acc, *refs = refs
    blocks, outs, held = refs[:count], refs[count:-1], refs[-1]
    heat = temperature(heat_log)
    if with_stats:
        *outs, rows_ref = outs
        pairs = pair_up(blocks, rows_ref)
    else:
        rows, block = blocks
        pairs = [(block, rows[3][0:1])]
    total, sums = add_tiles(
        with_stats,
        heat,
        shift[0],
        own[:ROWS, :],
        key[...],
        pairs,
        total_ref[...],
        [acc[k] for k in range(3)],
    )
    total = total * heat
    u = unit[...]
    inner = jnp.sum(u * total, axis=1, keepdims=True)
    du = (total - u * inner) / length[:, :1]
    held[...] = du.T.astype(BF16).reshape(held.shape)
    if with_stats:
        def full(x):
            return jnp.sum(jnp.sum(x, axis=1, keepdims=True), axis=0, keepdims=True)

        lane = lax.broadcasted_iota(jnp.int32, (KEY_ROWS, LANES), 1)
        row = lax.broadcasted_iota(jnp.int32, (KEY_ROWS, LANES), 0)
        kind = lane % 3
        value = jnp.where(
            kind == 0,
            full(sums[0]) * (1.0 / ROWS),
            jnp.where(kind == 1, full(sums[1]) * heat, full(sums[2])),
        )
        value = jnp.where((row == 0) & (lane < 9), value, 0.0)
        high = value.astype(BF16).astype(F32)
        middle = (value - high).astype(BF16).astype(F32)
        low = value - high - middle
        parts = jnp.where(lane < 3, high, jnp.where(lane < 6, middle, low)).astype(BF16)
        for out in outs:
            out[2 * COLS :, :] = parts
    for step, out in enumerate(outs):
        w = lax.rem(spot[0] + step, ways)
        for h in range(2):
            out[h * COLS : (h + 1) * COLS, :] = held[h * ways + w]


def late(with_stats, ways, spot, scal, own, partial, blocks):
    rows = 2 * COLS + (KEY_ROWS if with_stats else 0)
    shapes = [jax.ShapeDtypeStruct((rows, ROWS), BF16)] * ways
    if with_stats:
        shapes.append(jax.ShapeDtypeStruct((len(blocks), 8, LANES), F32))
    return pl.pallas_call(
        functools.partial(late_kernel, with_stats, ways, len(blocks)),
        in_specs=[SMEM] * 3 + [VMEM] * (6 + len(blocks)),
        out_specs=[VMEM] * len(shapes),
        out_shape=shapes,
        scratch_shapes=[pltpu.VMEM((2 * ways, COLS, ROWS), BF16)],
        compiler_params=params(56),
        cost_estimate=cost(4 * 2 * ROWS * ROWS * WIDTH, 4 * 2**20),
    )(spot, *scal, own, *partial, *blocks)


def head_kernel(with_stats, spot, feat, *refs):
    spreads, (kept, given, held) = refs[:-3], refs[-3:]
    ways = len(spreads)
    total = jnp.zeros((2 * COLS, feat.shape[1]), F32)
    for step, spread in enumerate(spreads):
        source = lax.rem(spot[0] + ways - step, ways)
        rows = feat[pl.ds(pl.multiple_of(source * ROWS, ROWS), ROWS), :]
        total += mm(spread[: 2 * COLS, :], rows)
    spare = None
    if with_stats:
        parts = jnp.zeros((KEY_ROWS, LANES), F32)
        for spread in spreads:
            parts += spread[2 * COLS :, :].astype(F32)
        lane = lax.broadcasted_iota(jnp.int32, (8, LANES), 1)
        row = lax.broadcasted_iota(jnp.int32, (8, LANES), 0)
        place = lane - STATS
        summed = jnp.zeros((8, LANES), F32)
        for k in range(3):
            number = jnp.sum(
                jnp.where((lane[:1] % 3 == k) & (lane[:1] < 9), parts[0:1], 0.0),
                axis=1,
                keepdims=True,
            )
            summed = jnp.where(place % 3 == k, number, summed)
        value = jnp.where((row == spot[1]) & (place >= 0) & (place < 9), summed, 0.0)
        high = value.astype(BF16).astype(F32)
        middle = (value - high).astype(BF16).astype(F32)
        low = value - high - middle
        spare = jnp.where(place < 3, high, jnp.where(place < 6, middle, low))
    for h in range(2):
        main = total[h * COLS : h * COLS + LANES, :].T
        rest = total[h * COLS + LANES : (h + 1) * COLS, :]
        for m in range(QUADS):
            for side in range(2):
                start = (2 * m + side) * CHUNK
                target = held.at[side, 2 * m + h]
                target[:CHUNK, :] = main[start : start + CHUNK]
                target[CHUNK:SLOT, :] = jnp.zeros((SLOT - CHUNK, LANES), F32)
                target[SLOT:, :] = jnp.zeros((8, LANES), F32) if spare is None else spare
                for k in range(2):
                    target[SLOT:, 64 * k : 64 * k + CHUNK] = rest[
                        8 * k : 8 * k + 8, start : start + CHUNK
                    ]
    kept[...] = held[spot[1]]
    given[...] = held[1 - spot[1]].astype(BF16)


def heads(with_stats, spot, feat, spreads):
    shape = (2 * QUADS, SLOT + 8, LANES)
    return pl.pallas_call(
        functools.partial(head_kernel, with_stats),
        in_specs=[SMEM] + [VMEM] * (1 + len(spreads)),
        out_specs=[VMEM, VMEM],
        out_shape=[jax.ShapeDtypeStruct(shape, F32), jax.ShapeDtypeStruct(shape, BF16)],
        scratch_shapes=[pltpu.VMEM((2, *shape), F32)],
        compiler_params=params(24),
        cost_estimate=cost(2 * 4 * ROWS * 2 * COLS * feat.shape[1], 4 * 2**20),
    )(spot, feat, *spreads)


def mix_kernel(kept_img, taken_img, kept_txt, taken_txt, out):
    out[:, :SLAB, :] = (kept_img[...] + taken_img[...].astype(F32)).astype(BF16)
    out[:, SLAB:, :] = (kept_txt[...] + taken_txt[...].astype(F32)).astype(BF16)


def mix(*arrays):
    return pl.pallas_call(
        mix_kernel,
        in_specs=[VMEM] * 4,
        out_specs=VMEM,
        out_shape=jax.ShapeDtypeStruct((2 * QUADS, 2 * SLAB, LANES), BF16),
        compiler_params=params(16),
        cost_estimate=cost(4 * QUADS * SLAB * LANES, 2**20),
    )(*arrays)


def final_kernel(count, parts, out_img, out_txt, stats):
    both = jnp.sum(parts[...].astype(F32), axis=0)
    for out, total in ((out_img, both[:SLAB]), (out_txt, both[SLAB:])):
        out[:, :LANES] = total[:CHUNK]
        rest = total[SLOT:, :].T
        out[:, LANES : LANES + 8] = rest[:CHUNK]
        out[:, LANES + 8 :] = rest[64 : 64 + CHUNK]
    place = lax.broadcasted_iota(jnp.int32, (1, LANES), 1) - STATS
    row = both[SLOT : SLOT + 1] + both[SLOT + 1 : SLOT + 2]
    for k in range(3):
        chosen = jnp.where((place % 3 == k) & (place >= 0) & (place < 9), row, 0.0)
        stats[k] = jnp.sum(chosen) * (1.0 / count)


def final(count, parts):
    grad = jax.ShapeDtypeStruct((CHUNK, COLS), F32)
    return pl.pallas_call(
        functools.partial(final_kernel, count),
        in_specs=[VMEM],
        out_specs=[VMEM, VMEM, SMEM],
        out_shape=[grad, grad, jax.ShapeDtypeStruct((3,), F32)],
        compiler_params=params(8),
        cost_estimate=cost(4 * QUADS * SLAB * LANES, 2**20),
    )(parts)


def body(pictures, sentences, keys, picture_weights, sentence_weights, heat_log, shift_value):
    ways = lax.axis_size("dx")
    spot = jnp.stack([lax.axis_index(axis) for axis in ("dx", "lc")]).astype(jnp.int32)
    scal = (heat_log, shift_value)
    txt = project(sentences[0], sentence_weights, keys)
    txt_a = exchange(txt, "lz", 1)
    txt_y2 = exchange(txt, "ly", 2)
    txt_y1 = exchange(txt, "ly", 1)
    txt_c = exchange(txt, "lc", 1)
    img_feat = lax.all_gather(after(pictures[0], txt), "dx", axis=0, tiled=True)
    txt_feat = lax.all_gather(after(sentences[0], txt), "dx", axis=0, tiled=True)

    img, near_rows, *img_part = early(True, scal, pictures[0], picture_weights, keys, [txt, txt_c])
    txt_b = exchange(after(txt_a, txt_y1, txt_y2), "lz", 3)
    img_a = exchange(img, "lz", 1)
    img_c = exchange(after(img, txt_a, txt_y1, txt_y2), "lc", 1)
    img_n = after(img, img_c)
    img_y2 = exchange(img_n, "ly", 2)
    img_y1 = exchange(img_n, "ly", 1)
    img_b = exchange(img_a, "lz", 3)

    count = 2 * QUADS * lax.axis_size("dz") * ways

    def turn(array, axis, step):
        size = lax.axis_size(axis)
        return lax.ppermute(array, axis, [(i, (i + step) % size) for i in range(size)])

    def columns(outs):
        return [outs[0]] + [turn(out, "dx", step) for step, out in enumerate(outs) if step]

    last = after(txt_b, img_feat, img_a, img_c, img_y1, img_y2)
    *img_outs, far_rows = late(
        True, ways, spot, scal, img, img_part, [txt_y1, txt_y2, txt_a, last]
    )
    img_cols = columns(img_outs)
    txt_part = early(
        False,
        scal,
        sentences[0],
        sentence_weights,
        keys,
        [txt, near_rows, far_rows, img, img_c, img_y1, img_y2, img_a],
    )
    last = after(img_b, *img_cols, *txt_part)
    outs = late(False, ways, spot, scal, txt, txt_part, [far_rows, last])
    txt_cols = columns(outs)
    img_kept, img_given = heads(True, spot, after(img_feat, outs[0], txt_feat), img_cols)
    img_taken = exchange(img_given, "lc", 1)
    txt_kept, txt_given = heads(False, spot, txt_feat, txt_cols)
    txt_taken = exchange(txt_given, "lc", 1)
    sums = mix(img_kept, img_taken, txt_kept, txt_taken)
    sums = lax.all_to_all(sums, ("ly", "lz", "dz"), 0, 0, tiled=True)
    grad_img, grad_txt, stats = final(count, sums)
    return grad_img, grad_txt, stats


def solution(mesh):
    split = Mesh(mesh.devices.reshape(4, 4, 2, 2, 4), ("ly", "lz", "lc", "dz", "dx"))
    dp = ("dz", "dx")
    return jax.shard_map(
        body,
        mesh=split,
        in_specs=(P(dp, LOSS, None), P(dp, LOSS, None), P(dp, LOSS), P(), P(), P(), P()),
        out_specs=(P(LOSS, dp), P(LOSS, dp), P()),
        check_vma=False,
    )
```

```python
import functools

import jax
import jax.numpy as jnp
from jax import lax
from jax.experimental import pallas as pl
from jax.experimental.pallas import tpu as pltpu
from jax.sharding import Mesh, PartitionSpec as P

EPSILON = 1e-06
LOSS = ("ly", "lz", "lc")
ROWS = 128
WIDTH = 1152
KEY_ROWS = 16
CHUNK = 36
SLOT = 40
COLS = 144
LANES = 128
TAIL = COLS - LANES
QUADS = 16
STATS = 112
DEPTH = 128
PIECES = WIDTH // DEPTH
SLAB = SLOT + 8
TEXT = ROWS + KEY_ROWS
SPREAD = 2 * COLS + KEY_ROWS
F32 = jnp.float32
BF16 = jnp.bfloat16

VMEM = pl.BlockSpec(memory_space=pltpu.VMEM)
SMEM = pl.BlockSpec(memory_space=pltpu.SMEM)
HBM = pl.BlockSpec(memory_space=pltpu.HBM)


def params(megabytes):
    return pltpu.CompilerParams(vmem_limit_bytes=megabytes * 2**20)


def cost(flops, moved):
    return pl.CostEstimate(flops=flops, bytes_accessed=moved, transcendentals=0)


def exchange(array, axis, apart):
    return lax.ppermute(array, axis, [(i, i ^ apart) for i in range(lax.axis_size(axis))])


def after(array, *others):
    return lax.optimization_barrier((array, *others))[0]


def nt(a, b):
    return lax.dot_general(a, b, (((1,), (1,)), ((), ())), preferred_element_type=F32)


def mm(a, b):
    return jnp.dot(a, b, preferred_element_type=F32)


def project_kernel(xs_hbm, xt_hbm, ws_hbm, wt_hbm, key_hbm, img, txt, both, x, w, key, sems):
    copies = [pltpu.make_async_copy(key_hbm, key, sems.at[0])]
    for t, (x_hbm, w_hbm) in enumerate(((xt_hbm, wt_hbm), (xs_hbm, ws_hbm))):
        base = 1 + t * (1 + PIECES)
        copies.append(pltpu.make_async_copy(x_hbm, x.at[t], sems.at[base]))
        for k in range(PIECES):
            span = pl.ds(k * DEPTH, DEPTH)
            copies.append(
                pltpu.make_async_copy(w_hbm.at[span], w.at[t, span], sems.at[base + 1 + k])
            )
    for copy in copies:
        copy.start()

    def unit(t):
        base = 1 + t * (1 + PIECES)
        copies[base].wait()
        u = jnp.zeros((ROWS, WIDTH), F32)
        for k in range(PIECES):
            copies[base + 1 + k].wait()
            span = slice(k * DEPTH, (k + 1) * DEPTH)
            u += mm(x[t, :, span], w[t, span])
        return (u / lengths(u)).astype(BF16)

    vec = unit(0)
    copies[0].wait()
    digit = jnp.broadcast_to(key[...], (KEY_ROWS, ROWS))
    row = lax.broadcasted_iota(jnp.int32, (KEY_ROWS, ROWS), 0)
    digit = jnp.where(row == 0, digit >> 7, jnp.where(row == 1, digit & 127, 0))
    for out in (txt, both):
        out[:ROWS, :] = vec
        out[ROWS:TEXT, :] = jnp.zeros((KEY_ROWS, WIDTH), BF16)
        out[ROWS:TEXT, :ROWS] = digit.astype(F32).astype(BF16)
    vec = unit(1)
    img[...] = vec
    both[TEXT:, :] = vec


def project(pictures, sentences, picture_weights, sentence_weights, keys):
    return pl.pallas_call(
        project_kernel,
        in_specs=[HBM] * 5,
        out_specs=[VMEM] * 3,
        out_shape=[
            jax.ShapeDtypeStruct((rows, WIDTH), BF16) for rows in (ROWS, TEXT, TEXT + ROWS)
        ],
        scratch_shapes=[
            pltpu.VMEM((2, ROWS, WIDTH), BF16),
            pltpu.VMEM((2, WIDTH, WIDTH), BF16),
            pltpu.VMEM((1, ROWS), jnp.int32),
            pltpu.SemaphoreType.DMA((1 + 2 * (1 + PIECES),)),
        ],
        compiler_params=params(56),
        cost_estimate=cost(4 * ROWS * WIDTH * WIDTH, 8 * 2**20),
    )(pictures, sentences, picture_weights, sentence_weights, keys)


def lengths(u):
    return jnp.sqrt(jnp.sum(u * u, axis=1, keepdims=True) + EPSILON)


def temperature(heat_log):
    return jnp.exp(jnp.full((1, 1), heat_log[0], F32))


def caption_row(block):
    digits = block[ROWS:TEXT, :LANES].astype(F32)
    return digits[0:1] * 128.0 + digits[1:2]


def add_tiles(with_stats, heat, shift, mine, key_col, pairs, total, sums):
    for block, key_row in pairs:
        vec = block[...]
        same = key_col == key_row
        sim = nt(mine, vec)
        logits = heat * sim + shift
        z = jnp.where(same, -logits, logits)
        t = jnp.exp(-jnp.abs(z))
        q = 1.0 / (1.0 + t)
        sig = jnp.where(z >= 0, q, t * q)
        g = jnp.where(same, -sig, sig) * (1.0 / ROWS)
        total += mm(g.astype(BF16), vec)
        if with_stats:
            new = (jnp.maximum(z, 0.0) + jnp.log1p(t), g * sim, g)
            sums = [old + add for old, add in zip(sums, new)]
    return total, sums


def early_kernel(heat_log, shift, xs, xt, ws_hbm, wt_hbm, key, *refs):
    za_txt, za_img, img, txt, core, y1, y2, *refs = refs
    total_img, unit_img, len_img, total_txt, unit_txt, len_txt, key_ref, sum_ref, w, sems = refs
    copies = [
        pltpu.make_async_copy(ws_hbm, w.at[0], sems.at[0]),
        pltpu.make_async_copy(wt_hbm, w.at[1], sems.at[1]),
    ]
    for copy in copies:
        copy.start()
    heat = temperature(heat_log)
    key_col = jnp.broadcast_to(key[...].astype(F32), (ROWS, ROWS)).T
    key_ref[...] = key_col
    rows = [caption_row(block) for block in (txt, core, y1, y2, za_txt)]
    texts = [block.at[:ROWS] for block in (txt, core, y1, y2, za_txt)]
    images = [img] + [block.at[TEXT:] for block in (core, y1, y2)] + [za_img]
    zero = jnp.zeros((ROWS, ROWS), F32)
    none = jnp.zeros((ROWS, WIDTH), F32)
    total, sums = add_tiles(
        True, heat, shift[0], img[...], key_col, zip(texts, rows), none, [zero] * 3
    )
    total_img[...] = total
    for k in range(3):
        sum_ref[k] = sums[k]
    total, _ = add_tiles(
        False, heat, shift[0], txt[:ROWS, :], key_col, zip(images, rows), none, [zero] * 3
    )
    total_txt[...] = total
    for t, (x, unit, length) in enumerate(((xs, unit_img, len_img), (xt, unit_txt, len_txt))):
        copies[t].wait()
        u = mm(x[...], w[t])
        r = lengths(u)
        unit[...] = u / r
        length[...] = jnp.broadcast_to(r, length.shape)


def early(scal, features, weights, keys, *blocks):
    tower = [(ROWS, WIDTH), (ROWS, WIDTH), (ROWS, LANES)]
    shapes = tower + tower + [(ROWS, ROWS), (3, ROWS, ROWS)]
    return pl.pallas_call(
        early_kernel,
        in_specs=[SMEM] * 2 + [VMEM] * 2 + [HBM] * 2 + [VMEM] * (1 + len(blocks)),
        out_specs=[VMEM] * len(shapes),
        out_shape=[jax.ShapeDtypeStruct(shape, F32) for shape in shapes],
        scratch_shapes=[pltpu.VMEM((2, WIDTH, WIDTH), BF16), pltpu.SemaphoreType.DMA((2,))],
        compiler_params=params(56),
        cost_estimate=cost(4 * 10 * ROWS * ROWS * WIDTH, 8 * 2**20),
    )(*scal, *features, *weights, keys, *blocks)


def directions(total, unit, length):
    u = unit[...]
    inner = jnp.sum(u * total, axis=1, keepdims=True)
    return ((total - u * inner) / length[:, :1]).T.astype(BF16)


def late_image_kernel(heat_log, shift, own, total_ref, unit, length, key, acc, block, *outs):
    held, parts_ref, row_ref = outs
    heat = temperature(heat_log)
    key_row = caption_row(block)
    row_ref[...] = jnp.broadcast_to(key_row, (8, LANES))
    total, sums = add_tiles(
        True,
        heat,
        shift[0],
        own[...],
        key[...],
        [(block.at[:ROWS], key_row)],
        total_ref[...],
        [acc[k] for k in range(3)],
    )
    held[...] = directions(total * heat, unit, length).reshape(held.shape)

    def full(x):
        return jnp.sum(jnp.sum(x, axis=1, keepdims=True), axis=0, keepdims=True)

    lane = lax.broadcasted_iota(jnp.int32, (KEY_ROWS, LANES), 1)
    row = lax.broadcasted_iota(jnp.int32, (KEY_ROWS, LANES), 0)
    kind = lane % 3
    value = jnp.where(
        kind == 0,
        full(sums[0]) * (1.0 / ROWS),
        jnp.where(kind == 1, full(sums[1]) * heat, full(sums[2])),
    )
    value = jnp.where((row == 0) & (lane < 9), value, 0.0)
    high = value.astype(BF16).astype(F32)
    middle = (value - high).astype(BF16).astype(F32)
    low = value - high - middle
    parts_ref[...] = jnp.where(lane < 3, high, jnp.where(lane < 6, middle, low)).astype(BF16)


def late_image(ways, scal, *arrays):
    return pl.pallas_call(
        late_image_kernel,
        in_specs=[SMEM] * 2 + [VMEM] * len(arrays),
        out_specs=[VMEM] * 3,
        out_shape=[
            jax.ShapeDtypeStruct((2 * ways, COLS, ROWS), BF16),
            jax.ShapeDtypeStruct((KEY_ROWS, LANES), BF16),
            jax.ShapeDtypeStruct((8, LANES), F32),
        ],
        compiler_params=params(56),
        cost_estimate=cost(4 * ROWS * ROWS * WIDTH, 4 * 2**20),
    )(*scal, *arrays)


def late_text_kernel(ways, spot, heat_log, shift, own, total_ref, unit, length, key, *refs):
    block, row, held_img, parts, *outs, held = refs
    heat = temperature(heat_log)
    pairs = [(block, row[0:1])]
    zero = jnp.zeros((ROWS, ROWS), F32)
    total, _ = add_tiles(
        False, heat, shift[0], own[:ROWS, :], key[...], pairs, total_ref[...], [zero] * 3
    )
    held[...] = directions(total * heat, unit, length).reshape(held.shape)
    for step, out in enumerate(outs):
        w = lax.rem(spot[0] + step, ways)
        for h in range(2):
            out[h * COLS : (h + 1) * COLS, :] = held_img[h * ways + w]
            out[SPREAD + h * COLS : SPREAD + (h + 1) * COLS, :] = held[h * ways + w]
        out[2 * COLS : SPREAD, :] = parts[...]


def late_text(ways, spot, scal, *arrays):
    return pl.pallas_call(
        functools.partial(late_text_kernel, ways),
        in_specs=[SMEM] * 3 + [VMEM] * len(arrays),
        out_specs=[VMEM] * ways,
        out_shape=[jax.ShapeDtypeStruct((SPREAD + 2 * COLS, ROWS), BF16)] * ways,
        scratch_shapes=[pltpu.VMEM((2 * ways, COLS, ROWS), BF16)],
        compiler_params=params(56),
        cost_estimate=cost(4 * ROWS * ROWS * WIDTH, 4 * 2**20),
    )(spot, *scal, *arrays)


def head_kernel(spot, feat_img, feat_txt, *refs):
    spreads, (kept, given, held) = refs[:-3], refs[-3:]
    ways = len(spreads)
    parts = jnp.zeros((KEY_ROWS, LANES), F32)
    for spread in spreads:
        parts += spread[2 * COLS : SPREAD, :].astype(F32)
    lane = lax.broadcasted_iota(jnp.int32, (8, LANES), 1)
    row = lax.broadcasted_iota(jnp.int32, (8, LANES), 0)
    place = lane - STATS
    summed = jnp.zeros((8, LANES), F32)
    for k in range(3):
        number = jnp.sum(
            jnp.where((lane[:1] % 3 == k) & (lane[:1] < 9), parts[0:1], 0.0),
            axis=1,
            keepdims=True,
        )
        summed = jnp.where(place % 3 == k, number, summed)
    value = jnp.where((row == spot[1]) & (place >= 0) & (place < 9), summed, 0.0)
    high = value.astype(BF16).astype(F32)
    middle = (value - high).astype(BF16).astype(F32)
    low = value - high - middle
    spare = jnp.where(place < 3, high, jnp.where(place < 6, middle, low))
    for t, feat in enumerate((feat_img, feat_txt)):
        total = jnp.zeros((2 * COLS, WIDTH), F32)
        for step, spread in enumerate(spreads):
            source = lax.rem(spot[0] + ways - step, ways)
            rows = feat[pl.ds(pl.multiple_of(source * ROWS, ROWS), ROWS), :]
            total += mm(spread[t * SPREAD : t * SPREAD + 2 * COLS, :], rows)
        top = t * SLAB
        for h in range(2):
            main = total[h * COLS : h * COLS + LANES, :].T
            rest = total[h * COLS + LANES : (h + 1) * COLS, :]
            for m in range(QUADS):
                for side in range(2):
                    start = (2 * m + side) * CHUNK
                    target = held.at[side, 2 * m + h]
                    target[top : top + CHUNK, :] = main[start : start + CHUNK]
                    target[top + CHUNK : top + SLOT, :] = jnp.zeros((SLOT - CHUNK, LANES), F32)
                    target[top + SLOT : top + SLAB, :] = spare * (1 - t)
                    for k in range(2):
                        target[top + SLOT : top + SLAB, 64 * k : 64 * k + CHUNK] = rest[
                            8 * k : 8 * k + 8, start : start + CHUNK
                        ]
    kept[...] = held[spot[1]]
    given[...] = held[1 - spot[1]].astype(BF16)


def heads(spot, feat_img, feat_txt, spreads):
    shape = (2 * QUADS, 2 * SLAB, LANES)
    return pl.pallas_call(
        head_kernel,
        in_specs=[SMEM] + [VMEM] * (2 + len(spreads)),
        out_specs=[VMEM, VMEM],
        out_shape=[jax.ShapeDtypeStruct(shape, F32), jax.ShapeDtypeStruct(shape, BF16)],
        scratch_shapes=[pltpu.VMEM((2, *shape), F32)],
        compiler_params=params(24),
        cost_estimate=cost(16 * ROWS * 2 * COLS * WIDTH, 4 * 2**20),
    )(spot, feat_img, feat_txt, *spreads)


def final_kernel(count, parts, out_img, out_txt, stats):
    both = jnp.sum(parts[...].astype(F32), axis=0)
    for out, total in ((out_img, both[:SLAB]), (out_txt, both[SLAB:])):
        out[:, :LANES] = total[:CHUNK]
        rest = total[SLOT:, :].T
        out[:, LANES : LANES + 8] = rest[:CHUNK]
        out[:, LANES + 8 :] = rest[64 : 64 + CHUNK]
    place = lax.broadcasted_iota(jnp.int32, (1, LANES), 1) - STATS
    row = both[SLOT : SLOT + 1] + both[SLOT + 1 : SLOT + 2]
    for k in range(3):
        chosen = jnp.where((place % 3 == k) & (place >= 0) & (place < 9), row, 0.0)
        stats[k] = jnp.sum(chosen) * (1.0 / count)


def final(count, parts):
    grad = jax.ShapeDtypeStruct((CHUNK, COLS), F32)
    return pl.pallas_call(
        functools.partial(final_kernel, count),
        in_specs=[VMEM],
        out_specs=[VMEM, VMEM, SMEM],
        out_shape=[grad, grad, jax.ShapeDtypeStruct((3,), F32)],
        compiler_params=params(8),
        cost_estimate=cost(4 * QUADS * SLAB * LANES, 2**20),
    )(parts)


def body(pictures, sentences, keys, picture_weights, sentence_weights, heat_log, shift_value):
    ways = lax.axis_size("dx")
    spot = jnp.stack([lax.axis_index(axis) for axis in ("dx", "lc")]).astype(jnp.int32)
    scal = (heat_log, shift_value)
    features = (pictures[0], sentences[0])
    weights = (picture_weights, sentence_weights)
    img, txt, both = project(*features, *weights, keys)
    za_txt = exchange(txt, "lz", 1)
    za_img = exchange(img, "lz", 1)
    y1 = exchange(both, "ly", 1)
    y2 = exchange(both, "ly", 2)
    core = exchange(both, "lc", 1)
    zb_txt = exchange(za_txt, "lz", 3)
    zb_img = exchange(za_img, "lz", 3)
    img_feat = lax.all_gather(after(pictures[0], img), "dx", axis=0, tiled=True)
    txt_feat = lax.all_gather(after(sentences[0], img), "dx", axis=0, tiled=True)

    def turn(array, step):
        return lax.ppermute(array, "dx", [(i, (i + step) % ways) for i in range(ways)])

    first = early(scal, features, weights, keys, za_txt, za_img, img, txt, core, y1, y2)
    key_col, acc = first[6:]
    held, parts, row = late_image(ways, scal, img, *first[:3], key_col, acc, zb_txt)
    outs = late_text(
        ways, spot, scal, txt, *first[3:6], key_col, after(zb_img, held), row, held, parts
    )
    cols = [outs[0]] + [turn(out, step) for step, out in enumerate(outs) if step]
    kept, given = heads(spot, after(img_feat, txt_feat), txt_feat, cols)
    taken = exchange(given, "lc", 1)
    sums = (kept + taken.astype(F32)).astype(BF16)
    sums = lax.all_to_all(sums, ("ly", "lz", "dz"), 0, 0, tiled=True)
    grad_img, grad_txt, stats = final(2 * QUADS * lax.axis_size("dz") * ways, sums)
    return grad_img, grad_txt, stats


def solution(mesh):
    split = Mesh(mesh.devices.reshape(4, 4, 2, 2, 4), ("ly", "lz", "lc", "dz", "dx"))
    dp = ("dz", "dx")
    return jax.shard_map(
        body,
        mesh=split,
        in_specs=(P(dp, LOSS, None), P(dp, LOSS, None), P(dp, LOSS), P(), P(), P(), P()),
        out_specs=(P(LOSS, dp), P(LOSS, dp), P()),
        check_vma=False,
    )
```

```python
import functools

import jax
import jax.numpy as jnp
from jax import lax
from jax.experimental import pallas as pl
from jax.experimental.pallas import tpu as pltpu
from jax.sharding import Mesh, PartitionSpec as P

EPSILON = 1e-06
LOSS = ("ly", "lz", "lc")
QUAD = ("ly", "lz", "dz")
ROWS = 128
WIDTH = 1152
KEY_ROWS = 16
CHUNK = 36
SLOT = 40
COLS = 144
LANES = 128
TAIL = COLS - LANES
QUADS = 16
STATS = 112
DEPTH = 128
PIECES = WIDTH // DEPTH
SLAB = SLOT + 8
F32 = jnp.float32
BF16 = jnp.bfloat16

VMEM = pl.BlockSpec(memory_space=pltpu.VMEM)
SMEM = pl.BlockSpec(memory_space=pltpu.SMEM)


def params(megabytes):
    return pltpu.CompilerParams(vmem_limit_bytes=megabytes * 2**20)


def cost(flops, moved):
    return pl.CostEstimate(flops=flops, bytes_accessed=moved, transcendentals=0)


def exchange(array, axis, apart):
    return lax.ppermute(array, axis, [(i, i ^ apart) for i in range(lax.axis_size(axis))])


def after(array, *others):
    return lax.optimization_barrier((array, *others))[0]


def nt(a, b):
    return lax.dot_general(a, b, (((1,), (1,)), ((), ())), preferred_element_type=F32)


def mm(a, b):
    return jnp.dot(a, b, preferred_element_type=F32)


def project_kernel(x_hbm, w_hbm, key_hbm, out_ref, x, w, key, sems):
    copies = [
        pltpu.make_async_copy(x_hbm, x, sems.at[0]),
        pltpu.make_async_copy(key_hbm, key, sems.at[1]),
    ]
    for k in range(PIECES):
        span = pl.ds(k * DEPTH, DEPTH)
        copies.append(pltpu.make_async_copy(w_hbm.at[span], w.at[span], sems.at[2 + k]))
    for copy in copies:
        copy.start()
    copies[0].wait()
    u = jnp.zeros((ROWS, WIDTH), F32)
    for k in range(PIECES):
        copies[2 + k].wait()
        span = slice(k * DEPTH, (k + 1) * DEPTH)
        u += mm(x[:, span], w[span])
    copies[1].wait()
    write_payload(out_ref, u / lengths(u), key[...])


def lengths(u):
    return jnp.sqrt(jnp.sum(u * u, axis=1, keepdims=True) + EPSILON)


def project(x, w, keys):
    return pl.pallas_call(
        project_kernel,
        in_specs=[pl.BlockSpec(memory_space=pltpu.HBM)] * 3,
        out_specs=VMEM,
        out_shape=jax.ShapeDtypeStruct((ROWS + KEY_ROWS, WIDTH), BF16),
        scratch_shapes=[
            pltpu.VMEM((ROWS, WIDTH), BF16),
            pltpu.VMEM((WIDTH, WIDTH), BF16),
            pltpu.VMEM((1, ROWS), jnp.int32),
            pltpu.SemaphoreType.DMA((2 + PIECES,)),
        ],
        compiler_params=params(56),
        cost_estimate=cost(2 * ROWS * WIDTH * WIDTH, 4 * 2**20),
    )(x, w, keys)


def temperature(heat_log):
    return jnp.exp(jnp.full((1, 1), heat_log[0], F32))


def caption_row(block):
    digits = block[ROWS:, :LANES].astype(F32)
    return digits[0:1] * 128.0 + digits[1:2]


def add_tiles(with_stats, heat, shift, mine, key_col, pairs, total, sums):
    for block, key_row in pairs:
        vec = block[:ROWS, :]
        same = key_col == key_row
        sim = nt(mine, vec)
        logits = heat * sim + shift
        z = jnp.where(same, -logits, logits)
        t = jnp.exp(-jnp.abs(z))
        q = 1.0 / (1.0 + t)
        sig = jnp.where(z >= 0, q, t * q)
        g = jnp.where(same, -sig, sig) * (1.0 / ROWS)
        total += mm(g.astype(BF16), vec)
        if with_stats:
            new = (jnp.maximum(z, 0.0) + jnp.log1p(t), g * sim, g)
            sums = [old + add for old, add in zip(sums, new)]
    return total, sums


def pair_up(blocks, rows_ref):
    pairs = []
    for k, block in enumerate(blocks):
        key_row = caption_row(block)
        rows_ref[k] = jnp.broadcast_to(key_row, (8, LANES))
        pairs.append((block, key_row))
    return pairs


def write_payload(out_ref, unit, key):
    digit = jnp.broadcast_to(key, (KEY_ROWS, ROWS))
    row = lax.broadcasted_iota(jnp.int32, (KEY_ROWS, ROWS), 0)
    digit = jnp.where(row == 0, digit >> 7, jnp.where(row == 1, digit & 127, 0))
    out_ref[:ROWS, :] = unit.astype(BF16)
    out_ref[ROWS:, :] = jnp.zeros((KEY_ROWS, WIDTH), BF16)
    out_ref[ROWS:, :ROWS] = digit.astype(F32).astype(BF16)


def early_kernel(first, heat_log, shift, x, w_hbm, key, *refs):
    refs, (total_ref, unit_ref, len_ref, key_ref, sum_ref, w, sem) = refs[:-7], refs[-7:]
    copy = pltpu.make_async_copy(w_hbm, w, sem)
    copy.start()
    key_col = jnp.broadcast_to(key[...].astype(F32), (ROWS, ROWS)).T
    key_ref[...] = key_col

    def norm():
        copy.wait()
        u = mm(x[...], w[...])
        length = lengths(u)
        unit_ref[...] = u / length
        len_ref[...] = jnp.broadcast_to(length, len_ref.shape)

    if first:
        blocks, (own, rows_ref) = refs[:-2], refs[-2:]
        norm()
        own[...] = unit_ref[...].astype(BF16)
        pairs = pair_up(blocks, rows_ref)
    else:
        own, near_rows, far_rows, *blocks = refs
        rows = [near_rows[0], near_rows[1], far_rows[0], far_rows[1], far_rows[2]]
        pairs = [(block, row[0:1]) for block, row in zip(blocks, rows)]
    zero = jnp.zeros((ROWS, ROWS), F32)
    total, sums = add_tiles(
        first,
        temperature(heat_log),
        shift[0],
        own[:ROWS, :],
        key_col,
        pairs,
        jnp.zeros((ROWS, WIDTH), F32),
        [zero] * 3,
    )
    total_ref[...] = total
    for k in range(3):
        sum_ref[k] = sums[k]
    if not first:
        norm()


def early(first, scal, x, w, keys, blocks):
    shapes = [(ROWS, WIDTH), (ROWS, WIDTH), (ROWS, LANES), (ROWS, ROWS), (3, ROWS, ROWS)]
    outs = [jax.ShapeDtypeStruct(shape, F32) for shape in shapes]
    if first:
        outs = [
            jax.ShapeDtypeStruct((ROWS, WIDTH), BF16),
            jax.ShapeDtypeStruct((len(blocks), 8, LANES), F32),
        ] + outs
    hbm = pl.BlockSpec(memory_space=pltpu.HBM)
    return pl.pallas_call(
        functools.partial(early_kernel, first),
        in_specs=[SMEM, SMEM, VMEM, hbm, VMEM] + [VMEM] * len(blocks),
        out_specs=[VMEM] * len(outs),
        out_shape=outs,
        scratch_shapes=[pltpu.VMEM((WIDTH, WIDTH), BF16), pltpu.SemaphoreType.DMA],
        compiler_params=params(56),
        cost_estimate=cost(4 * 5 * ROWS * ROWS * WIDTH, 8 * 2**20),
    )(*scal, x, w, keys, *blocks)


def late_kernel(with_stats, ways, count, spot, heat_log, shift, own, *refs):
    total_ref, unit, length, key, acc, *refs = refs
    blocks, outs, held = refs[:count], refs[count:-1], refs[-1]
    heat = temperature(heat_log)
    if with_stats:
        *outs, rows_ref = outs
        pairs = pair_up(blocks, rows_ref)
    else:
        rows, block = blocks
        pairs = [(block, rows[3][0:1])]
    total, sums = add_tiles(
        with_stats,
        heat,
        shift[0],
        own[:ROWS, :],
        key[...],
        pairs,
        total_ref[...],
        [acc[k] for k in range(3)],
    )
    total = total * heat
    u = unit[...]
    inner = jnp.sum(u * total, axis=1, keepdims=True)
    du = (total - u * inner) / length[:, :1]
    held[...] = du.T.astype(BF16).reshape(held.shape)
    if with_stats:
        def full(x):
            return jnp.sum(jnp.sum(x, axis=1, keepdims=True), axis=0, keepdims=True)

        lane = lax.broadcasted_iota(jnp.int32, (KEY_ROWS, LANES), 1)
        row = lax.broadcasted_iota(jnp.int32, (KEY_ROWS, LANES), 0)
        kind = lane % 3
        value = jnp.where(
            kind == 0,
            full(sums[0]) * (1.0 / ROWS),
            jnp.where(kind == 1, full(sums[1]) * heat, full(sums[2])),
        )
        value = jnp.where((row == 0) & (lane < 9), value, 0.0)
        high = value.astype(BF16).astype(F32)
        middle = (value - high).astype(BF16).astype(F32)
        low = value - high - middle
        parts = jnp.where(lane < 3, high, jnp.where(lane < 6, middle, low)).astype(BF16)
        for out in outs:
            out[2 * COLS :, :] = parts
    for step, out in enumerate(outs):
        w = lax.rem(spot[0] + step, ways)
        for h in range(2):
            out[h * COLS : (h + 1) * COLS, :] = held[h * ways + w]


def late(with_stats, ways, spot, scal, own, partial, blocks):
    rows = 2 * COLS + (KEY_ROWS if with_stats else 0)
    shapes = [jax.ShapeDtypeStruct((rows, ROWS), BF16)] * ways
    if with_stats:
        shapes.append(jax.ShapeDtypeStruct((len(blocks), 8, LANES), F32))
    return pl.pallas_call(
        functools.partial(late_kernel, with_stats, ways, len(blocks)),
        in_specs=[SMEM] * 3 + [VMEM] * (6 + len(blocks)),
        out_specs=[VMEM] * len(shapes),
        out_shape=shapes,
        scratch_shapes=[pltpu.VMEM((2 * ways, COLS, ROWS), BF16)],
        compiler_params=params(56),
        cost_estimate=cost(4 * 2 * ROWS * ROWS * WIDTH, 4 * 2**20),
    )(spot, *scal, own, *partial, *blocks)


def head_kernel(with_stats, spot, feat, *refs):
    spreads, (kept, given, held) = refs[:-3], refs[-3:]
    ways = len(spreads)
    total = jnp.zeros((2 * COLS, feat.shape[1]), F32)
    for step, spread in enumerate(spreads):
        source = lax.rem(spot[0] + ways - step, ways)
        rows = feat[pl.ds(pl.multiple_of(source * ROWS, ROWS), ROWS), :]
        total += mm(spread[: 2 * COLS, :], rows)
    spare = None
    if with_stats:
        parts = jnp.zeros((KEY_ROWS, LANES), F32)
        for spread in spreads:
            parts += spread[2 * COLS :, :].astype(F32)
        lane = lax.broadcasted_iota(jnp.int32, (8, LANES), 1)
        row = lax.broadcasted_iota(jnp.int32, (8, LANES), 0)
        place = lane - STATS
        summed = jnp.zeros((8, LANES), F32)
        for k in range(3):
            number = jnp.sum(
                jnp.where((lane[:1] % 3 == k) & (lane[:1] < 9), parts[0:1], 0.0),
                axis=1,
                keepdims=True,
            )
            summed = jnp.where(place % 3 == k, number, summed)
        value = jnp.where((row == spot[1]) & (place >= 0) & (place < 9), summed, 0.0)
        high = value.astype(BF16).astype(F32)
        middle = (value - high).astype(BF16).astype(F32)
        low = value - high - middle
        spare = jnp.where(place < 3, high, jnp.where(place < 6, middle, low))
    for h in range(2):
        main = total[h * COLS : h * COLS + LANES, :].T
        rest = total[h * COLS + LANES : (h + 1) * COLS, :]
        for m in range(QUADS):
            for side in range(2):
                start = (2 * m + side) * CHUNK
                target = held.at[side, 2 * m + h]
                target[:CHUNK, :] = main[start : start + CHUNK]
                target[CHUNK:SLOT, :] = jnp.zeros((SLOT - CHUNK, LANES), F32)
                target[SLOT:, :] = jnp.zeros((8, LANES), F32) if spare is None else spare
                for k in range(2):
                    target[SLOT:, 64 * k : 64 * k + CHUNK] = rest[
                        8 * k : 8 * k + 8, start : start + CHUNK
                    ]
    kept[...] = held[spot[1]]
    given[...] = held[1 - spot[1]].astype(BF16)


def heads(with_stats, spot, feat, spreads):
    shape = (2 * QUADS, SLOT + 8, LANES)
    return pl.pallas_call(
        functools.partial(head_kernel, with_stats),
        in_specs=[SMEM] + [VMEM] * (1 + len(spreads)),
        out_specs=[VMEM, VMEM],
        out_shape=[jax.ShapeDtypeStruct(shape, F32), jax.ShapeDtypeStruct(shape, BF16)],
        scratch_shapes=[pltpu.VMEM((2, *shape), F32)],
        compiler_params=params(24),
        cost_estimate=cost(2 * 4 * ROWS * 2 * COLS * feat.shape[1], 4 * 2**20),
    )(spot, feat, *spreads)


def mix_kernel(kept_img, taken_img, kept_txt, taken_txt, out):
    out[:, :SLAB, :] = (kept_img[...] + taken_img[...].astype(F32)).astype(BF16)
    out[:, SLAB:, :] = (kept_txt[...] + taken_txt[...].astype(F32)).astype(BF16)


def mix(*arrays):
    return pl.pallas_call(
        mix_kernel,
        in_specs=[VMEM] * 4,
        out_specs=VMEM,
        out_shape=jax.ShapeDtypeStruct((2 * QUADS, 2 * SLAB, LANES), BF16),
        compiler_params=params(16),
        cost_estimate=cost(4 * QUADS * SLAB * LANES, 2**20),
    )(*arrays)


def final_kernel(count, slot, parts, own_img, own_txt, out_img, out_txt, stats):
    both = jnp.sum(parts[...].astype(F32), axis=0) - parts[slot[0]].astype(F32)
    both = both + jnp.concatenate([own_img[...], own_txt[...]], axis=0)
    for out, total in ((out_img, both[:SLAB]), (out_txt, both[SLAB:])):
        out[:, :LANES] = total[:CHUNK]
        rest = total[SLOT:, :].T
        out[:, LANES : LANES + 8] = rest[:CHUNK]
        out[:, LANES + 8 :] = rest[64 : 64 + CHUNK]
    place = lax.broadcasted_iota(jnp.int32, (1, LANES), 1) - STATS
    row = both[SLOT : SLOT + 1] + both[SLOT + 1 : SLOT + 2]
    for k in range(3):
        chosen = jnp.where((place % 3 == k) & (place >= 0) & (place < 9), row, 0.0)
        stats[k] = jnp.sum(chosen) * (1.0 / count)


def final(count, slot, *arrays):
    grad = jax.ShapeDtypeStruct((CHUNK, COLS), F32)
    return pl.pallas_call(
        functools.partial(final_kernel, count),
        in_specs=[SMEM] + [VMEM] * len(arrays),
        out_specs=[VMEM, VMEM, SMEM],
        out_shape=[grad, grad, jax.ShapeDtypeStruct((3,), F32)],
        compiler_params=params(8),
        cost_estimate=cost(4 * QUADS * SLAB * LANES, 2**20),
    )(slot, *arrays)


def body(pictures, sentences, keys, picture_weights, sentence_weights, heat_log, shift_value):
    ways = lax.axis_size("dx")
    spot = jnp.stack([lax.axis_index(axis) for axis in ("dx", "lc")]).astype(jnp.int32)
    scal = (heat_log, shift_value)
    txt = project(sentences[0], sentence_weights, keys)
    txt_a = exchange(txt, "lz", 1)
    txt_y2 = exchange(txt, "ly", 2)
    txt_y1 = exchange(txt, "ly", 1)
    txt_c = exchange(txt, "lc", 1)
    img_feat = lax.all_gather(after(pictures[0], txt), "dx", axis=0, tiled=True)
    txt_feat = lax.all_gather(after(sentences[0], txt), "dx", axis=0, tiled=True)

    img, near_rows, *img_part = early(True, scal, pictures[0], picture_weights, keys, [txt, txt_c])
    txt_b = exchange(after(txt_a, txt_y1, txt_y2), "lz", 3)
    img_a = exchange(img, "lz", 1)
    img_c = exchange(after(img, txt_a, txt_y1, txt_y2), "lc", 1)
    img_n = after(img, img_c)
    img_y2 = exchange(img_n, "ly", 2)
    img_y1 = exchange(img_n, "ly", 1)
    img_b = exchange(img_a, "lz", 3)

    count = 2 * QUADS * lax.axis_size("dz") * ways

    def turn(array, axis, step):
        size = lax.axis_size(axis)
        return lax.ppermute(array, axis, [(i, (i + step) % size) for i in range(size)])

    def columns(outs):
        return [outs[0]] + [turn(out, "dx", step) for step, out in enumerate(outs) if step]

    last = after(txt_b, img_feat, img_a, img_c, img_y1, img_y2)
    *img_outs, far_rows = late(
        True, ways, spot, scal, img, img_part, [txt_a, txt_y1, txt_y2, last]
    )
    img_cols = columns(img_outs)
    txt_part = early(
        False,
        scal,
        sentences[0],
        sentence_weights,
        keys,
        [txt, near_rows, far_rows, img, img_c, img_a, img_y1, img_y2],
    )
    last = after(img_b, *img_cols, *txt_part)
    outs = late(False, ways, spot, scal, txt, txt_part, [far_rows, last])
    txt_cols = columns(outs)
    img_kept, img_given = heads(True, spot, after(img_feat, outs[0], txt_feat), img_cols)
    img_taken = exchange(img_given, "lc", 1)
    txt_kept, txt_given = heads(False, spot, txt_feat, txt_cols)
    txt_taken = exchange(txt_given, "lc", 1)
    sums = mix(img_kept, img_taken, txt_kept, txt_taken)
    sums = lax.all_to_all(sums, QUAD, 0, 0, tiled=True)
    slot = lax.axis_index(QUAD)

    def own_part(kept, taken):
        return kept[slot] + taken[slot].astype(F32)

    mine = (own_part(img_kept, img_taken), own_part(txt_kept, txt_taken))
    grad_img, grad_txt, stats = final(count, slot.astype(jnp.int32)[None], sums, *mine)
    return grad_img, grad_txt, stats


def solution(mesh):
    split = Mesh(mesh.devices.reshape(4, 4, 2, 2, 4), ("ly", "lz", "lc", "dz", "dx"))
    dp = ("dz", "dx")
    return jax.shard_map(
        body,
        mesh=split,
        in_specs=(P(dp, LOSS, None), P(dp, LOSS, None), P(dp, LOSS), P(), P(), P(), P()),
        out_specs=(P(LOSS, dp), P(LOSS, dp), P()),
        check_vma=False,
    )
```

```python
import functools

import jax
import jax.numpy as jnp
from jax import lax
from jax.experimental import pallas as pl
from jax.experimental.pallas import tpu as pltpu
from jax.sharding import Mesh, PartitionSpec as P

EPSILON = 1e-06
LOSS = ("ly", "lz", "lc")
ROWS = 128
WIDTH = 1152
KEY_ROWS = 16
CHUNK = 36
SLOT = 40
COLS = 144
LANES = 128
TAIL = COLS - LANES
QUADS = 16
STATS = 112
DEPTH = 128
PIECES = WIDTH // DEPTH
SLAB = SLOT + 8
F32 = jnp.float32
BF16 = jnp.bfloat16

VMEM = pl.BlockSpec(memory_space=pltpu.VMEM)
SMEM = pl.BlockSpec(memory_space=pltpu.SMEM)


def params(megabytes):
    return pltpu.CompilerParams(vmem_limit_bytes=megabytes * 2**20)


def cost(flops, moved):
    return pl.CostEstimate(flops=flops, bytes_accessed=moved, transcendentals=0)


def exchange(array, axis, apart):
    return lax.ppermute(array, axis, [(i, i ^ apart) for i in range(lax.axis_size(axis))])


def after(array, *others):
    return lax.optimization_barrier((array, *others))[0]


def nt(a, b):
    return lax.dot_general(a, b, (((1,), (1,)), ((), ())), preferred_element_type=F32)


def mm(a, b):
    return jnp.dot(a, b, preferred_element_type=F32)


def project_kernel(x_hbm, w_hbm, key_hbm, out_ref, x, w, key, sems):
    copies = [
        pltpu.make_async_copy(x_hbm, x, sems.at[0]),
        pltpu.make_async_copy(key_hbm, key, sems.at[1]),
    ]
    for k in range(PIECES):
        span = pl.ds(k * DEPTH, DEPTH)
        copies.append(pltpu.make_async_copy(w_hbm.at[span], w.at[span], sems.at[2 + k]))
    for copy in copies:
        copy.start()
    copies[0].wait()
    u = jnp.zeros((ROWS, WIDTH), F32)
    for k in range(PIECES):
        copies[2 + k].wait()
        span = slice(k * DEPTH, (k + 1) * DEPTH)
        u += mm(x[:, span], w[span])
    copies[1].wait()
    write_payload(out_ref, u / lengths(u), key[...])


def lengths(u):
    return jnp.sqrt(jnp.sum(u * u, axis=1, keepdims=True) + EPSILON)


def project(x, w, keys):
    return pl.pallas_call(
        project_kernel,
        in_specs=[pl.BlockSpec(memory_space=pltpu.HBM)] * 3,
        out_specs=VMEM,
        out_shape=jax.ShapeDtypeStruct((ROWS + KEY_ROWS, WIDTH), BF16),
        scratch_shapes=[
            pltpu.VMEM((ROWS, WIDTH), BF16),
            pltpu.VMEM((WIDTH, WIDTH), BF16),
            pltpu.VMEM((1, ROWS), jnp.int32),
            pltpu.SemaphoreType.DMA((2 + PIECES,)),
        ],
        compiler_params=params(56),
        cost_estimate=cost(2 * ROWS * WIDTH * WIDTH, 4 * 2**20),
    )(x, w, keys)


def temperature(heat_log):
    return jnp.exp(jnp.full((1, 1), heat_log[0], F32))


def caption_row(block):
    digits = block[ROWS:, :LANES].astype(F32)
    return digits[0:1] * 128.0 + digits[1:2]


def add_tiles(with_stats, heat, shift, mine, key_col, pairs, total, sums):
    for block, key_row in pairs:
        vec = block[:ROWS, :]
        same = key_col == key_row
        sim = nt(mine, vec)
        logits = heat * sim + shift
        z = jnp.where(same, -logits, logits)
        t = jnp.exp(-jnp.abs(z))
        q = 1.0 / (1.0 + t)
        sig = jnp.where(z >= 0, q, t * q)
        g = jnp.where(same, -sig, sig) * (1.0 / ROWS)
        total += mm(g.astype(BF16), vec)
        if with_stats:
            new = (jnp.maximum(z, 0.0) + jnp.log1p(t), g * sim, g)
            sums = [old + add for old, add in zip(sums, new)]
    return total, sums


def pair_up(blocks, rows_ref):
    pairs = []
    for k, block in enumerate(blocks):
        key_row = caption_row(block)
        rows_ref[k] = jnp.broadcast_to(key_row, (8, LANES))
        pairs.append((block, key_row))
    return pairs


def write_payload(out_ref, unit, key):
    digit = jnp.broadcast_to(key, (KEY_ROWS, ROWS))
    row = lax.broadcasted_iota(jnp.int32, (KEY_ROWS, ROWS), 0)
    digit = jnp.where(row == 0, digit >> 7, jnp.where(row == 1, digit & 127, 0))
    out_ref[:ROWS, :] = unit.astype(BF16)
    out_ref[ROWS:, :] = jnp.zeros((KEY_ROWS, WIDTH), BF16)
    out_ref[ROWS:, :ROWS] = digit.astype(F32).astype(BF16)


def early_kernel(spot, heat_log, shift, xs, xt, ws_hbm, wt_hbm, key, *refs):
    *blocks, own, rows_ref, total_ref, unit_img, len_img, unit_txt, len_txt = refs[:-4]
    key_ref, sum_ref, w, sems = refs[-4:]
    copies = [
        pltpu.make_async_copy(ws_hbm, w.at[0], sems.at[0]),
        pltpu.make_async_copy(wt_hbm, w.at[1], sems.at[1]),
    ]
    for copy in copies:
        copy.start()
    key_col = jnp.broadcast_to(key[...].astype(F32), (ROWS, ROWS)).T
    key_ref[...] = key_col
    towers = ((xs, unit_img, len_img), (xt, unit_txt, len_txt))

    def norm(t):
        x, unit_ref, len_ref = towers[t]
        copies[t].wait()
        u = mm(x[...], w[t])
        length = lengths(u)
        unit_ref[...] = u / length
        len_ref[...] = jnp.broadcast_to(length, len_ref.shape)

    norm(0)
    own[...] = unit_img[...].astype(BF16)
    zero = jnp.zeros((ROWS, ROWS), F32)
    total, sums = add_tiles(
        True,
        temperature(heat_log),
        shift[0],
        own[...],
        key_col,
        pair_up(blocks, rows_ref),
        jnp.zeros((ROWS, WIDTH), F32),
        [zero] * 3,
    )
    total_ref[...] = total
    for k in range(3):
        sum_ref[k] = sums[k]
    norm(1)


def early(spot, scal, features, weights, keys, blocks):
    shapes = [(ROWS, WIDTH), (ROWS, LANES)]
    shapes = [(ROWS, WIDTH), *shapes, *shapes, (ROWS, ROWS), (3, ROWS, ROWS)]
    outs = [
        jax.ShapeDtypeStruct((ROWS, WIDTH), BF16),
        jax.ShapeDtypeStruct((len(blocks), 8, LANES), F32),
    ] + [jax.ShapeDtypeStruct(shape, F32) for shape in shapes]
    hbm = pl.BlockSpec(memory_space=pltpu.HBM)
    return pl.pallas_call(
        early_kernel,
        in_specs=[SMEM] * 3 + [VMEM] * 2 + [hbm] * 2 + [VMEM] * (1 + len(blocks)),
        out_specs=[VMEM] * len(outs),
        out_shape=outs,
        scratch_shapes=[pltpu.VMEM((2, WIDTH, WIDTH), BF16), pltpu.SemaphoreType.DMA((2,))],
        compiler_params=params(56),
        cost_estimate=cost(4 * 5 * ROWS * ROWS * WIDTH, 8 * 2**20),
    )(spot, *scal, *features, *weights, keys, *blocks)


def middle_kernel(heat_log, shift, own, key, near_rows, far_rows, *refs):
    *blocks, total_ref = refs
    rows = [near_rows[0], near_rows[1], far_rows[0], far_rows[1], far_rows[2]]
    zero = jnp.zeros((ROWS, ROWS), F32)
    total, _ = add_tiles(
        False,
        temperature(heat_log),
        shift[0],
        own[:ROWS, :],
        key[...],
        [(block, row[0:1]) for block, row in zip(blocks, rows)],
        jnp.zeros((ROWS, WIDTH), F32),
        [zero] * 3,
    )
    total_ref[...] = total


def middle(scal, *arrays):
    return pl.pallas_call(
        middle_kernel,
        in_specs=[SMEM] * 2 + [VMEM] * len(arrays),
        out_specs=VMEM,
        out_shape=jax.ShapeDtypeStruct((ROWS, WIDTH), F32),
        compiler_params=params(56),
        cost_estimate=cost(4 * 5 * ROWS * ROWS * WIDTH, 4 * 2**20),
    )(*scal, *arrays)


def late_kernel(with_stats, ways, count, spot, heat_log, shift, own, *refs):
    total_ref, unit, length, key, acc, *refs = refs
    blocks, outs, held = refs[:count], refs[count:-1], refs[-1]
    heat = temperature(heat_log)
    if with_stats:
        *outs, rows_ref = outs
        pairs = pair_up(blocks, rows_ref)
    else:
        rows, block = blocks
        pairs = [(block, rows[3][0:1])]
    total, sums = add_tiles(
        with_stats,
        heat,
        shift[0],
        own[:ROWS, :],
        key[...],
        pairs,
        total_ref[...],
        [acc[k] for k in range(3)] if with_stats else [acc[...]] * 3,
    )
    total = total * heat
    u = unit[...]
    inner = jnp.sum(u * total, axis=1, keepdims=True)
    du = (total - u * inner) / length[:, :1]
    held[...] = du.T.astype(BF16).reshape(held.shape)
    if with_stats:
        def full(x):
            return jnp.sum(jnp.sum(x, axis=1, keepdims=True), axis=0, keepdims=True)

        lane = lax.broadcasted_iota(jnp.int32, (KEY_ROWS, LANES), 1)
        row = lax.broadcasted_iota(jnp.int32, (KEY_ROWS, LANES), 0)
        kind = lane % 3
        value = jnp.where(
            kind == 0,
            full(sums[0]) * (1.0 / ROWS),
            jnp.where(kind == 1, full(sums[1]) * heat, full(sums[2])),
        )
        value = jnp.where((row == 0) & (lane < 9), value, 0.0)
        high = value.astype(BF16).astype(F32)
        middle = (value - high).astype(BF16).astype(F32)
        low = value - high - middle
        parts = jnp.where(lane < 3, high, jnp.where(lane < 6, middle, low)).astype(BF16)
        for out in outs:
            out[2 * COLS :, :] = parts
    for step, out in enumerate(outs):
        w = lax.rem(spot[0] + step, ways)
        for h in range(2):
            out[h * COLS : (h + 1) * COLS, :] = held[h * ways + w]


def late(with_stats, ways, spot, scal, own, partial, blocks):
    rows = 2 * COLS + (KEY_ROWS if with_stats else 0)
    shapes = [jax.ShapeDtypeStruct((rows, ROWS), BF16)] * ways
    if with_stats:
        shapes.append(jax.ShapeDtypeStruct((len(blocks), 8, LANES), F32))
    return pl.pallas_call(
        functools.partial(late_kernel, with_stats, ways, len(blocks)),
        in_specs=[SMEM] * 3 + [VMEM] * (6 + len(blocks)),
        out_specs=[VMEM] * len(shapes),
        out_shape=shapes,
        scratch_shapes=[pltpu.VMEM((2 * ways, COLS, ROWS), BF16)],
        compiler_params=params(56),
        cost_estimate=cost(4 * 2 * ROWS * ROWS * WIDTH, 4 * 2**20),
    )(spot, *scal, own, *partial, *blocks)


def head_kernel(with_stats, spot, feat, *refs):
    spreads, (kept, given, held) = refs[:-3], refs[-3:]
    ways = len(spreads)
    total = jnp.zeros((2 * COLS, feat.shape[1]), F32)
    for step, spread in enumerate(spreads):
        source = lax.rem(spot[0] + ways - step, ways)
        rows = feat[pl.ds(pl.multiple_of(source * ROWS, ROWS), ROWS), :]
        total += mm(spread[: 2 * COLS, :], rows)
    spare = None
    if with_stats:
        parts = jnp.zeros((KEY_ROWS, LANES), F32)
        for spread in spreads:
            parts += spread[2 * COLS :, :].astype(F32)
        lane = lax.broadcasted_iota(jnp.int32, (8, LANES), 1)
        row = lax.broadcasted_iota(jnp.int32, (8, LANES), 0)
        place = lane - STATS
        summed = jnp.zeros((8, LANES), F32)
        for k in range(3):
            number = jnp.sum(
                jnp.where((lane[:1] % 3 == k) & (lane[:1] < 9), parts[0:1], 0.0),
                axis=1,
                keepdims=True,
            )
            summed = jnp.where(place % 3 == k, number, summed)
        value = jnp.where((row == spot[1]) & (place >= 0) & (place < 9), summed, 0.0)
        high = value.astype(BF16).astype(F32)
        middle = (value - high).astype(BF16).astype(F32)
        low = value - high - middle
        spare = jnp.where(place < 3, high, jnp.where(place < 6, middle, low))
    for h in range(2):
        main = total[h * COLS : h * COLS + LANES, :].T
        rest = total[h * COLS + LANES : (h + 1) * COLS, :]
        for m in range(QUADS):
            for side in range(2):
                start = (2 * m + side) * CHUNK
                target = held.at[side, 2 * m + h]
                target[:CHUNK, :] = main[start : start + CHUNK]
                target[CHUNK:SLOT, :] = jnp.zeros((SLOT - CHUNK, LANES), F32)
                target[SLOT:, :] = jnp.zeros((8, LANES), F32) if spare is None else spare
                for k in range(2):
                    target[SLOT:, 64 * k : 64 * k + CHUNK] = rest[
                        8 * k : 8 * k + 8, start : start + CHUNK
                    ]
    kept[...] = held[spot[1]]
    given[...] = held[1 - spot[1]].astype(BF16)


def heads(with_stats, spot, feat, spreads):
    shape = (2 * QUADS, SLOT + 8, LANES)
    return pl.pallas_call(
        functools.partial(head_kernel, with_stats),
        in_specs=[SMEM] + [VMEM] * (1 + len(spreads)),
        out_specs=[VMEM, VMEM],
        out_shape=[jax.ShapeDtypeStruct(shape, F32), jax.ShapeDtypeStruct(shape, BF16)],
        scratch_shapes=[pltpu.VMEM((2, *shape), F32)],
        compiler_params=params(24),
        cost_estimate=cost(2 * 4 * ROWS * 2 * COLS * feat.shape[1], 4 * 2**20),
    )(spot, feat, *spreads)


def mix_kernel(kept_img, taken_img, kept_txt, taken_txt, out):
    out[:, :SLAB, :] = (kept_img[...] + taken_img[...].astype(F32)).astype(BF16)
    out[:, SLAB:, :] = (kept_txt[...] + taken_txt[...].astype(F32)).astype(BF16)


def mix(*arrays):
    return pl.pallas_call(
        mix_kernel,
        in_specs=[VMEM] * 4,
        out_specs=VMEM,
        out_shape=jax.ShapeDtypeStruct((2 * QUADS, 2 * SLAB, LANES), BF16),
        compiler_params=params(16),
        cost_estimate=cost(4 * QUADS * SLAB * LANES, 2**20),
    )(*arrays)


def final_kernel(count, parts, out_img, out_txt, stats):
    both = jnp.sum(parts[...].astype(F32), axis=0)
    for out, total in ((out_img, both[:SLAB]), (out_txt, both[SLAB:])):
        out[:, :LANES] = total[:CHUNK]
        rest = total[SLOT:, :].T
        out[:, LANES : LANES + 8] = rest[:CHUNK]
        out[:, LANES + 8 :] = rest[64 : 64 + CHUNK]
    place = lax.broadcasted_iota(jnp.int32, (1, LANES), 1) - STATS
    row = both[SLOT : SLOT + 1] + both[SLOT + 1 : SLOT + 2]
    for k in range(3):
        chosen = jnp.where((place % 3 == k) & (place >= 0) & (place < 9), row, 0.0)
        stats[k] = jnp.sum(chosen) * (1.0 / count)


def final(count, parts):
    grad = jax.ShapeDtypeStruct((CHUNK, COLS), F32)
    return pl.pallas_call(
        functools.partial(final_kernel, count),
        in_specs=[VMEM],
        out_specs=[VMEM, VMEM, SMEM],
        out_shape=[grad, grad, jax.ShapeDtypeStruct((3,), F32)],
        compiler_params=params(8),
        cost_estimate=cost(4 * QUADS * SLAB * LANES, 2**20),
    )(parts)


def body(pictures, sentences, keys, picture_weights, sentence_weights, heat_log, shift_value):
    ways = lax.axis_size("dx")
    spot = jnp.stack([lax.axis_index(axis) for axis in ("dx", "lc")]).astype(jnp.int32)
    scal = (heat_log, shift_value)
    txt = project(sentences[0], sentence_weights, keys)
    txt_a = exchange(txt, "lz", 1)
    txt_y2 = exchange(txt, "ly", 2)
    txt_y1 = exchange(txt, "ly", 1)
    txt_c = exchange(txt, "lc", 1)
    img_feat = lax.all_gather(after(pictures[0], txt), "dx", axis=0, tiled=True)
    txt_feat = lax.all_gather(after(sentences[0], txt), "dx", axis=0, tiled=True)

    features = (pictures[0], sentences[0])
    weights = (picture_weights, sentence_weights)
    img, near_rows, *first = early(spot, scal, features, weights, keys, [txt, txt_c])
    img_part = (*first[:3], *first[5:])
    txt_b = exchange(after(txt_a, txt_y1, txt_y2), "lz", 3)
    img_a = exchange(img, "lz", 1)
    img_c = exchange(after(img, txt_a, txt_y1, txt_y2), "lc", 1)
    img_n = after(img, img_c)
    img_y2 = exchange(img_n, "ly", 2)
    img_y1 = exchange(img_n, "ly", 1)
    img_b = exchange(img_a, "lz", 3)

    count = 2 * QUADS * lax.axis_size("dz") * ways

    def turn(array, axis, step):
        size = lax.axis_size(axis)
        return lax.ppermute(array, axis, [(i, (i + step) % size) for i in range(size)])

    def columns(outs):
        return [outs[0]] + [turn(out, "dx", step) for step, out in enumerate(outs) if step]

    last = after(txt_b, img_feat, img_a, img_c, img_y1, img_y2)
    *img_outs, far_rows = late(
        True, ways, spot, scal, img, img_part, [txt_y1, txt_y2, txt_a, last]
    )
    img_cols = columns(img_outs)
    txt_total = middle(
        scal, txt, first[5], near_rows, far_rows, img, img_c, img_y1, img_y2, img_a
    )
    txt_part = (txt_total, *first[3:5], first[5], first[5])
    last = after(img_b, txt_feat, *img_cols, txt_total)
    outs = late(False, ways, spot, scal, txt, txt_part, [far_rows, last])
    txt_cols = columns(outs)
    img_kept, img_given = heads(True, spot, after(img_feat, outs[0]), img_cols)
    img_taken = exchange(img_given, "lc", 1)
    txt_kept, txt_given = heads(False, spot, txt_feat, txt_cols)
    txt_taken = exchange(txt_given, "lc", 1)
    sums = mix(img_kept, img_taken, txt_kept, txt_taken)
    sums = lax.all_to_all(sums, ("ly", "lz", "dz"), 0, 0, tiled=True)
    grad_img, grad_txt, stats = final(count, sums)
    return grad_img, grad_txt, stats


def solution(mesh):
    split = Mesh(mesh.devices.reshape(4, 4, 2, 2, 4), ("ly", "lz", "lc", "dz", "dx"))
    dp = ("dz", "dx")
    return jax.shard_map(
        body,
        mesh=split,
        in_specs=(P(dp, LOSS, None), P(dp, LOSS, None), P(dp, LOSS), P(), P(), P(), P()),
        out_specs=(P(LOSS, dp), P(LOSS, dp), P()),
        check_vma=False,
    )
```

```python
import functools

import jax
import jax.numpy as jnp
from jax import lax
from jax.experimental import pallas as pl
from jax.experimental.pallas import tpu as pltpu
from jax.sharding import Mesh, PartitionSpec as P

EPSILON = 1e-06
LOSS = ("ly", "lz", "lc")
ROWS = 128
WIDTH = 1152
KEY_ROWS = 16
CHUNK = 36
SLOT = 40
COLS = 144
LANES = 128
TAIL = COLS - LANES
QUADS = 16
STATS = 112
DEPTH = 128
PIECES = WIDTH // DEPTH
SLAB = SLOT + 8
F32 = jnp.float32
BF16 = jnp.bfloat16

VMEM = pl.BlockSpec(memory_space=pltpu.VMEM)
SMEM = pl.BlockSpec(memory_space=pltpu.SMEM)


def params(megabytes):
    return pltpu.CompilerParams(vmem_limit_bytes=megabytes * 2**20)


def cost(flops, moved):
    return pl.CostEstimate(flops=flops, bytes_accessed=moved, transcendentals=0)


def exchange(array, axis, apart):
    return lax.ppermute(array, axis, [(i, i ^ apart) for i in range(lax.axis_size(axis))])


def after(array, *others):
    return lax.optimization_barrier((array, *others))[0]


def nt(a, b):
    return lax.dot_general(a, b, (((1,), (1,)), ((), ())), preferred_element_type=F32)


def mm(a, b):
    return jnp.dot(a, b, preferred_element_type=F32)


def project_kernel(x_hbm, w_hbm, key_hbm, out_ref, x, w, key, sems):
    copies = [
        pltpu.make_async_copy(x_hbm, x, sems.at[0]),
        pltpu.make_async_copy(key_hbm, key, sems.at[1]),
    ]
    for k in range(PIECES):
        span = pl.ds(k * DEPTH, DEPTH)
        copies.append(pltpu.make_async_copy(w_hbm.at[span], w.at[span], sems.at[2 + k]))
    for copy in copies:
        copy.start()
    copies[0].wait()
    u = jnp.zeros((ROWS, WIDTH), F32)
    for k in range(PIECES):
        copies[2 + k].wait()
        span = slice(k * DEPTH, (k + 1) * DEPTH)
        u += mm(x[:, span], w[span])
    copies[1].wait()
    write_payload(out_ref, u / lengths(u), key[...])


def lengths(u):
    return jnp.sqrt(jnp.sum(u * u, axis=1, keepdims=True) + EPSILON)


def project(x, w, keys):
    return pl.pallas_call(
        project_kernel,
        in_specs=[pl.BlockSpec(memory_space=pltpu.HBM)] * 3,
        out_specs=VMEM,
        out_shape=jax.ShapeDtypeStruct((ROWS + KEY_ROWS, WIDTH), BF16),
        scratch_shapes=[
            pltpu.VMEM((ROWS, WIDTH), BF16),
            pltpu.VMEM((WIDTH, WIDTH), BF16),
            pltpu.VMEM((1, ROWS), jnp.int32),
            pltpu.SemaphoreType.DMA((2 + PIECES,)),
        ],
        compiler_params=params(56),
        cost_estimate=cost(2 * ROWS * WIDTH * WIDTH, 4 * 2**20),
    )(x, w, keys)


def temperature(heat_log):
    return jnp.exp(jnp.full((1, 1), heat_log[0], F32))


def caption_row(block):
    digits = block[ROWS:, :LANES].astype(F32)
    return digits[0:1] * 128.0 + digits[1:2]


def add_tiles(with_stats, heat, shift, mine, key_col, pairs, total, sums):
    for block, key_row in pairs:
        vec = block[:ROWS, :]
        same = key_col == key_row
        sim = nt(mine, vec)
        logits = heat * sim + shift
        z = jnp.where(same, -logits, logits)
        t = jnp.exp(-jnp.abs(z))
        q = 1.0 / (1.0 + t)
        sig = jnp.where(z >= 0, q, t * q)
        g = jnp.where(same, -sig, sig) * (1.0 / ROWS)
        total += mm(g.astype(BF16), vec)
        if with_stats:
            new = (jnp.maximum(z, 0.0) + jnp.log1p(t), g * sim, g)
            sums = [old + add for old, add in zip(sums, new)]
    return total, sums


def pair_up(blocks, rows_ref):
    pairs = []
    for k, block in enumerate(blocks):
        key_row = caption_row(block)
        rows_ref[k] = jnp.broadcast_to(key_row, (8, LANES))
        pairs.append((block, key_row))
    return pairs


def write_payload(out_ref, unit, key):
    digit = jnp.broadcast_to(key, (KEY_ROWS, ROWS))
    row = lax.broadcasted_iota(jnp.int32, (KEY_ROWS, ROWS), 0)
    digit = jnp.where(row == 0, digit >> 7, jnp.where(row == 1, digit & 127, 0))
    out_ref[:ROWS, :] = unit.astype(BF16)
    out_ref[ROWS:, :] = jnp.zeros((KEY_ROWS, WIDTH), BF16)
    out_ref[ROWS:, :ROWS] = digit.astype(F32).astype(BF16)


def early_kernel(spot, heat_log, shift, xs, xt, ws_hbm, wt_hbm, key, *refs):
    *blocks, own, rows_ref, total_ref, unit_img, len_img, unit_txt, len_txt = refs[:-4]
    key_ref, sum_ref, w, sems = refs[-4:]
    copies = [
        pltpu.make_async_copy(ws_hbm, w.at[0], sems.at[0]),
        pltpu.make_async_copy(wt_hbm, w.at[1], sems.at[1]),
    ]
    for copy in copies:
        copy.start()
    key_col = jnp.broadcast_to(key[...].astype(F32), (ROWS, ROWS)).T
    key_ref[...] = key_col
    towers = ((xs, unit_img, len_img), (xt, unit_txt, len_txt))

    def norm(t):
        x, unit_ref, len_ref = towers[t]
        copies[t].wait()
        u = mm(x[...], w[t])
        length = lengths(u)
        unit_ref[...] = u / length
        len_ref[...] = jnp.broadcast_to(length, len_ref.shape)

    norm(0)
    own[...] = unit_img[...].astype(BF16)
    zero = jnp.zeros((ROWS, ROWS), F32)
    total, sums = add_tiles(
        True,
        temperature(heat_log),
        shift[0],
        own[...],
        key_col,
        pair_up(blocks, rows_ref),
        jnp.zeros((ROWS, WIDTH), F32),
        [zero] * 3,
    )
    total_ref[...] = total
    for k in range(3):
        sum_ref[k] = sums[k]
    norm(1)


def early(spot, scal, features, weights, keys, blocks):
    shapes = [(ROWS, WIDTH), (ROWS, LANES)]
    shapes = [(ROWS, WIDTH), *shapes, *shapes, (ROWS, ROWS), (3, ROWS, ROWS)]
    outs = [
        jax.ShapeDtypeStruct((ROWS, WIDTH), BF16),
        jax.ShapeDtypeStruct((len(blocks), 8, LANES), F32),
    ] + [jax.ShapeDtypeStruct(shape, F32) for shape in shapes]
    hbm = pl.BlockSpec(memory_space=pltpu.HBM)
    return pl.pallas_call(
        early_kernel,
        in_specs=[SMEM] * 3 + [VMEM] * 2 + [hbm] * 2 + [VMEM] * (1 + len(blocks)),
        out_specs=[VMEM] * len(outs),
        out_shape=outs,
        scratch_shapes=[pltpu.VMEM((2, WIDTH, WIDTH), BF16), pltpu.SemaphoreType.DMA((2,))],
        compiler_params=params(56),
        cost_estimate=cost(4 * 5 * ROWS * ROWS * WIDTH, 8 * 2**20),
    )(spot, *scal, *features, *weights, keys, *blocks)


def middle_kernel(heat_log, shift, own, key, near_rows, far_rows, *refs):
    *blocks, total_ref = refs
    rows = [near_rows[0], near_rows[1], far_rows[0], far_rows[1], far_rows[2]]
    zero = jnp.zeros((ROWS, ROWS), F32)
    total, _ = add_tiles(
        False,
        temperature(heat_log),
        shift[0],
        own[:ROWS, :],
        key[...],
        [(block, row[0:1]) for block, row in zip(blocks, rows)],
        jnp.zeros((ROWS, WIDTH), F32),
        [zero] * 3,
    )
    total_ref[...] = total


def middle(scal, *arrays):
    return pl.pallas_call(
        middle_kernel,
        in_specs=[SMEM] * 2 + [VMEM] * len(arrays),
        out_specs=VMEM,
        out_shape=jax.ShapeDtypeStruct((ROWS, WIDTH), F32),
        compiler_params=params(56),
        cost_estimate=cost(4 * 5 * ROWS * ROWS * WIDTH, 4 * 2**20),
    )(*scal, *arrays)


def late_kernel(with_stats, ways, count, spot, heat_log, shift, own, *refs):
    total_ref, unit, length, key, acc, *refs = refs
    blocks, outs, held = refs[:count], refs[count:-1], refs[-1]
    heat = temperature(heat_log)
    if with_stats:
        *outs, rows_ref = outs
        pairs = pair_up(blocks, rows_ref)
    else:
        rows, block = blocks
        pairs = [(block, rows[3][0:1])]
    total, sums = add_tiles(
        with_stats,
        heat,
        shift[0],
        own[:ROWS, :],
        key[...],
        pairs,
        total_ref[...],
        [acc[k] for k in range(3)] if with_stats else [acc[...]] * 3,
    )
    total = total * heat
    u = unit[...]
    inner = jnp.sum(u * total, axis=1, keepdims=True)
    du = (total - u * inner) / length[:, :1]
    held[...] = du.T.astype(BF16).reshape(held.shape)
    if with_stats:
        def full(x):
            return jnp.sum(jnp.sum(x, axis=1, keepdims=True), axis=0, keepdims=True)

        lane = lax.broadcasted_iota(jnp.int32, (KEY_ROWS, LANES), 1)
        row = lax.broadcasted_iota(jnp.int32, (KEY_ROWS, LANES), 0)
        kind = lane % 3
        value = jnp.where(
            kind == 0,
            full(sums[0]) * (1.0 / ROWS),
            jnp.where(kind == 1, full(sums[1]) * heat, full(sums[2])),
        )
        value = jnp.where((row == 0) & (lane < 9), value, 0.0)
        high = value.astype(BF16).astype(F32)
        middle = (value - high).astype(BF16).astype(F32)
        low = value - high - middle
        parts = jnp.where(lane < 3, high, jnp.where(lane < 6, middle, low)).astype(BF16)
        for out in outs:
            out[2 * COLS :, :] = parts
    for step, out in enumerate(outs):
        w = lax.rem(spot[0] + step, ways)
        for h in range(2):
            out[h * COLS : (h + 1) * COLS, :] = held[h * ways + w]


def late(with_stats, ways, spot, scal, own, partial, blocks):
    rows = 2 * COLS + (KEY_ROWS if with_stats else 0)
    shapes = [jax.ShapeDtypeStruct((rows, ROWS), BF16)] * ways
    if with_stats:
        shapes.append(jax.ShapeDtypeStruct((len(blocks), 8, LANES), F32))
    return pl.pallas_call(
        functools.partial(late_kernel, with_stats, ways, len(blocks)),
        in_specs=[SMEM] * 3 + [VMEM] * (6 + len(blocks)),
        out_specs=[VMEM] * len(shapes),
        out_shape=shapes,
        scratch_shapes=[pltpu.VMEM((2 * ways, COLS, ROWS), BF16)],
        compiler_params=params(56),
        cost_estimate=cost(4 * 2 * ROWS * ROWS * WIDTH, 4 * 2**20),
    )(spot, *scal, own, *partial, *blocks)


def head_kernel(with_stats, spot, feat, *refs):
    spreads, (kept, given, held) = refs[:-3], refs[-3:]
    ways = len(spreads)
    total = jnp.zeros((2 * COLS, feat.shape[1]), F32)
    for step, spread in enumerate(spreads):
        source = lax.rem(spot[0] + ways - step, ways)
        rows = feat[pl.ds(pl.multiple_of(source * ROWS, ROWS), ROWS), :]
        total += mm(spread[: 2 * COLS, :], rows)
    spare = None
    if with_stats:
        parts = jnp.zeros((KEY_ROWS, LANES), F32)
        for spread in spreads:
            parts += spread[2 * COLS :, :].astype(F32)
        lane = lax.broadcasted_iota(jnp.int32, (8, LANES), 1)
        row = lax.broadcasted_iota(jnp.int32, (8, LANES), 0)
        place = lane - STATS
        summed = jnp.zeros((8, LANES), F32)
        for k in range(3):
            number = jnp.sum(
                jnp.where((lane[:1] % 3 == k) & (lane[:1] < 9), parts[0:1], 0.0),
                axis=1,
                keepdims=True,
            )
            summed = jnp.where(place % 3 == k, number, summed)
        value = jnp.where((row == spot[1]) & (place >= 0) & (place < 9), summed, 0.0)
        high = value.astype(BF16).astype(F32)
        middle = (value - high).astype(BF16).astype(F32)
        low = value - high - middle
        spare = jnp.where(place < 3, high, jnp.where(place < 6, middle, low))
    for h in range(2):
        main = total[h * COLS : h * COLS + LANES, :].T
        rest = total[h * COLS + LANES : (h + 1) * COLS, :]
        for m in range(QUADS):
            for side in range(2):
                start = (2 * m + side) * CHUNK
                target = held.at[side, 2 * m + h]
                target[:CHUNK, :] = main[start : start + CHUNK]
                target[CHUNK:SLOT, :] = jnp.zeros((SLOT - CHUNK, LANES), F32)
                target[SLOT:, :] = jnp.zeros((8, LANES), F32) if spare is None else spare
                for k in range(2):
                    target[SLOT:, 64 * k : 64 * k + CHUNK] = rest[
                        8 * k : 8 * k + 8, start : start + CHUNK
                    ]
    kept[...] = held[spot[1]]
    given[...] = held[1 - spot[1]].astype(BF16)


def heads(with_stats, spot, feat, spreads):
    shape = (2 * QUADS, SLOT + 8, LANES)
    return pl.pallas_call(
        functools.partial(head_kernel, with_stats),
        in_specs=[SMEM] + [VMEM] * (1 + len(spreads)),
        out_specs=[VMEM, VMEM],
        out_shape=[jax.ShapeDtypeStruct(shape, F32), jax.ShapeDtypeStruct(shape, BF16)],
        scratch_shapes=[pltpu.VMEM((2, *shape), F32)],
        compiler_params=params(24),
        cost_estimate=cost(2 * 4 * ROWS * 2 * COLS * feat.shape[1], 4 * 2**20),
    )(spot, feat, *spreads)


def mix_kernel(kept_img, taken_img, kept_txt, taken_txt, out):
    out[:, :SLAB, :] = (kept_img[...] + taken_img[...].astype(F32)).astype(BF16)
    out[:, SLAB:, :] = (kept_txt[...] + taken_txt[...].astype(F32)).astype(BF16)


def mix(*arrays):
    return pl.pallas_call(
        mix_kernel,
        in_specs=[VMEM] * 4,
        out_specs=VMEM,
        out_shape=jax.ShapeDtypeStruct((2 * QUADS, 2 * SLAB, LANES), BF16),
        compiler_params=params(16),
        cost_estimate=cost(4 * QUADS * SLAB * LANES, 2**20),
    )(*arrays)


def final_kernel(count, parts, out_img, out_txt, stats):
    both = jnp.sum(parts[...].astype(F32), axis=0)
    for out, total in ((out_img, both[:SLAB]), (out_txt, both[SLAB:])):
        out[:, :LANES] = total[:CHUNK]
        rest = total[SLOT:, :].T
        out[:, LANES : LANES + 8] = rest[:CHUNK]
        out[:, LANES + 8 :] = rest[64 : 64 + CHUNK]
    place = lax.broadcasted_iota(jnp.int32, (1, LANES), 1) - STATS
    row = both[SLOT : SLOT + 1] + both[SLOT + 1 : SLOT + 2]
    for k in range(3):
        chosen = jnp.where((place % 3 == k) & (place >= 0) & (place < 9), row, 0.0)
        stats[k] = jnp.sum(chosen) * (1.0 / count)


def final(count, parts):
    grad = jax.ShapeDtypeStruct((CHUNK, COLS), F32)
    return pl.pallas_call(
        functools.partial(final_kernel, count),
        in_specs=[VMEM],
        out_specs=[VMEM, VMEM, SMEM],
        out_shape=[grad, grad, jax.ShapeDtypeStruct((3,), F32)],
        compiler_params=params(8),
        cost_estimate=cost(4 * QUADS * SLAB * LANES, 2**20),
    )(parts)


def body(pictures, sentences, keys, picture_weights, sentence_weights, heat_log, shift_value):
    ways = lax.axis_size("dx")
    spot = jnp.stack([lax.axis_index(axis) for axis in ("dx", "lc")]).astype(jnp.int32)
    scal = (heat_log, shift_value)
    txt = project(sentences[0], sentence_weights, keys)
    txt_a = exchange(txt, "lz", 1)
    txt_y2 = exchange(txt, "ly", 2)
    txt_y1 = exchange(txt, "ly", 1)
    txt_c = exchange(txt, "lc", 1)
    img_feat = lax.all_gather(after(pictures[0], txt), "dx", axis=0, tiled=True)
    txt_feat = lax.all_gather(after(sentences[0], txt), "dx", axis=0, tiled=True)

    features = (pictures[0], sentences[0])
    weights = (picture_weights, sentence_weights)
    img, near_rows, *first = early(spot, scal, features, weights, keys, [txt, txt_c])
    img_part = (*first[:3], *first[5:])
    txt_b = exchange(after(txt_a, txt_y1, txt_y2), "lz", 3)
    img_a = exchange(img, "lz", 1)
    img_c = exchange(after(img, txt_a, txt_y1, txt_y2), "lc", 1)
    img_n = after(img, img_c)
    img_y2 = exchange(img_n, "ly", 2)
    img_y1 = exchange(img_n, "ly", 1)
    img_b = exchange(img_a, "lz", 3)

    count = 2 * QUADS * lax.axis_size("dz") * ways

    def turn(array, axis, step):
        size = lax.axis_size(axis)
        return lax.ppermute(array, axis, [(i, (i + step) % size) for i in range(size)])

    def columns(outs):
        return [outs[0]] + [turn(out, "dx", step) for step, out in enumerate(outs) if step]

    last = after(txt_b, img_feat, img_a, img_c, img_y1, img_y2)
    *img_outs, far_rows = late(
        True, ways, spot, scal, img, img_part, [txt_y1, txt_y2, txt_a, last]
    )
    img_cols = columns(img_outs)
    txt_total = middle(
        scal, txt, first[5], near_rows, far_rows, img, img_c, img_y1, img_y2, img_a
    )
    txt_part = (txt_total, *first[3:5], first[5], first[5])
    last = after(img_b, *img_cols, txt_total)
    outs = late(False, ways, spot, scal, txt, txt_part, [far_rows, last])
    txt_cols = columns(outs)
    img_kept, img_given = heads(True, spot, after(img_feat, outs[0], txt_feat), img_cols)
    img_taken = exchange(img_given, "lc", 1)
    txt_kept, txt_given = heads(False, spot, txt_feat, txt_cols)
    txt_taken = exchange(txt_given, "lc", 1)
    sums = mix(img_kept, img_taken, txt_kept, txt_taken)
    sums = lax.all_to_all(sums, ("ly", "lz", "dz"), 0, 0, tiled=True)
    grad_img, grad_txt, stats = final(count, sums)
    return grad_img, grad_txt, stats


def solution(mesh):
    split = Mesh(mesh.devices.reshape(4, 4, 2, 2, 4), ("ly", "lz", "lc", "dz", "dx"))
    dp = ("dz", "dx")
    return jax.shard_map(
        body,
        mesh=split,
        in_specs=(P(dp, LOSS, None), P(dp, LOSS, None), P(dp, LOSS), P(), P(), P(), P()),
        out_specs=(P(LOSS, dp), P(LOSS, dp), P()),
        check_vma=False,
    )
```

```python
import functools

import jax
import jax.numpy as jnp
from jax import lax
from jax.experimental import pallas as pl
from jax.experimental.pallas import tpu as pltpu
from jax.sharding import Mesh, PartitionSpec as P

EPSILON = 1e-06
LOSS = ("ly", "lz", "lc")
ROWS = 128
WIDTH = 1152
KEY_ROWS = 16
CHUNK = 36
SLOT = 40
COLS = 144
LANES = 128
TAIL = COLS - LANES
QUADS = 16
STATS = 112
DEPTH = 128
PIECES = WIDTH // DEPTH
SLAB = SLOT + 8
F32 = jnp.float32
BF16 = jnp.bfloat16

VMEM = pl.BlockSpec(memory_space=pltpu.VMEM)
SMEM = pl.BlockSpec(memory_space=pltpu.SMEM)


def params(megabytes):
    return pltpu.CompilerParams(vmem_limit_bytes=megabytes * 2**20)


def cost(flops, moved):
    return pl.CostEstimate(flops=flops, bytes_accessed=moved, transcendentals=0)


def exchange(array, axis, apart):
    return lax.ppermute(array, axis, [(i, i ^ apart) for i in range(lax.axis_size(axis))])


def after(array, *others):
    return lax.optimization_barrier((array, *others))[0]


def nt(a, b):
    return lax.dot_general(a, b, (((1,), (1,)), ((), ())), preferred_element_type=F32)


def mm(a, b):
    return jnp.dot(a, b, preferred_element_type=F32)


def project_kernel(x_hbm, w_hbm, key_hbm, out_ref, x, w, key, sems):
    copies = [
        pltpu.make_async_copy(x_hbm, x, sems.at[0]),
        pltpu.make_async_copy(key_hbm, key, sems.at[1]),
    ]
    for k in range(PIECES):
        span = pl.ds(k * DEPTH, DEPTH)
        copies.append(pltpu.make_async_copy(w_hbm.at[span], w.at[span], sems.at[2 + k]))
    for copy in copies:
        copy.start()
    copies[0].wait()
    u = jnp.zeros((ROWS, WIDTH), F32)
    for k in range(PIECES):
        copies[2 + k].wait()
        span = slice(k * DEPTH, (k + 1) * DEPTH)
        u += mm(x[:, span], w[span])
    copies[1].wait()
    write_payload(out_ref, u / lengths(u), key[...])


def lengths(u):
    return jnp.sqrt(jnp.sum(u * u, axis=1, keepdims=True) + EPSILON)


def project(x, w, keys):
    return pl.pallas_call(
        project_kernel,
        in_specs=[pl.BlockSpec(memory_space=pltpu.HBM)] * 3,
        out_specs=VMEM,
        out_shape=jax.ShapeDtypeStruct((ROWS + KEY_ROWS, WIDTH), BF16),
        scratch_shapes=[
            pltpu.VMEM((ROWS, WIDTH), BF16),
            pltpu.VMEM((WIDTH, WIDTH), BF16),
            pltpu.VMEM((1, ROWS), jnp.int32),
            pltpu.SemaphoreType.DMA((2 + PIECES,)),
        ],
        compiler_params=params(56),
        cost_estimate=cost(2 * ROWS * WIDTH * WIDTH, 4 * 2**20),
    )(x, w, keys)


def temperature(heat_log):
    return jnp.exp(jnp.full((1, 1), heat_log[0], F32))


def caption_row(block):
    digits = block[ROWS:, :LANES].astype(F32)
    return digits[0:1] * 128.0 + digits[1:2]


def add_tiles(with_stats, heat, shift, mine, key_col, pairs, total, sums):
    for block, key_row in pairs:
        vec = block[:ROWS, :]
        same = key_col == key_row
        sim = nt(mine, vec)
        logits = heat * sim + shift
        z = jnp.where(same, -logits, logits)
        t = jnp.exp(-jnp.abs(z))
        q = 1.0 / (1.0 + t)
        sig = jnp.where(z >= 0, q, t * q)
        g = jnp.where(same, -sig, sig) * (1.0 / ROWS)
        total += mm(g.astype(BF16), vec)
        if with_stats:
            new = (jnp.maximum(z, 0.0) + jnp.log1p(t), g * sim, g)
            sums = [old + add for old, add in zip(sums, new)]
    return total, sums


def pair_up(blocks, rows_ref):
    pairs = []
    for k, block in enumerate(blocks):
        key_row = caption_row(block)
        rows_ref[k] = jnp.broadcast_to(key_row, (8, LANES))
        pairs.append((block, key_row))
    return pairs


def write_payload(out_ref, unit, key):
    digit = jnp.broadcast_to(key, (KEY_ROWS, ROWS))
    row = lax.broadcasted_iota(jnp.int32, (KEY_ROWS, ROWS), 0)
    digit = jnp.where(row == 0, digit >> 7, jnp.where(row == 1, digit & 127, 0))
    out_ref[:ROWS, :] = unit.astype(BF16)
    out_ref[ROWS:, :] = jnp.zeros((KEY_ROWS, WIDTH), BF16)
    out_ref[ROWS:, :ROWS] = digit.astype(F32).astype(BF16)


def early_kernel(spot, heat_log, shift, xs, xt, ws_hbm, wt_hbm, key, *refs):
    *blocks, own, rows_ref, total_ref, unit_img, len_img, unit_txt, len_txt = refs[:-4]
    key_ref, sum_ref, w, sems = refs[-4:]
    copies = [
        pltpu.make_async_copy(ws_hbm, w.at[0], sems.at[0]),
        pltpu.make_async_copy(wt_hbm, w.at[1], sems.at[1]),
    ]
    for copy in copies:
        copy.start()
    key_col = jnp.broadcast_to(key[...].astype(F32), (ROWS, ROWS)).T
    key_ref[...] = key_col
    towers = ((xs, unit_img, len_img), (xt, unit_txt, len_txt))

    def norm(t):
        x, unit_ref, len_ref = towers[t]
        copies[t].wait()
        u = mm(x[...], w[t])
        length = lengths(u)
        unit_ref[...] = u / length
        len_ref[...] = jnp.broadcast_to(length, len_ref.shape)

    norm(0)
    own[...] = unit_img[...].astype(BF16)
    zero = jnp.zeros((ROWS, ROWS), F32)
    total, sums = add_tiles(
        True,
        temperature(heat_log),
        shift[0],
        own[...],
        key_col,
        pair_up(blocks, rows_ref),
        jnp.zeros((ROWS, WIDTH), F32),
        [zero] * 3,
    )
    total_ref[...] = total
    for k in range(3):
        sum_ref[k] = sums[k]
    norm(1)


def early(spot, scal, features, weights, keys, blocks):
    shapes = [(ROWS, WIDTH), (ROWS, LANES)]
    shapes = [(ROWS, WIDTH), *shapes, *shapes, (ROWS, ROWS), (3, ROWS, ROWS)]
    outs = [
        jax.ShapeDtypeStruct((ROWS, WIDTH), BF16),
        jax.ShapeDtypeStruct((len(blocks), 8, LANES), F32),
    ] + [jax.ShapeDtypeStruct(shape, F32) for shape in shapes]
    hbm = pl.BlockSpec(memory_space=pltpu.HBM)
    return pl.pallas_call(
        early_kernel,
        in_specs=[SMEM] * 3 + [VMEM] * 2 + [hbm] * 2 + [VMEM] * (1 + len(blocks)),
        out_specs=[VMEM] * len(outs),
        out_shape=outs,
        scratch_shapes=[pltpu.VMEM((2, WIDTH, WIDTH), BF16), pltpu.SemaphoreType.DMA((2,))],
        compiler_params=params(56),
        cost_estimate=cost(4 * 5 * ROWS * ROWS * WIDTH, 8 * 2**20),
    )(spot, *scal, *features, *weights, keys, *blocks)


def image_kernel(heat_log, shift, own, total_ref, key, acc, *refs):
    *blocks, out_ref, sum_ref, rows_ref = refs
    total, sums = add_tiles(
        True,
        temperature(heat_log),
        shift[0],
        own[...],
        key[...],
        pair_up(blocks, rows_ref),
        total_ref[...],
        [acc[k] for k in range(3)],
    )
    out_ref[...] = total
    for k in range(3):
        sum_ref[k] = sums[k]


def image_tiles(scal, own, total, key, acc, blocks):
    shapes = [(ROWS, WIDTH), (3, ROWS, ROWS), (len(blocks), 8, LANES)]
    return pl.pallas_call(
        image_kernel,
        in_specs=[SMEM] * 2 + [VMEM] * (4 + len(blocks)),
        out_specs=[VMEM] * 3,
        out_shape=[jax.ShapeDtypeStruct(shape, F32) for shape in shapes],
        compiler_params=params(56),
        cost_estimate=cost(4 * 3 * ROWS * ROWS * WIDTH, 4 * 2**20),
    )(*scal, own, total, key, acc, *blocks)


def middle_kernel(heat_log, shift, own, key, near_rows, far_rows, *refs):
    *blocks, total_ref = refs
    rows = [near_rows[0], near_rows[1], far_rows[0], far_rows[1], far_rows[2]]
    zero = jnp.zeros((ROWS, ROWS), F32)
    total, _ = add_tiles(
        False,
        temperature(heat_log),
        shift[0],
        own[:ROWS, :],
        key[...],
        [(block, row[0:1]) for block, row in zip(blocks, rows)],
        jnp.zeros((ROWS, WIDTH), F32),
        [zero] * 3,
    )
    total_ref[...] = total


def middle(scal, *arrays):
    return pl.pallas_call(
        middle_kernel,
        in_specs=[SMEM] * 2 + [VMEM] * len(arrays),
        out_specs=VMEM,
        out_shape=jax.ShapeDtypeStruct((ROWS, WIDTH), F32),
        compiler_params=params(56),
        cost_estimate=cost(4 * 5 * ROWS * ROWS * WIDTH, 4 * 2**20),
    )(*scal, *arrays)


def late_kernel(with_stats, ways, count, spot, heat_log, shift, own, *refs):
    total_ref, unit, length, key, acc, *refs = refs
    blocks, outs, held = refs[:count], refs[count:-1], refs[-1]
    heat = temperature(heat_log)
    if with_stats:
        *outs, rows_ref = outs
        pairs = pair_up(blocks, rows_ref)
    else:
        rows, block = blocks
        pairs = [(block, rows[0][0:1])]
    total, sums = add_tiles(
        with_stats,
        heat,
        shift[0],
        own[:ROWS, :],
        key[...],
        pairs,
        total_ref[...],
        [acc[k] for k in range(3)] if with_stats else [acc[...]] * 3,
    )
    total = total * heat
    u = unit[...]
    inner = jnp.sum(u * total, axis=1, keepdims=True)
    du = (total - u * inner) / length[:, :1]
    held[...] = du.T.astype(BF16).reshape(held.shape)
    if with_stats:
        def full(x):
            return jnp.sum(jnp.sum(x, axis=1, keepdims=True), axis=0, keepdims=True)

        lane = lax.broadcasted_iota(jnp.int32, (KEY_ROWS, LANES), 1)
        row = lax.broadcasted_iota(jnp.int32, (KEY_ROWS, LANES), 0)
        kind = lane % 3
        value = jnp.where(
            kind == 0,
            full(sums[0]) * (1.0 / ROWS),
            jnp.where(kind == 1, full(sums[1]) * heat, full(sums[2])),
        )
        value = jnp.where((row == 0) & (lane < 9), value, 0.0)
        high = value.astype(BF16).astype(F32)
        middle = (value - high).astype(BF16).astype(F32)
        low = value - high - middle
        parts = jnp.where(lane < 3, high, jnp.where(lane < 6, middle, low)).astype(BF16)
        for out in outs:
            out[2 * COLS :, :] = parts
    for step, out in enumerate(outs):
        w = lax.rem(spot[0] + step, ways)
        for h in range(2):
            out[h * COLS : (h + 1) * COLS, :] = held[h * ways + w]


def late(with_stats, ways, spot, scal, own, partial, blocks):
    rows = 2 * COLS + (KEY_ROWS if with_stats else 0)
    shapes = [jax.ShapeDtypeStruct((rows, ROWS), BF16)] * ways
    if with_stats:
        shapes.append(jax.ShapeDtypeStruct((len(blocks), 8, LANES), F32))
    return pl.pallas_call(
        functools.partial(late_kernel, with_stats, ways, len(blocks)),
        in_specs=[SMEM] * 3 + [VMEM] * (6 + len(blocks)),
        out_specs=[VMEM] * len(shapes),
        out_shape=shapes,
        scratch_shapes=[pltpu.VMEM((2 * ways, COLS, ROWS), BF16)],
        compiler_params=params(56),
        cost_estimate=cost(4 * 2 * ROWS * ROWS * WIDTH, 4 * 2**20),
    )(spot, *scal, own, *partial, *blocks)


def head_kernel(with_stats, spot, feat, *refs):
    spreads, (kept, given, held) = refs[:-3], refs[-3:]
    ways = len(spreads)
    total = jnp.zeros((2 * COLS, feat.shape[1]), F32)
    for step, spread in enumerate(spreads):
        source = lax.rem(spot[0] + ways - step, ways)
        rows = feat[pl.ds(pl.multiple_of(source * ROWS, ROWS), ROWS), :]
        total += mm(spread[: 2 * COLS, :], rows)
    spare = None
    if with_stats:
        parts = jnp.zeros((KEY_ROWS, LANES), F32)
        for spread in spreads:
            parts += spread[2 * COLS :, :].astype(F32)
        lane = lax.broadcasted_iota(jnp.int32, (8, LANES), 1)
        row = lax.broadcasted_iota(jnp.int32, (8, LANES), 0)
        place = lane - STATS
        summed = jnp.zeros((8, LANES), F32)
        for k in range(3):
            number = jnp.sum(
                jnp.where((lane[:1] % 3 == k) & (lane[:1] < 9), parts[0:1], 0.0),
                axis=1,
                keepdims=True,
            )
            summed = jnp.where(place % 3 == k, number, summed)
        value = jnp.where((row == spot[1]) & (place >= 0) & (place < 9), summed, 0.0)
        high = value.astype(BF16).astype(F32)
        middle = (value - high).astype(BF16).astype(F32)
        low = value - high - middle
        spare = jnp.where(place < 3, high, jnp.where(place < 6, middle, low))
    for h in range(2):
        main = total[h * COLS : h * COLS + LANES, :].T
        rest = total[h * COLS + LANES : (h + 1) * COLS, :]
        for m in range(QUADS):
            for side in range(2):
                start = (2 * m + side) * CHUNK
                target = held.at[side, 2 * m + h]
                target[:CHUNK, :] = main[start : start + CHUNK]
                target[CHUNK:SLOT, :] = jnp.zeros((SLOT - CHUNK, LANES), F32)
                target[SLOT:, :] = jnp.zeros((8, LANES), F32) if spare is None else spare
                for k in range(2):
                    target[SLOT:, 64 * k : 64 * k + CHUNK] = rest[
                        8 * k : 8 * k + 8, start : start + CHUNK
                    ]
    kept[...] = held[spot[1]]
    given[...] = held[1 - spot[1]].astype(BF16)


def heads(with_stats, spot, feat, spreads):
    shape = (2 * QUADS, SLOT + 8, LANES)
    return pl.pallas_call(
        functools.partial(head_kernel, with_stats),
        in_specs=[SMEM] + [VMEM] * (1 + len(spreads)),
        out_specs=[VMEM, VMEM],
        out_shape=[jax.ShapeDtypeStruct(shape, F32), jax.ShapeDtypeStruct(shape, BF16)],
        scratch_shapes=[pltpu.VMEM((2, *shape), F32)],
        compiler_params=params(24),
        cost_estimate=cost(2 * 4 * ROWS * 2 * COLS * feat.shape[1], 4 * 2**20),
    )(spot, feat, *spreads)


def mix_kernel(kept_img, taken_img, kept_txt, taken_txt, out):
    out[:, :SLAB, :] = (kept_img[...] + taken_img[...].astype(F32)).astype(BF16)
    out[:, SLAB:, :] = (kept_txt[...] + taken_txt[...].astype(F32)).astype(BF16)


def mix(*arrays):
    return pl.pallas_call(
        mix_kernel,
        in_specs=[VMEM] * 4,
        out_specs=VMEM,
        out_shape=jax.ShapeDtypeStruct((2 * QUADS, 2 * SLAB, LANES), BF16),
        compiler_params=params(16),
        cost_estimate=cost(4 * QUADS * SLAB * LANES, 2**20),
    )(*arrays)


def final_kernel(count, parts, out_img, out_txt, stats):
    both = jnp.sum(parts[...].astype(F32), axis=0)
    for out, total in ((out_img, both[:SLAB]), (out_txt, both[SLAB:])):
        out[:, :LANES] = total[:CHUNK]
        rest = total[SLOT:, :].T
        out[:, LANES : LANES + 8] = rest[:CHUNK]
        out[:, LANES + 8 :] = rest[64 : 64 + CHUNK]
    place = lax.broadcasted_iota(jnp.int32, (1, LANES), 1) - STATS
    row = both[SLOT : SLOT + 1] + both[SLOT + 1 : SLOT + 2]
    for k in range(3):
        chosen = jnp.where((place % 3 == k) & (place >= 0) & (place < 9), row, 0.0)
        stats[k] = jnp.sum(chosen) * (1.0 / count)


def final(count, parts):
    grad = jax.ShapeDtypeStruct((CHUNK, COLS), F32)
    return pl.pallas_call(
        functools.partial(final_kernel, count),
        in_specs=[VMEM],
        out_specs=[VMEM, VMEM, SMEM],
        out_shape=[grad, grad, jax.ShapeDtypeStruct((3,), F32)],
        compiler_params=params(8),
        cost_estimate=cost(4 * QUADS * SLAB * LANES, 2**20),
    )(parts)


def body(pictures, sentences, keys, picture_weights, sentence_weights, heat_log, shift_value):
    ways = lax.axis_size("dx")
    spot = jnp.stack([lax.axis_index(axis) for axis in ("dx", "lc")]).astype(jnp.int32)
    scal = (heat_log, shift_value)
    txt = project(sentences[0], sentence_weights, keys)
    txt_a = exchange(txt, "lz", 1)
    txt_y2 = exchange(txt, "ly", 2)
    txt_y1 = exchange(txt, "ly", 1)
    txt_c = exchange(txt, "lc", 1)
    img_feat = lax.all_gather(after(pictures[0], txt), "dx", axis=0, tiled=True)
    txt_feat = lax.all_gather(after(sentences[0], txt), "dx", axis=0, tiled=True)

    features = (pictures[0], sentences[0])
    weights = (picture_weights, sentence_weights)
    img, near_rows, *first = early(spot, scal, features, weights, keys, [txt, txt_c])
    txt_b = exchange(after(txt_a, txt_y1, txt_y2), "lz", 3)
    img_a = exchange(img, "lz", 1)
    img_c = exchange(after(img, txt_a, txt_y1, txt_y2), "lc", 1)
    total, acc, mid_rows = image_tiles(
        scal, img, first[0], first[5], first[6], [after(txt_y1, img_c), txt_y2, txt_a]
    )
    img_part = (total, *first[1:3], first[5], acc)
    img_n = after(img, img_c, acc)
    img_y2 = exchange(img_n, "ly", 2)
    img_y1 = exchange(img_n, "ly", 1)
    img_b = exchange(img_a, "lz", 3)

    count = 2 * QUADS * lax.axis_size("dz") * ways

    def turn(array, axis, step):
        size = lax.axis_size(axis)
        return lax.ppermute(array, axis, [(i, (i + step) % size) for i in range(size)])

    def columns(outs):
        return [outs[0]] + [turn(out, "dx", step) for step, out in enumerate(outs) if step]

    last = after(txt_b, img_feat, img_a, img_c, img_y1, img_y2)
    *img_outs, far_rows = late(
        True, ways, spot, scal, img, img_part, [last]
    )
    img_cols = columns(img_outs)
    txt_total = middle(
        scal, txt, first[5], near_rows, mid_rows, img, img_c, img_y1, img_y2, img_a
    )
    txt_part = (txt_total, *first[3:5], first[5], first[5])
    last = after(img_b, *img_cols, txt_total)
    outs = late(False, ways, spot, scal, txt, txt_part, [far_rows, last])
    txt_cols = columns(outs)
    img_kept, img_given = heads(True, spot, after(img_feat, outs[0], txt_feat), img_cols)
    img_taken = exchange(img_given, "lc", 1)
    txt_kept, txt_given = heads(False, spot, txt_feat, txt_cols)
    txt_taken = exchange(txt_given, "lc", 1)
    sums = mix(img_kept, img_taken, txt_kept, txt_taken)
    sums = lax.all_to_all(sums, ("ly", "lz", "dz"), 0, 0, tiled=True)
    grad_img, grad_txt, stats = final(count, sums)
    return grad_img, grad_txt, stats


def solution(mesh):
    split = Mesh(mesh.devices.reshape(4, 4, 2, 2, 4), ("ly", "lz", "lc", "dz", "dx"))
    dp = ("dz", "dx")
    return jax.shard_map(
        body,
        mesh=split,
        in_specs=(P(dp, LOSS, None), P(dp, LOSS, None), P(dp, LOSS), P(), P(), P(), P()),
        out_specs=(P(LOSS, dp), P(LOSS, dp), P()),
        check_vma=False,
    )
```

```python
import functools

import jax
import jax.numpy as jnp
from jax import lax
from jax.experimental import pallas as pl
from jax.experimental.pallas import tpu as pltpu
from jax.sharding import Mesh, PartitionSpec as P

EPSILON = 1e-06
LOSS = ("ly", "lz", "lc")
ROWS = 128
WIDTH = 1152
KEY_ROWS = 16
CHUNK = 36
SLOT = 40
COLS = 144
LANES = 128
TAIL = COLS - LANES
QUADS = 16
STATS = 112
DEPTH = 128
PIECES = WIDTH // DEPTH
SLAB = SLOT + 8
F32 = jnp.float32
BF16 = jnp.bfloat16

VMEM = pl.BlockSpec(memory_space=pltpu.VMEM)
SMEM = pl.BlockSpec(memory_space=pltpu.SMEM)


def params(megabytes):
    return pltpu.CompilerParams(vmem_limit_bytes=megabytes * 2**20)


def cost(flops, moved):
    return pl.CostEstimate(flops=flops, bytes_accessed=moved, transcendentals=0)


def exchange(array, axis, apart):
    return lax.ppermute(array, axis, [(i, i ^ apart) for i in range(lax.axis_size(axis))])


def after(array, *others):
    return lax.optimization_barrier((array, *others))[0]


def nt(a, b):
    return lax.dot_general(a, b, (((1,), (1,)), ((), ())), preferred_element_type=F32)


def mm(a, b):
    return jnp.dot(a, b, preferred_element_type=F32)


def project_kernel(x_hbm, w_hbm, key_hbm, out_ref, x, w, key, sems):
    copies = [
        pltpu.make_async_copy(x_hbm, x, sems.at[0]),
        pltpu.make_async_copy(key_hbm, key, sems.at[1]),
    ]
    for k in range(PIECES):
        span = pl.ds(k * DEPTH, DEPTH)
        copies.append(pltpu.make_async_copy(w_hbm.at[span], w.at[span], sems.at[2 + k]))
    for copy in copies:
        copy.start()
    copies[0].wait()
    u = jnp.zeros((ROWS, WIDTH), F32)
    for k in range(PIECES):
        copies[2 + k].wait()
        span = slice(k * DEPTH, (k + 1) * DEPTH)
        u += mm(x[:, span], w[span])
    copies[1].wait()
    write_payload(out_ref, u / lengths(u), key[...])


def lengths(u):
    return jnp.sqrt(jnp.sum(u * u, axis=1, keepdims=True) + EPSILON)


def project(x, w, keys):
    return pl.pallas_call(
        project_kernel,
        in_specs=[pl.BlockSpec(memory_space=pltpu.HBM)] * 3,
        out_specs=VMEM,
        out_shape=jax.ShapeDtypeStruct((ROWS + KEY_ROWS, WIDTH), BF16),
        scratch_shapes=[
            pltpu.VMEM((ROWS, WIDTH), BF16),
            pltpu.VMEM((WIDTH, WIDTH), BF16),
            pltpu.VMEM((1, ROWS), jnp.int32),
            pltpu.SemaphoreType.DMA((2 + PIECES,)),
        ],
        compiler_params=params(56),
        cost_estimate=cost(2 * ROWS * WIDTH * WIDTH, 4 * 2**20),
    )(x, w, keys)


def temperature(heat_log):
    return jnp.exp(jnp.full((1, 1), heat_log[0], F32))


def caption_row(block):
    digits = block[ROWS:, :LANES].astype(F32)
    return digits[0:1] * 128.0 + digits[1:2]


def add_tiles(with_stats, heat, shift, mine, key_col, pairs, total, sums):
    for block, key_row in pairs:
        vec = block[:ROWS, :]
        same = key_col == key_row
        sim = nt(mine, vec)
        logits = heat * sim + shift
        z = jnp.where(same, -logits, logits)
        t = jnp.exp(-jnp.abs(z))
        q = 1.0 / (1.0 + t)
        sig = jnp.where(z >= 0, q, t * q)
        g = jnp.where(same, -sig, sig) * (1.0 / ROWS)
        total += mm(g.astype(BF16), vec)
        if with_stats:
            new = (jnp.maximum(z, 0.0) + jnp.log1p(t), g * sim, g)
            sums = [old + add for old, add in zip(sums, new)]
    return total, sums


def pair_up(blocks, rows_ref):
    pairs = []
    for k, block in enumerate(blocks):
        key_row = caption_row(block)
        rows_ref[k] = jnp.broadcast_to(key_row, (8, LANES))
        pairs.append((block, key_row))
    return pairs


def write_payload(out_ref, unit, key):
    digit = jnp.broadcast_to(key, (KEY_ROWS, ROWS))
    row = lax.broadcasted_iota(jnp.int32, (KEY_ROWS, ROWS), 0)
    digit = jnp.where(row == 0, digit >> 7, jnp.where(row == 1, digit & 127, 0))
    out_ref[:ROWS, :] = unit.astype(BF16)
    out_ref[ROWS:, :] = jnp.zeros((KEY_ROWS, WIDTH), BF16)
    out_ref[ROWS:, :ROWS] = digit.astype(F32).astype(BF16)


def early_kernel(spot, heat_log, shift, xs, xt, ws_hbm, wt_hbm, key, *refs):
    *blocks, own, rows_ref, total_ref, unit_img, len_img, unit_txt, len_txt = refs[:-4]
    key_ref, sum_ref, w, sems = refs[-4:]
    copies = [
        pltpu.make_async_copy(ws_hbm, w.at[0], sems.at[0]),
        pltpu.make_async_copy(wt_hbm, w.at[1], sems.at[1]),
    ]
    for copy in copies:
        copy.start()
    key_col = jnp.broadcast_to(key[...].astype(F32), (ROWS, ROWS)).T
    key_ref[...] = key_col
    towers = ((xs, unit_img, len_img), (xt, unit_txt, len_txt))

    def norm(t):
        x, unit_ref, len_ref = towers[t]
        copies[t].wait()
        u = mm(x[...], w[t])
        length = lengths(u)
        unit_ref[...] = u / length
        len_ref[...] = jnp.broadcast_to(length, len_ref.shape)

    norm(0)
    own[...] = unit_img[...].astype(BF16)
    zero = jnp.zeros((ROWS, ROWS), F32)
    total, sums = add_tiles(
        True,
        temperature(heat_log),
        shift[0],
        own[...],
        key_col,
        pair_up(blocks, rows_ref),
        jnp.zeros((ROWS, WIDTH), F32),
        [zero] * 3,
    )
    total_ref[...] = total
    for k in range(3):
        sum_ref[k] = sums[k]
    norm(1)


def early(spot, scal, features, weights, keys, blocks):
    shapes = [(ROWS, WIDTH), (ROWS, LANES)]
    shapes = [(ROWS, WIDTH), *shapes, *shapes, (ROWS, ROWS), (3, ROWS, ROWS)]
    outs = [
        jax.ShapeDtypeStruct((ROWS, WIDTH), BF16),
        jax.ShapeDtypeStruct((len(blocks), 8, LANES), F32),
    ] + [jax.ShapeDtypeStruct(shape, F32) for shape in shapes]
    hbm = pl.BlockSpec(memory_space=pltpu.HBM)
    return pl.pallas_call(
        early_kernel,
        in_specs=[SMEM] * 3 + [VMEM] * 2 + [hbm] * 2 + [VMEM] * (1 + len(blocks)),
        out_specs=[VMEM] * len(outs),
        out_shape=outs,
        scratch_shapes=[pltpu.VMEM((2, WIDTH, WIDTH), BF16), pltpu.SemaphoreType.DMA((2,))],
        compiler_params=params(56),
        cost_estimate=cost(4 * 5 * ROWS * ROWS * WIDTH, 8 * 2**20),
    )(spot, *scal, *features, *weights, keys, *blocks)


def image_kernel(heat_log, shift, own, total_ref, key, acc, *refs):
    *blocks, out_ref, sum_ref, rows_ref = refs
    total, sums = add_tiles(
        True,
        temperature(heat_log),
        shift[0],
        own[...],
        key[...],
        pair_up(blocks, rows_ref),
        total_ref[...],
        [acc[k] for k in range(3)],
    )
    out_ref[...] = total
    for k in range(3):
        sum_ref[k] = sums[k]


def image_tiles(scal, own, total, key, acc, blocks):
    shapes = [(ROWS, WIDTH), (3, ROWS, ROWS), (len(blocks), 8, LANES)]
    return pl.pallas_call(
        image_kernel,
        in_specs=[SMEM] * 2 + [VMEM] * (4 + len(blocks)),
        out_specs=[VMEM] * 3,
        out_shape=[jax.ShapeDtypeStruct(shape, F32) for shape in shapes],
        compiler_params=params(56),
        cost_estimate=cost(4 * 3 * ROWS * ROWS * WIDTH, 4 * 2**20),
    )(*scal, own, total, key, acc, *blocks)


def middle_kernel(heat_log, shift, own, key, near_rows, far_rows, *refs):
    *blocks, total_ref = refs
    rows = [near_rows[0], near_rows[1], far_rows[0], far_rows[1], far_rows[2]]
    zero = jnp.zeros((ROWS, ROWS), F32)
    total, _ = add_tiles(
        False,
        temperature(heat_log),
        shift[0],
        own[:ROWS, :],
        key[...],
        [(block, row[0:1]) for block, row in zip(blocks, rows)],
        jnp.zeros((ROWS, WIDTH), F32),
        [zero] * 3,
    )
    total_ref[...] = total


def middle(scal, *arrays):
    return pl.pallas_call(
        middle_kernel,
        in_specs=[SMEM] * 2 + [VMEM] * len(arrays),
        out_specs=VMEM,
        out_shape=jax.ShapeDtypeStruct((ROWS, WIDTH), F32),
        compiler_params=params(56),
        cost_estimate=cost(4 * 5 * ROWS * ROWS * WIDTH, 4 * 2**20),
    )(*scal, *arrays)


def late_kernel(with_stats, ways, count, spot, heat_log, shift, own, *refs):
    total_ref, unit, length, key, acc, *refs = refs
    blocks, outs, held = refs[:count], refs[count:-1], refs[-1]
    heat = temperature(heat_log)
    if with_stats:
        *outs, rows_ref = outs
        pairs = pair_up(blocks, rows_ref)
    else:
        rows, block = blocks
        pairs = [(block, rows[0][0:1])]
    total, sums = add_tiles(
        with_stats,
        heat,
        shift[0],
        own[:ROWS, :],
        key[...],
        pairs,
        total_ref[...],
        [acc[k] for k in range(3)] if with_stats else [acc[...]] * 3,
    )
    total = total * heat
    u = unit[...]
    inner = jnp.sum(u * total, axis=1, keepdims=True)
    du = (total - u * inner) / length[:, :1]
    held[...] = du.T.astype(BF16).reshape(held.shape)
    if with_stats:
        def full(x):
            return jnp.sum(jnp.sum(x, axis=1, keepdims=True), axis=0, keepdims=True)

        lane = lax.broadcasted_iota(jnp.int32, (KEY_ROWS, LANES), 1)
        row = lax.broadcasted_iota(jnp.int32, (KEY_ROWS, LANES), 0)
        kind = lane % 3
        value = jnp.where(
            kind == 0,
            full(sums[0]) * (1.0 / ROWS),
            jnp.where(kind == 1, full(sums[1]) * heat, full(sums[2])),
        )
        value = jnp.where((row == 0) & (lane < 9), value, 0.0)
        high = value.astype(BF16).astype(F32)
        middle = (value - high).astype(BF16).astype(F32)
        low = value - high - middle
        parts = jnp.where(lane < 3, high, jnp.where(lane < 6, middle, low)).astype(BF16)
        for out in outs:
            out[2 * COLS :, :] = parts
    for step, out in enumerate(outs):
        w = lax.rem(spot[0] + step, ways)
        for h in range(2):
            out[h * COLS : (h + 1) * COLS, :] = held[h * ways + w]


def late(with_stats, ways, spot, scal, own, partial, blocks):
    rows = 2 * COLS + (KEY_ROWS if with_stats else 0)
    shapes = [jax.ShapeDtypeStruct((rows, ROWS), BF16)] * ways
    if with_stats:
        shapes.append(jax.ShapeDtypeStruct((len(blocks), 8, LANES), F32))
    return pl.pallas_call(
        functools.partial(late_kernel, with_stats, ways, len(blocks)),
        in_specs=[SMEM] * 3 + [VMEM] * (6 + len(blocks)),
        out_specs=[VMEM] * len(shapes),
        out_shape=shapes,
        scratch_shapes=[pltpu.VMEM((2 * ways, COLS, ROWS), BF16)],
        compiler_params=params(56),
        cost_estimate=cost(4 * 2 * ROWS * ROWS * WIDTH, 4 * 2**20),
    )(spot, *scal, own, *partial, *blocks)


def head_kernel(with_stats, spot, feat, *refs):
    spreads, (kept, given, held) = refs[:-3], refs[-3:]
    ways = len(spreads)
    total = jnp.zeros((2 * COLS, feat.shape[1]), F32)
    for step, spread in enumerate(spreads):
        source = lax.rem(spot[0] + ways - step, ways)
        rows = feat[pl.ds(pl.multiple_of(source * ROWS, ROWS), ROWS), :]
        total += mm(spread[: 2 * COLS, :], rows)
    spare = None
    if with_stats:
        parts = jnp.zeros((KEY_ROWS, LANES), F32)
        for spread in spreads:
            parts += spread[2 * COLS :, :].astype(F32)
        lane = lax.broadcasted_iota(jnp.int32, (8, LANES), 1)
        row = lax.broadcasted_iota(jnp.int32, (8, LANES), 0)
        place = lane - STATS
        summed = jnp.zeros((8, LANES), F32)
        for k in range(3):
            number = jnp.sum(
                jnp.where((lane[:1] % 3 == k) & (lane[:1] < 9), parts[0:1], 0.0),
                axis=1,
                keepdims=True,
            )
            summed = jnp.where(place % 3 == k, number, summed)
        value = jnp.where((row == spot[1]) & (place >= 0) & (place < 9), summed, 0.0)
        high = value.astype(BF16).astype(F32)
        middle = (value - high).astype(BF16).astype(F32)
        low = value - high - middle
        spare = jnp.where(place < 3, high, jnp.where(place < 6, middle, low))
    for h in range(2):
        main = total[h * COLS : h * COLS + LANES, :].T
        rest = total[h * COLS + LANES : (h + 1) * COLS, :]
        for m in range(QUADS):
            for side in range(2):
                start = (2 * m + side) * CHUNK
                target = held.at[side, 2 * m + h]
                target[:CHUNK, :] = main[start : start + CHUNK]
                target[CHUNK:SLOT, :] = jnp.zeros((SLOT - CHUNK, LANES), F32)
                target[SLOT:, :] = jnp.zeros((8, LANES), F32) if spare is None else spare
                for k in range(2):
                    target[SLOT:, 64 * k : 64 * k + CHUNK] = rest[
                        8 * k : 8 * k + 8, start : start + CHUNK
                    ]
    kept[...] = held[spot[1]]
    given[...] = held[1 - spot[1]].astype(BF16)


def heads(with_stats, spot, feat, spreads):
    shape = (2 * QUADS, SLOT + 8, LANES)
    return pl.pallas_call(
        functools.partial(head_kernel, with_stats),
        in_specs=[SMEM] + [VMEM] * (1 + len(spreads)),
        out_specs=[VMEM, VMEM],
        out_shape=[jax.ShapeDtypeStruct(shape, F32), jax.ShapeDtypeStruct(shape, BF16)],
        scratch_shapes=[pltpu.VMEM((2, *shape), F32)],
        compiler_params=params(24),
        cost_estimate=cost(2 * 4 * ROWS * 2 * COLS * feat.shape[1], 4 * 2**20),
    )(spot, feat, *spreads)


def mix_kernel(kept_img, taken_img, kept_txt, taken_txt, out):
    out[:, :SLAB, :] = (kept_img[...] + taken_img[...].astype(F32)).astype(BF16)
    out[:, SLAB:, :] = (kept_txt[...] + taken_txt[...].astype(F32)).astype(BF16)


def mix(*arrays):
    return pl.pallas_call(
        mix_kernel,
        in_specs=[VMEM] * 4,
        out_specs=VMEM,
        out_shape=jax.ShapeDtypeStruct((2 * QUADS, 2 * SLAB, LANES), BF16),
        compiler_params=params(16),
        cost_estimate=cost(4 * QUADS * SLAB * LANES, 2**20),
    )(*arrays)


def final_kernel(count, parts, out_img, out_txt, stats):
    both = jnp.sum(parts[...].astype(F32), axis=0)
    for out, total in ((out_img, both[:SLAB]), (out_txt, both[SLAB:])):
        out[:, :LANES] = total[:CHUNK]
        rest = total[SLOT:, :].T
        out[:, LANES : LANES + 8] = rest[:CHUNK]
        out[:, LANES + 8 :] = rest[64 : 64 + CHUNK]
    place = lax.broadcasted_iota(jnp.int32, (1, LANES), 1) - STATS
    row = both[SLOT : SLOT + 1] + both[SLOT + 1 : SLOT + 2]
    for k in range(3):
        chosen = jnp.where((place % 3 == k) & (place >= 0) & (place < 9), row, 0.0)
        stats[k] = jnp.sum(chosen) * (1.0 / count)


def final(count, parts):
    grad = jax.ShapeDtypeStruct((CHUNK, COLS), F32)
    return pl.pallas_call(
        functools.partial(final_kernel, count),
        in_specs=[VMEM],
        out_specs=[VMEM, VMEM, SMEM],
        out_shape=[grad, grad, jax.ShapeDtypeStruct((3,), F32)],
        compiler_params=params(8),
        cost_estimate=cost(4 * QUADS * SLAB * LANES, 2**20),
    )(parts)


def body(pictures, sentences, keys, picture_weights, sentence_weights, heat_log, shift_value):
    ways = lax.axis_size("dx")
    spot = jnp.stack([lax.axis_index(axis) for axis in ("dx", "lc")]).astype(jnp.int32)
    scal = (heat_log, shift_value)
    txt = project(sentences[0], sentence_weights, keys)
    txt_a = exchange(txt, "lz", 1)
    txt_y2 = exchange(txt, "ly", 2)
    txt_y1 = exchange(txt, "ly", 1)
    txt_c = exchange(txt, "lc", 1)
    img_feat = lax.all_gather(after(pictures[0], txt), "dx", axis=0, tiled=True)
    txt_feat = lax.all_gather(after(sentences[0], txt), "dx", axis=0, tiled=True)

    features = (pictures[0], sentences[0])
    weights = (picture_weights, sentence_weights)
    img, near_rows, *first = early(spot, scal, features, weights, keys, [txt, txt_c])
    txt_b = exchange(after(txt_a, txt_y1, txt_y2), "lz", 3)
    img_a = exchange(img, "lz", 1)
    img_c = exchange(after(img, txt_a, txt_y1, txt_y2), "lc", 1)
    total, acc, mid_rows = image_tiles(
        scal, img, first[0], first[5], first[6], [after(txt_y1, img_c), txt_y2, txt_a]
    )
    img_part = (total, *first[1:3], first[5], acc)
    img_n = after(img, img_c, acc)
    img_y2 = exchange(img_n, "ly", 2)
    img_y1 = exchange(img_n, "ly", 1)
    img_b = exchange(img_a, "lz", 3)

    count = 2 * QUADS * lax.axis_size("dz") * ways

    def turn(array, axis, step):
        size = lax.axis_size(axis)
        return lax.ppermute(array, axis, [(i, (i + step) % size) for i in range(size)])

    def columns(outs):
        return [outs[0]] + [turn(out, "dx", step) for step, out in enumerate(outs) if step]

    last = after(txt_b, img_feat, img_a, img_c)
    *img_outs, far_rows = late(
        True, ways, spot, scal, img, img_part, [last]
    )
    img_outs = list(lax.optimization_barrier((*img_outs, img_y1, img_y2))[:-2])
    img_cols = columns(img_outs)
    txt_total = middle(
        scal, txt, first[5], near_rows, mid_rows, img, img_c, img_y1, img_y2, img_a
    )
    txt_part = (txt_total, *first[3:5], first[5], first[5])
    last = after(img_b, *img_cols, txt_total)
    outs = late(False, ways, spot, scal, txt, txt_part, [far_rows, last])
    txt_cols = columns(outs)
    img_kept, img_given = heads(True, spot, after(img_feat, outs[0], txt_feat), img_cols)
    img_taken = exchange(img_given, "lc", 1)
    txt_kept, txt_given = heads(False, spot, txt_feat, txt_cols)
    txt_taken = exchange(txt_given, "lc", 1)
    sums = mix(img_kept, img_taken, txt_kept, txt_taken)
    sums = lax.all_to_all(sums, ("ly", "lz", "dz"), 0, 0, tiled=True)
    grad_img, grad_txt, stats = final(count, sums)
    return grad_img, grad_txt, stats


def solution(mesh):
    split = Mesh(mesh.devices.reshape(4, 4, 2, 2, 4), ("ly", "lz", "lc", "dz", "dx"))
    dp = ("dz", "dx")
    return jax.shard_map(
        body,
        mesh=split,
        in_specs=(P(dp, LOSS, None), P(dp, LOSS, None), P(dp, LOSS), P(), P(), P(), P()),
        out_specs=(P(LOSS, dp), P(LOSS, dp), P()),
        check_vma=False,
    )
```

```python
import functools

import jax
import jax.numpy as jnp
from jax import lax
from jax.experimental import pallas as pl
from jax.experimental.pallas import tpu as pltpu
from jax.sharding import Mesh, PartitionSpec as P

EPSILON = 1e-06
LOSS = ("ly", "lz", "lc")
ROWS = 128
WIDTH = 1152
KEY_ROWS = 16
CHUNK = 36
SLOT = 40
COLS = 144
LANES = 128
TAIL = COLS - LANES
QUADS = 16
STATS = 112
DEPTH = 128
PIECES = WIDTH // DEPTH
SLAB = SLOT + 8
F32 = jnp.float32
BF16 = jnp.bfloat16

VMEM = pl.BlockSpec(memory_space=pltpu.VMEM)
SMEM = pl.BlockSpec(memory_space=pltpu.SMEM)


def params(megabytes):
    return pltpu.CompilerParams(vmem_limit_bytes=megabytes * 2**20)


def cost(flops, moved):
    return pl.CostEstimate(flops=flops, bytes_accessed=moved, transcendentals=0)


def exchange(array, axis, apart):
    return lax.ppermute(array, axis, [(i, i ^ apart) for i in range(lax.axis_size(axis))])


def after(array, *others):
    return lax.optimization_barrier((array, *others))[0]


def nt(a, b):
    return lax.dot_general(a, b, (((1,), (1,)), ((), ())), preferred_element_type=F32)


def mm(a, b):
    return jnp.dot(a, b, preferred_element_type=F32)


def project_kernel(x_hbm, w_hbm, key_hbm, out_ref, x, w, key, sems):
    copies = [
        pltpu.make_async_copy(x_hbm, x, sems.at[0]),
        pltpu.make_async_copy(key_hbm, key, sems.at[1]),
    ]
    for k in range(PIECES):
        span = pl.ds(k * DEPTH, DEPTH)
        copies.append(pltpu.make_async_copy(w_hbm.at[span], w.at[span], sems.at[2 + k]))
    for copy in copies:
        copy.start()
    copies[0].wait()
    u = jnp.zeros((ROWS, WIDTH), F32)
    for k in range(PIECES):
        copies[2 + k].wait()
        span = slice(k * DEPTH, (k + 1) * DEPTH)
        u += mm(x[:, span], w[span])
    copies[1].wait()
    write_payload(out_ref, u / lengths(u), key[...])


def lengths(u):
    return jnp.sqrt(jnp.sum(u * u, axis=1, keepdims=True) + EPSILON)


def project(x, w, keys):
    return pl.pallas_call(
        project_kernel,
        in_specs=[pl.BlockSpec(memory_space=pltpu.HBM)] * 3,
        out_specs=VMEM,
        out_shape=jax.ShapeDtypeStruct((ROWS + KEY_ROWS, WIDTH), BF16),
        scratch_shapes=[
            pltpu.VMEM((ROWS, WIDTH), BF16),
            pltpu.VMEM((WIDTH, WIDTH), BF16),
            pltpu.VMEM((1, ROWS), jnp.int32),
            pltpu.SemaphoreType.DMA((2 + PIECES,)),
        ],
        compiler_params=params(56),
        cost_estimate=cost(2 * ROWS * WIDTH * WIDTH, 4 * 2**20),
    )(x, w, keys)


def temperature(heat_log):
    return jnp.exp(jnp.full((1, 1), heat_log[0], F32))


def caption_row(block):
    digits = block[ROWS:, :LANES].astype(F32)
    return digits[0:1] * 128.0 + digits[1:2]


def add_tiles(with_stats, heat, shift, mine, key_col, pairs, total, sums):
    for block, key_row in pairs:
        vec = block[:ROWS, :]
        same = key_col == key_row
        sim = nt(mine, vec)
        logits = heat * sim + shift
        z = jnp.where(same, -logits, logits)
        t = jnp.exp(-jnp.abs(z))
        q = 1.0 / (1.0 + t)
        sig = jnp.where(z >= 0, q, t * q)
        g = jnp.where(same, -sig, sig) * (1.0 / ROWS)
        total += mm(g.astype(BF16), vec)
        if with_stats:
            new = (jnp.maximum(z, 0.0) + jnp.log1p(t), g * sim, g)
            sums = [old + add for old, add in zip(sums, new)]
    return total, sums


def pair_up(blocks, rows_ref):
    pairs = []
    for k, block in enumerate(blocks):
        key_row = caption_row(block)
        rows_ref[k] = jnp.broadcast_to(key_row, (8, LANES))
        pairs.append((block, key_row))
    return pairs


def write_payload(out_ref, unit, key):
    digit = jnp.broadcast_to(key, (KEY_ROWS, ROWS))
    row = lax.broadcasted_iota(jnp.int32, (KEY_ROWS, ROWS), 0)
    digit = jnp.where(row == 0, digit >> 7, jnp.where(row == 1, digit & 127, 0))
    out_ref[:ROWS, :] = unit.astype(BF16)
    out_ref[ROWS:, :] = jnp.zeros((KEY_ROWS, WIDTH), BF16)
    out_ref[ROWS:, :ROWS] = digit.astype(F32).astype(BF16)


def early_kernel(spot, heat_log, shift, xs, xt, ws_hbm, wt_hbm, key, *refs):
    *blocks, own, rows_ref, total_ref, unit_img, len_img, unit_txt, len_txt = refs[:-4]
    key_ref, sum_ref, w, sems = refs[-4:]
    copies = [
        pltpu.make_async_copy(ws_hbm, w.at[0], sems.at[0]),
        pltpu.make_async_copy(wt_hbm, w.at[1], sems.at[1]),
    ]
    for copy in copies:
        copy.start()
    key_col = jnp.broadcast_to(key[...].astype(F32), (ROWS, ROWS)).T
    key_ref[...] = key_col
    towers = ((xs, unit_img, len_img), (xt, unit_txt, len_txt))

    def norm(t):
        x, unit_ref, len_ref = towers[t]
        copies[t].wait()
        u = mm(x[...], w[t])
        length = lengths(u)
        unit_ref[...] = u / length
        len_ref[...] = jnp.broadcast_to(length, len_ref.shape)

    norm(0)
    own[...] = unit_img[...].astype(BF16)
    zero = jnp.zeros((ROWS, ROWS), F32)
    total, sums = add_tiles(
        True,
        temperature(heat_log),
        shift[0],
        own[...],
        key_col,
        pair_up(blocks, rows_ref),
        jnp.zeros((ROWS, WIDTH), F32),
        [zero] * 3,
    )
    total_ref[...] = total
    for k in range(3):
        sum_ref[k] = sums[k]
    norm(1)


def early(spot, scal, features, weights, keys, blocks):
    shapes = [(ROWS, WIDTH), (ROWS, LANES)]
    shapes = [(ROWS, WIDTH), *shapes, *shapes, (ROWS, ROWS), (3, ROWS, ROWS)]
    outs = [
        jax.ShapeDtypeStruct((ROWS, WIDTH), BF16),
        jax.ShapeDtypeStruct((len(blocks), 8, LANES), F32),
    ] + [jax.ShapeDtypeStruct(shape, F32) for shape in shapes]
    hbm = pl.BlockSpec(memory_space=pltpu.HBM)
    return pl.pallas_call(
        early_kernel,
        in_specs=[SMEM] * 3 + [VMEM] * 2 + [hbm] * 2 + [VMEM] * (1 + len(blocks)),
        out_specs=[VMEM] * len(outs),
        out_shape=outs,
        scratch_shapes=[pltpu.VMEM((2, WIDTH, WIDTH), BF16), pltpu.SemaphoreType.DMA((2,))],
        compiler_params=params(56),
        cost_estimate=cost(4 * 5 * ROWS * ROWS * WIDTH, 8 * 2**20),
    )(spot, *scal, *features, *weights, keys, *blocks)


def image_kernel(heat_log, shift, own, total_ref, key, acc, *refs):
    *blocks, out_ref, sum_ref, rows_ref = refs
    total, sums = add_tiles(
        True,
        temperature(heat_log),
        shift[0],
        own[...],
        key[...],
        pair_up(blocks, rows_ref),
        total_ref[...],
        [acc[k] for k in range(3)],
    )
    out_ref[...] = total
    for k in range(3):
        sum_ref[k] = sums[k]


def image_tiles(scal, own, total, key, acc, blocks):
    shapes = [(ROWS, WIDTH), (3, ROWS, ROWS), (len(blocks), 8, LANES)]
    return pl.pallas_call(
        image_kernel,
        in_specs=[SMEM] * 2 + [VMEM] * (4 + len(blocks)),
        out_specs=[VMEM] * 3,
        out_shape=[jax.ShapeDtypeStruct(shape, F32) for shape in shapes],
        compiler_params=params(56),
        cost_estimate=cost(4 * 3 * ROWS * ROWS * WIDTH, 4 * 2**20),
    )(*scal, own, total, key, acc, *blocks)


def middle_kernel(heat_log, shift, own, key, near_rows, far_rows, *refs):
    *blocks, total_ref = refs
    rows = [near_rows[0], near_rows[1], far_rows[0], far_rows[1], far_rows[2]]
    zero = jnp.zeros((ROWS, ROWS), F32)
    total, _ = add_tiles(
        False,
        temperature(heat_log),
        shift[0],
        own[:ROWS, :],
        key[...],
        [(block, row[0:1]) for block, row in zip(blocks, rows)],
        jnp.zeros((ROWS, WIDTH), F32),
        [zero] * 3,
    )
    total_ref[...] = total


def middle(scal, *arrays):
    return pl.pallas_call(
        middle_kernel,
        in_specs=[SMEM] * 2 + [VMEM] * len(arrays),
        out_specs=VMEM,
        out_shape=jax.ShapeDtypeStruct((ROWS, WIDTH), F32),
        compiler_params=params(56),
        cost_estimate=cost(4 * 5 * ROWS * ROWS * WIDTH, 4 * 2**20),
    )(*scal, *arrays)


def late_kernel(with_stats, ways, count, spot, heat_log, shift, own, *refs):
    total_ref, unit, length, key, acc, *refs = refs
    blocks, outs, held = refs[:count], refs[count:-1], refs[-1]
    heat = temperature(heat_log)
    if with_stats:
        *outs, rows_ref = outs
        pairs = pair_up(blocks, rows_ref)
    else:
        rows, block = blocks
        pairs = [(block, rows[0][0:1])]
    total, sums = add_tiles(
        with_stats,
        heat,
        shift[0],
        own[:ROWS, :],
        key[...],
        pairs,
        total_ref[...],
        [acc[k] for k in range(3)] if with_stats else [acc[...]] * 3,
    )
    total = total * heat
    u = unit[...]
    inner = jnp.sum(u * total, axis=1, keepdims=True)
    du = (total - u * inner) / length[:, :1]
    held[...] = du.T.astype(BF16).reshape(held.shape)
    if with_stats:
        def full(x):
            return jnp.sum(jnp.sum(x, axis=1, keepdims=True), axis=0, keepdims=True)

        lane = lax.broadcasted_iota(jnp.int32, (KEY_ROWS, LANES), 1)
        row = lax.broadcasted_iota(jnp.int32, (KEY_ROWS, LANES), 0)
        kind = lane % 3
        value = jnp.where(
            kind == 0,
            full(sums[0]) * (1.0 / ROWS),
            jnp.where(kind == 1, full(sums[1]) * heat, full(sums[2])),
        )
        value = jnp.where((row == 0) & (lane < 9), value, 0.0)
        high = value.astype(BF16).astype(F32)
        middle = (value - high).astype(BF16).astype(F32)
        low = value - high - middle
        parts = jnp.where(lane < 3, high, jnp.where(lane < 6, middle, low)).astype(BF16)
        for out in outs:
            out[2 * COLS :, :] = parts
    for step, out in enumerate(outs):
        w = lax.rem(spot[0] + step, ways)
        for h in range(2):
            out[h * COLS : (h + 1) * COLS, :] = held[h * ways + w]


def late(with_stats, ways, spot, scal, own, partial, blocks):
    rows = 2 * COLS + (KEY_ROWS if with_stats else 0)
    shapes = [jax.ShapeDtypeStruct((rows, ROWS), BF16)] * ways
    if with_stats:
        shapes.append(jax.ShapeDtypeStruct((len(blocks), 8, LANES), F32))
    return pl.pallas_call(
        functools.partial(late_kernel, with_stats, ways, len(blocks)),
        in_specs=[SMEM] * 3 + [VMEM] * (6 + len(blocks)),
        out_specs=[VMEM] * len(shapes),
        out_shape=shapes,
        scratch_shapes=[pltpu.VMEM((2 * ways, COLS, ROWS), BF16)],
        compiler_params=params(56),
        cost_estimate=cost(4 * 2 * ROWS * ROWS * WIDTH, 4 * 2**20),
    )(spot, *scal, own, *partial, *blocks)


def head_kernel(with_stats, spot, feat, *refs):
    spreads, (kept, given, held) = refs[:-3], refs[-3:]
    ways = len(spreads)
    total = jnp.zeros((2 * COLS, feat.shape[1]), F32)
    for step, spread in enumerate(spreads):
        source = lax.rem(spot[0] + ways - step, ways)
        rows = feat[pl.ds(pl.multiple_of(source * ROWS, ROWS), ROWS), :]
        total += mm(spread[: 2 * COLS, :], rows)
    spare = None
    if with_stats:
        parts = jnp.zeros((KEY_ROWS, LANES), F32)
        for spread in spreads:
            parts += spread[2 * COLS :, :].astype(F32)
        lane = lax.broadcasted_iota(jnp.int32, (8, LANES), 1)
        row = lax.broadcasted_iota(jnp.int32, (8, LANES), 0)
        place = lane - STATS
        summed = jnp.zeros((8, LANES), F32)
        for k in range(3):
            number = jnp.sum(
                jnp.where((lane[:1] % 3 == k) & (lane[:1] < 9), parts[0:1], 0.0),
                axis=1,
                keepdims=True,
            )
            summed = jnp.where(place % 3 == k, number, summed)
        value = jnp.where((row == spot[1]) & (place >= 0) & (place < 9), summed, 0.0)
        high = value.astype(BF16).astype(F32)
        middle = (value - high).astype(BF16).astype(F32)
        low = value - high - middle
        spare = jnp.where(place < 3, high, jnp.where(place < 6, middle, low))
    for h in range(2):
        main = total[h * COLS : h * COLS + LANES, :].T
        rest = total[h * COLS + LANES : (h + 1) * COLS, :]
        for m in range(QUADS):
            for side in range(2):
                start = (2 * m + side) * CHUNK
                target = held.at[side, 2 * m + h]
                target[:CHUNK, :] = main[start : start + CHUNK]
                target[CHUNK:SLOT, :] = jnp.zeros((SLOT - CHUNK, LANES), F32)
                target[SLOT:, :] = jnp.zeros((8, LANES), F32) if spare is None else spare
                for k in range(2):
                    target[SLOT:, 64 * k : 64 * k + CHUNK] = rest[
                        8 * k : 8 * k + 8, start : start + CHUNK
                    ]
    kept[...] = held[spot[1]]
    given[...] = held[1 - spot[1]].astype(BF16)


def heads(with_stats, spot, feat, spreads):
    shape = (2 * QUADS, SLOT + 8, LANES)
    return pl.pallas_call(
        functools.partial(head_kernel, with_stats),
        in_specs=[SMEM] + [VMEM] * (1 + len(spreads)),
        out_specs=[VMEM, VMEM],
        out_shape=[jax.ShapeDtypeStruct(shape, F32), jax.ShapeDtypeStruct(shape, BF16)],
        scratch_shapes=[pltpu.VMEM((2, *shape), F32)],
        compiler_params=params(24),
        cost_estimate=cost(2 * 4 * ROWS * 2 * COLS * feat.shape[1], 4 * 2**20),
    )(spot, feat, *spreads)


def mix_kernel(kept_img, taken_img, kept_txt, taken_txt, out):
    out[:, :SLAB, :] = (kept_img[...] + taken_img[...].astype(F32)).astype(BF16)
    out[:, SLAB:, :] = (kept_txt[...] + taken_txt[...].astype(F32)).astype(BF16)


def mix(*arrays):
    return pl.pallas_call(
        mix_kernel,
        in_specs=[VMEM] * 4,
        out_specs=VMEM,
        out_shape=jax.ShapeDtypeStruct((2 * QUADS, 2 * SLAB, LANES), BF16),
        compiler_params=params(16),
        cost_estimate=cost(4 * QUADS * SLAB * LANES, 2**20),
    )(*arrays)


def final_kernel(count, parts, out_img, out_txt, stats):
    both = jnp.sum(parts[...].astype(F32), axis=0)
    for out, total in ((out_img, both[:SLAB]), (out_txt, both[SLAB:])):
        out[:, :LANES] = total[:CHUNK]
        rest = total[SLOT:, :].T
        out[:, LANES : LANES + 8] = rest[:CHUNK]
        out[:, LANES + 8 :] = rest[64 : 64 + CHUNK]
    place = lax.broadcasted_iota(jnp.int32, (1, LANES), 1) - STATS
    row = both[SLOT : SLOT + 1] + both[SLOT + 1 : SLOT + 2]
    for k in range(3):
        chosen = jnp.where((place % 3 == k) & (place >= 0) & (place < 9), row, 0.0)
        stats[k] = jnp.sum(chosen) * (1.0 / count)


def final(count, parts):
    grad = jax.ShapeDtypeStruct((CHUNK, COLS), F32)
    return pl.pallas_call(
        functools.partial(final_kernel, count),
        in_specs=[VMEM],
        out_specs=[VMEM, VMEM, SMEM],
        out_shape=[grad, grad, jax.ShapeDtypeStruct((3,), F32)],
        compiler_params=params(8),
        cost_estimate=cost(4 * QUADS * SLAB * LANES, 2**20),
    )(parts)


def body(pictures, sentences, keys, picture_weights, sentence_weights, heat_log, shift_value):
    ways = lax.axis_size("dx")
    spot = jnp.stack([lax.axis_index(axis) for axis in ("dx", "lc")]).astype(jnp.int32)
    scal = (heat_log, shift_value)
    txt = project(sentences[0], sentence_weights, keys)
    txt_a = exchange(txt, "lz", 1)
    txt_y2 = exchange(txt, "ly", 2)
    txt_y1 = exchange(txt, "ly", 1)
    txt_c = exchange(txt, "lc", 1)
    img_feat = lax.all_gather(after(pictures[0], txt), "dx", axis=0, tiled=True)
    txt_feat = lax.all_gather(after(sentences[0], txt), "dx", axis=0, tiled=True)

    features = (pictures[0], sentences[0])
    weights = (picture_weights, sentence_weights)
    img, near_rows, *first = early(spot, scal, features, weights, keys, [txt, txt_c])
    txt_b = exchange(after(txt_a, txt_y1, txt_y2), "lz", 3)
    img_a = exchange(img, "lz", 1)
    img_c = exchange(after(img, txt_a, txt_y1, txt_y2), "lc", 1)
    total, acc, mid_rows = image_tiles(
        scal, img, first[0], first[5], first[6], [after(txt_y1, img_c), txt_y2, txt_a]
    )
    img_part = (total, *first[1:3], first[5], acc)
    img_n = after(img, img_c, acc)
    img_y2 = exchange(img_n, "ly", 2)
    img_y1 = exchange(img_n, "ly", 1)
    img_b = exchange(img_a, "lz", 3)

    count = 2 * QUADS * lax.axis_size("dz") * ways

    def turn(array, axis, step):
        size = lax.axis_size(axis)
        return lax.ppermute(array, axis, [(i, (i + step) % size) for i in range(size)])

    def columns(outs):
        return [outs[0]] + [turn(out, "dx", step) for step, out in enumerate(outs) if step]

    last = after(txt_b, img_feat, img_a, img_c)
    *img_outs, far_rows = late(
        True, ways, spot, scal, img, img_part, [last]
    )
    img_outs = list(lax.optimization_barrier((*img_outs, img_y1, img_y2))[:-2])
    img_cols = columns(img_outs)
    txt_total = middle(
        scal, txt, first[5], near_rows, mid_rows, img, img_c, img_y1, img_y2, img_a
    )
    txt_part = (txt_total, *first[3:5], first[5], first[5])
    last = after(img_b, img_cols[1], img_cols[3], txt_total)
    outs = late(False, ways, spot, scal, txt, txt_part, [far_rows, last])
    txt_cols = columns(outs)
    img_kept, img_given = heads(True, spot, after(img_feat, outs[0], txt_feat), img_cols)
    img_taken = exchange(img_given, "lc", 1)
    txt_kept, txt_given = heads(False, spot, txt_feat, txt_cols)
    txt_taken = exchange(txt_given, "lc", 1)
    sums = mix(img_kept, img_taken, txt_kept, txt_taken)
    sums = lax.all_to_all(sums, ("ly", "lz", "dz"), 0, 0, tiled=True)
    grad_img, grad_txt, stats = final(count, sums)
    return grad_img, grad_txt, stats


def solution(mesh):
    split = Mesh(mesh.devices.reshape(4, 4, 2, 2, 4), ("ly", "lz", "lc", "dz", "dx"))
    dp = ("dz", "dx")
    return jax.shard_map(
        body,
        mesh=split,
        in_specs=(P(dp, LOSS, None), P(dp, LOSS, None), P(dp, LOSS), P(), P(), P(), P()),
        out_specs=(P(LOSS, dp), P(LOSS, dp), P()),
        check_vma=False,
    )
```

```python
import functools

import jax
import jax.numpy as jnp
from jax import lax
from jax.experimental import pallas as pl
from jax.experimental.pallas import tpu as pltpu
from jax.sharding import Mesh, PartitionSpec as P

EPSILON = 1e-06
LOSS = ("ly", "lz", "lc")
ROWS = 128
WIDTH = 1152
KEY_ROWS = 16
CHUNK = 36
SLOT = 40
COLS = 144
LANES = 128
TAIL = COLS - LANES
QUADS = 16
STATS = 112
DEPTH = 128
PIECES = WIDTH // DEPTH
SLAB = SLOT + 8
F32 = jnp.float32
BF16 = jnp.bfloat16

VMEM = pl.BlockSpec(memory_space=pltpu.VMEM)
SMEM = pl.BlockSpec(memory_space=pltpu.SMEM)


def params(megabytes):
    return pltpu.CompilerParams(vmem_limit_bytes=megabytes * 2**20)


def cost(flops, moved):
    return pl.CostEstimate(flops=flops, bytes_accessed=moved, transcendentals=0)


def exchange(array, axis, apart):
    return lax.ppermute(array, axis, [(i, i ^ apart) for i in range(lax.axis_size(axis))])


def after(array, *others):
    return lax.optimization_barrier((array, *others))[0]


def nt(a, b):
    return lax.dot_general(a, b, (((1,), (1,)), ((), ())), preferred_element_type=F32)


def mm(a, b):
    return jnp.dot(a, b, preferred_element_type=F32)


def project_kernel(x_hbm, w_hbm, key_hbm, out_ref, x, w, key, sems):
    copies = [
        pltpu.make_async_copy(x_hbm, x, sems.at[0]),
        pltpu.make_async_copy(key_hbm, key, sems.at[1]),
    ]
    for k in range(PIECES):
        span = pl.ds(k * DEPTH, DEPTH)
        copies.append(pltpu.make_async_copy(w_hbm.at[span], w.at[span], sems.at[2 + k]))
    for copy in copies:
        copy.start()
    copies[0].wait()
    u = jnp.zeros((ROWS, WIDTH), F32)
    for k in range(PIECES):
        copies[2 + k].wait()
        span = slice(k * DEPTH, (k + 1) * DEPTH)
        u += mm(x[:, span], w[span])
    copies[1].wait()
    write_payload(out_ref, u / lengths(u), key[...])


def lengths(u):
    return jnp.sqrt(jnp.sum(u * u, axis=1, keepdims=True) + EPSILON)


def project(x, w, keys):
    return pl.pallas_call(
        project_kernel,
        in_specs=[pl.BlockSpec(memory_space=pltpu.HBM)] * 3,
        out_specs=VMEM,
        out_shape=jax.ShapeDtypeStruct((ROWS + KEY_ROWS, WIDTH), BF16),
        scratch_shapes=[
            pltpu.VMEM((ROWS, WIDTH), BF16),
            pltpu.VMEM((WIDTH, WIDTH), BF16),
            pltpu.VMEM((1, ROWS), jnp.int32),
            pltpu.SemaphoreType.DMA((2 + PIECES,)),
        ],
        compiler_params=params(56),
        cost_estimate=cost(2 * ROWS * WIDTH * WIDTH, 4 * 2**20),
    )(x, w, keys)


def temperature(heat_log):
    return jnp.exp(jnp.full((1, 1), heat_log[0], F32))


def caption_row(block):
    digits = block[ROWS:, :LANES].astype(F32)
    return digits[0:1] * 128.0 + digits[1:2]


def add_tiles(with_stats, heat, shift, mine, key_col, pairs, total, sums):
    for block, key_row in pairs:
        vec = block[:ROWS, :]
        same = key_col == key_row
        sim = nt(mine, vec)
        logits = heat * sim + shift
        z = jnp.where(same, -logits, logits)
        t = jnp.exp(-jnp.abs(z))
        q = 1.0 / (1.0 + t)
        sig = jnp.where(z >= 0, q, t * q)
        g = jnp.where(same, -sig, sig) * (1.0 / ROWS)
        total += mm(g.astype(BF16), vec)
        if with_stats:
            new = (jnp.maximum(z, 0.0) + jnp.log1p(t), g * sim, g)
            sums = [old + add for old, add in zip(sums, new)]
    return total, sums


def pair_up(blocks, rows_ref):
    pairs = []
    for k, block in enumerate(blocks):
        key_row = caption_row(block)
        rows_ref[k] = jnp.broadcast_to(key_row, (8, LANES))
        pairs.append((block, key_row))
    return pairs


def write_payload(out_ref, unit, key):
    digit = jnp.broadcast_to(key, (KEY_ROWS, ROWS))
    row = lax.broadcasted_iota(jnp.int32, (KEY_ROWS, ROWS), 0)
    digit = jnp.where(row == 0, digit >> 7, jnp.where(row == 1, digit & 127, 0))
    out_ref[:ROWS, :] = unit.astype(BF16)
    out_ref[ROWS:, :] = jnp.zeros((KEY_ROWS, WIDTH), BF16)
    out_ref[ROWS:, :ROWS] = digit.astype(F32).astype(BF16)


def early_kernel(spot, heat_log, shift, xs, xt, ws_hbm, wt_hbm, key, *refs):
    *blocks, own, rows_ref, total_ref, unit_img, len_img, unit_txt, len_txt = refs[:-4]
    key_ref, sum_ref, w, sems = refs[-4:]
    copies = [
        pltpu.make_async_copy(ws_hbm, w.at[0], sems.at[0]),
        pltpu.make_async_copy(wt_hbm, w.at[1], sems.at[1]),
    ]
    for copy in copies:
        copy.start()
    key_col = jnp.broadcast_to(key[...].astype(F32), (ROWS, ROWS)).T
    key_ref[...] = key_col
    towers = ((xs, unit_img, len_img), (xt, unit_txt, len_txt))

    def norm(t):
        x, unit_ref, len_ref = towers[t]
        copies[t].wait()
        u = mm(x[...], w[t])
        length = lengths(u)
        unit_ref[...] = u / length
        len_ref[...] = jnp.broadcast_to(length, len_ref.shape)

    norm(0)
    own[...] = unit_img[...].astype(BF16)
    zero = jnp.zeros((ROWS, ROWS), F32)
    total, sums = add_tiles(
        True,
        temperature(heat_log),
        shift[0],
        own[...],
        key_col,
        pair_up(blocks, rows_ref),
        jnp.zeros((ROWS, WIDTH), F32),
        [zero] * 3,
    )
    total_ref[...] = total
    for k in range(3):
        sum_ref[k] = sums[k]
    norm(1)


def early(spot, scal, features, weights, keys, blocks):
    shapes = [(ROWS, WIDTH), (ROWS, LANES)]
    shapes = [(ROWS, WIDTH), *shapes, *shapes, (ROWS, ROWS), (3, ROWS, ROWS)]
    outs = [
        jax.ShapeDtypeStruct((ROWS, WIDTH), BF16),
        jax.ShapeDtypeStruct((len(blocks), 8, LANES), F32),
    ] + [jax.ShapeDtypeStruct(shape, F32) for shape in shapes]
    hbm = pl.BlockSpec(memory_space=pltpu.HBM)
    return pl.pallas_call(
        early_kernel,
        in_specs=[SMEM] * 3 + [VMEM] * 2 + [hbm] * 2 + [VMEM] * (1 + len(blocks)),
        out_specs=[VMEM] * len(outs),
        out_shape=outs,
        scratch_shapes=[pltpu.VMEM((2, WIDTH, WIDTH), BF16), pltpu.SemaphoreType.DMA((2,))],
        compiler_params=params(56),
        cost_estimate=cost(4 * 5 * ROWS * ROWS * WIDTH, 8 * 2**20),
    )(spot, *scal, *features, *weights, keys, *blocks)


def image_kernel(heat_log, shift, own, total_ref, key, acc, *refs):
    *blocks, out_ref, sum_ref, rows_ref = refs
    total, sums = add_tiles(
        True,
        temperature(heat_log),
        shift[0],
        own[...],
        key[...],
        pair_up(blocks, rows_ref),
        total_ref[...],
        [acc[k] for k in range(3)],
    )
    out_ref[...] = total
    for k in range(3):
        sum_ref[k] = sums[k]


def image_tiles(scal, own, total, key, acc, blocks):
    shapes = [(ROWS, WIDTH), (3, ROWS, ROWS), (len(blocks), 8, LANES)]
    return pl.pallas_call(
        image_kernel,
        in_specs=[SMEM] * 2 + [VMEM] * (4 + len(blocks)),
        out_specs=[VMEM] * 3,
        out_shape=[jax.ShapeDtypeStruct(shape, F32) for shape in shapes],
        compiler_params=params(56),
        cost_estimate=cost(4 * 3 * ROWS * ROWS * WIDTH, 4 * 2**20),
    )(*scal, own, total, key, acc, *blocks)


def middle_kernel(heat_log, shift, own, key, near_rows, far_rows, *refs):
    *blocks, total_ref = refs
    rows = [near_rows[0], near_rows[1], far_rows[0], far_rows[1], far_rows[2]]
    zero = jnp.zeros((ROWS, ROWS), F32)
    total, _ = add_tiles(
        False,
        temperature(heat_log),
        shift[0],
        own[:ROWS, :],
        key[...],
        [(block, row[0:1]) for block, row in zip(blocks, rows)],
        jnp.zeros((ROWS, WIDTH), F32),
        [zero] * 3,
    )
    total_ref[...] = total


def middle(scal, *arrays):
    return pl.pallas_call(
        middle_kernel,
        in_specs=[SMEM] * 2 + [VMEM] * len(arrays),
        out_specs=VMEM,
        out_shape=jax.ShapeDtypeStruct((ROWS, WIDTH), F32),
        compiler_params=params(56),
        cost_estimate=cost(4 * 5 * ROWS * ROWS * WIDTH, 4 * 2**20),
    )(*scal, *arrays)


def late_kernel(with_stats, ways, count, spot, heat_log, shift, own, *refs):
    total_ref, unit, length, key, acc, *refs = refs
    blocks, outs, held = refs[:count], refs[count:-1], refs[-1]
    heat = temperature(heat_log)
    if with_stats:
        *outs, rows_ref = outs
        pairs = pair_up(blocks, rows_ref)
    else:
        rows, block = blocks
        pairs = [(block, rows[0][0:1])]
    total, sums = add_tiles(
        with_stats,
        heat,
        shift[0],
        own[:ROWS, :],
        key[...],
        pairs,
        total_ref[...],
        [acc[k] for k in range(3)] if with_stats else [acc[...]] * 3,
    )
    total = total * heat
    u = unit[...]
    inner = jnp.sum(u * total, axis=1, keepdims=True)
    du = (total - u * inner) / length[:, :1]
    held[...] = du.T.astype(BF16).reshape(held.shape)
    if with_stats:
        def full(x):
            return jnp.sum(jnp.sum(x, axis=1, keepdims=True), axis=0, keepdims=True)

        lane = lax.broadcasted_iota(jnp.int32, (KEY_ROWS, LANES), 1)
        row = lax.broadcasted_iota(jnp.int32, (KEY_ROWS, LANES), 0)
        kind = lane % 3
        value = jnp.where(
            kind == 0,
            full(sums[0]) * (1.0 / ROWS),
            jnp.where(kind == 1, full(sums[1]) * heat, full(sums[2])),
        )
        value = jnp.where((row == 0) & (lane < 9), value, 0.0)
        high = value.astype(BF16).astype(F32)
        middle = (value - high).astype(BF16).astype(F32)
        low = value - high - middle
        parts = jnp.where(lane < 3, high, jnp.where(lane < 6, middle, low)).astype(BF16)
        for out in outs:
            out[2 * COLS :, :] = parts
    for step, out in enumerate(outs):
        w = lax.rem(spot[0] + step, ways)
        for h in range(2):
            out[h * COLS : (h + 1) * COLS, :] = held[h * ways + w]


def late(with_stats, ways, spot, scal, own, partial, blocks):
    rows = 2 * COLS + (KEY_ROWS if with_stats else 0)
    shapes = [jax.ShapeDtypeStruct((rows, ROWS), BF16)] * ways
    if with_stats:
        shapes.append(jax.ShapeDtypeStruct((len(blocks), 8, LANES), F32))
    return pl.pallas_call(
        functools.partial(late_kernel, with_stats, ways, len(blocks)),
        in_specs=[SMEM] * 3 + [VMEM] * (6 + len(blocks)),
        out_specs=[VMEM] * len(shapes),
        out_shape=shapes,
        scratch_shapes=[pltpu.VMEM((2 * ways, COLS, ROWS), BF16)],
        compiler_params=params(56),
        cost_estimate=cost(4 * 2 * ROWS * ROWS * WIDTH, 4 * 2**20),
    )(spot, *scal, own, *partial, *blocks)


def head_kernel(with_stats, spot, feat, *refs):
    spreads, (kept, given, held) = refs[:-3], refs[-3:]
    ways = len(spreads)
    total = jnp.zeros((2 * COLS, feat.shape[1]), F32)
    for step, spread in enumerate(spreads):
        source = lax.rem(spot[0] + ways - step, ways)
        rows = feat[pl.ds(pl.multiple_of(source * ROWS, ROWS), ROWS), :]
        total += mm(spread[: 2 * COLS, :], rows)
    spare = None
    if with_stats:
        parts = jnp.zeros((KEY_ROWS, LANES), F32)
        for spread in spreads:
            parts += spread[2 * COLS :, :].astype(F32)
        lane = lax.broadcasted_iota(jnp.int32, (8, LANES), 1)
        row = lax.broadcasted_iota(jnp.int32, (8, LANES), 0)
        place = lane - STATS
        summed = jnp.zeros((8, LANES), F32)
        for k in range(3):
            number = jnp.sum(
                jnp.where((lane[:1] % 3 == k) & (lane[:1] < 9), parts[0:1], 0.0),
                axis=1,
                keepdims=True,
            )
            summed = jnp.where(place % 3 == k, number, summed)
        value = jnp.where((row == spot[1]) & (place >= 0) & (place < 9), summed, 0.0)
        high = value.astype(BF16).astype(F32)
        middle = (value - high).astype(BF16).astype(F32)
        low = value - high - middle
        spare = jnp.where(place < 3, high, jnp.where(place < 6, middle, low))
    for h in range(2):
        main = total[h * COLS : h * COLS + LANES, :].T
        rest = total[h * COLS + LANES : (h + 1) * COLS, :]
        for m in range(QUADS):
            for side in range(2):
                start = (2 * m + side) * CHUNK
                target = held.at[side, 2 * m + h]
                target[:CHUNK, :] = main[start : start + CHUNK]
                target[CHUNK:SLOT, :] = jnp.zeros((SLOT - CHUNK, LANES), F32)
                target[SLOT:, :] = jnp.zeros((8, LANES), F32) if spare is None else spare
                for k in range(2):
                    target[SLOT:, 64 * k : 64 * k + CHUNK] = rest[
                        8 * k : 8 * k + 8, start : start + CHUNK
                    ]
    kept[...] = held[spot[1]]
    given[...] = held[1 - spot[1]].astype(BF16)


def heads(with_stats, spot, feat, spreads):
    shape = (2 * QUADS, SLOT + 8, LANES)
    return pl.pallas_call(
        functools.partial(head_kernel, with_stats),
        in_specs=[SMEM] + [VMEM] * (1 + len(spreads)),
        out_specs=[VMEM, VMEM],
        out_shape=[jax.ShapeDtypeStruct(shape, F32), jax.ShapeDtypeStruct(shape, BF16)],
        scratch_shapes=[pltpu.VMEM((2, *shape), F32)],
        compiler_params=params(24),
        cost_estimate=cost(2 * 4 * ROWS * 2 * COLS * feat.shape[1], 4 * 2**20),
    )(spot, feat, *spreads)


def mix_kernel(kept_img, taken_img, kept_txt, taken_txt, out):
    out[:, :SLAB, :] = (kept_img[...] + taken_img[...].astype(F32)).astype(BF16)
    out[:, SLAB:, :] = (kept_txt[...] + taken_txt[...].astype(F32)).astype(BF16)


def mix(*arrays):
    return pl.pallas_call(
        mix_kernel,
        in_specs=[VMEM] * 4,
        out_specs=VMEM,
        out_shape=jax.ShapeDtypeStruct((2 * QUADS, 2 * SLAB, LANES), BF16),
        compiler_params=params(16),
        cost_estimate=cost(4 * QUADS * SLAB * LANES, 2**20),
    )(*arrays)


def final_kernel(count, parts, out_img, out_txt, stats):
    both = jnp.sum(parts[...].astype(F32), axis=0)
    for out, total in ((out_img, both[:SLAB]), (out_txt, both[SLAB:])):
        out[:, :LANES] = total[:CHUNK]
        rest = total[SLOT:, :].T
        out[:, LANES : LANES + 8] = rest[:CHUNK]
        out[:, LANES + 8 :] = rest[64 : 64 + CHUNK]
    place = lax.broadcasted_iota(jnp.int32, (1, LANES), 1) - STATS
    row = both[SLOT : SLOT + 1] + both[SLOT + 1 : SLOT + 2]
    for k in range(3):
        chosen = jnp.where((place % 3 == k) & (place >= 0) & (place < 9), row, 0.0)
        stats[k] = jnp.sum(chosen) * (1.0 / count)


def final(count, parts):
    grad = jax.ShapeDtypeStruct((CHUNK, COLS), F32)
    return pl.pallas_call(
        functools.partial(final_kernel, count),
        in_specs=[VMEM],
        out_specs=[VMEM, VMEM, SMEM],
        out_shape=[grad, grad, jax.ShapeDtypeStruct((3,), F32)],
        compiler_params=params(8),
        cost_estimate=cost(4 * QUADS * SLAB * LANES, 2**20),
    )(parts)


def body(pictures, sentences, keys, picture_weights, sentence_weights, heat_log, shift_value):
    ways = lax.axis_size("dx")
    spot = jnp.stack([lax.axis_index(axis) for axis in ("dx", "lc")]).astype(jnp.int32)
    scal = (heat_log, shift_value)
    txt = project(sentences[0], sentence_weights, keys)
    txt_a = exchange(txt, "lz", 1)
    txt_y2 = exchange(txt, "ly", 2)
    txt_y1 = exchange(txt, "ly", 1)
    txt_c = exchange(txt, "lc", 1)
    img_feat = lax.all_gather(after(pictures[0], txt), "dx", axis=0, tiled=True)
    txt_feat = lax.all_gather(after(sentences[0], txt), "dx", axis=0, tiled=True)

    features = (pictures[0], sentences[0])
    weights = (picture_weights, sentence_weights)
    img, near_rows, *first = early(spot, scal, features, weights, keys, [txt, txt_c])
    txt_b = exchange(after(txt_a, txt_y1, txt_y2), "lz", 3)
    img_a = exchange(img, "lz", 1)
    img_c = exchange(after(img, txt_a, txt_y1, txt_y2), "lc", 1)
    total, acc, mid_rows = image_tiles(
        scal, img, first[0], first[5], first[6], [after(txt_y1, img_c), txt_y2, txt_a]
    )
    img_part = (total, *first[1:3], first[5], acc)
    img_n = after(img, img_c, acc)
    img_y2 = exchange(img_n, "ly", 2)
    img_y1 = exchange(img_n, "ly", 1)
    img_b = exchange(img_a, "lz", 3)

    count = 2 * QUADS * lax.axis_size("dz") * ways

    def turn(array, axis, step):
        size = lax.axis_size(axis)
        return lax.ppermute(array, axis, [(i, (i + step) % size) for i in range(size)])

    def columns(outs):
        return [outs[0]] + [turn(out, "dx", step) for step, out in enumerate(outs) if step]

    txt_total = middle(
        scal, txt, first[5], near_rows, mid_rows, img, img_c, img_y1, img_y2, img_a
    )
    last = after(txt_b, img_feat, img_a, img_c, txt_total)
    *img_outs, far_rows = late(
        True, ways, spot, scal, img, img_part, [last]
    )
    img_outs = list(lax.optimization_barrier((*img_outs, img_y1, img_y2))[:-2])
    img_cols = columns(img_outs)
    txt_part = (txt_total, *first[3:5], first[5], first[5])
    last = after(img_b, img_cols[1], img_cols[3], txt_total)
    outs = late(False, ways, spot, scal, txt, txt_part, [far_rows, last])
    txt_cols = columns(outs)
    img_kept, img_given = heads(True, spot, after(img_feat, outs[0], txt_feat), img_cols)
    img_taken = exchange(img_given, "lc", 1)
    txt_kept, txt_given = heads(False, spot, txt_feat, txt_cols)
    txt_taken = exchange(txt_given, "lc", 1)
    sums = mix(img_kept, img_taken, txt_kept, txt_taken)
    sums = lax.all_to_all(sums, ("ly", "lz", "dz"), 0, 0, tiled=True)
    grad_img, grad_txt, stats = final(count, sums)
    return grad_img, grad_txt, stats


def solution(mesh):
    split = Mesh(mesh.devices.reshape(4, 4, 2, 2, 4), ("ly", "lz", "lc", "dz", "dx"))
    dp = ("dz", "dx")
    return jax.shard_map(
        body,
        mesh=split,
        in_specs=(P(dp, LOSS, None), P(dp, LOSS, None), P(dp, LOSS), P(), P(), P(), P()),
        out_specs=(P(LOSS, dp), P(LOSS, dp), P()),
        check_vma=False,
    )
```

```python
import functools

import jax
import jax.numpy as jnp
from jax import lax
from jax.experimental import pallas as pl
from jax.experimental.pallas import tpu as pltpu
from jax.sharding import Mesh, PartitionSpec as P

EPSILON = 1e-06
LOSS = ("ly", "lz", "lc")
ROWS = 128
WIDTH = 1152
KEY_ROWS = 16
CHUNK = 36
SLOT = 40
COLS = 144
LANES = 128
TAIL = COLS - LANES
QUADS = 16
STATS = 112
DEPTH = 128
PIECES = WIDTH // DEPTH
SLAB = SLOT + 8
F32 = jnp.float32
BF16 = jnp.bfloat16

VMEM = pl.BlockSpec(memory_space=pltpu.VMEM)
SMEM = pl.BlockSpec(memory_space=pltpu.SMEM)


def params(megabytes):
    return pltpu.CompilerParams(vmem_limit_bytes=megabytes * 2**20)


def cost(flops, moved):
    return pl.CostEstimate(flops=flops, bytes_accessed=moved, transcendentals=0)


def exchange(array, axis, apart):
    return lax.ppermute(array, axis, [(i, i ^ apart) for i in range(lax.axis_size(axis))])


def after(array, *others):
    return lax.optimization_barrier((array, *others))[0]


def nt(a, b):
    return lax.dot_general(a, b, (((1,), (1,)), ((), ())), preferred_element_type=F32)


def mm(a, b):
    return jnp.dot(a, b, preferred_element_type=F32)


def project_kernel(x_hbm, w_hbm, key_hbm, out_ref, x, w, key, sems):
    copies = [
        pltpu.make_async_copy(x_hbm, x, sems.at[0]),
        pltpu.make_async_copy(key_hbm, key, sems.at[1]),
    ]
    for k in range(PIECES):
        span = pl.ds(k * DEPTH, DEPTH)
        copies.append(pltpu.make_async_copy(w_hbm.at[span], w.at[span], sems.at[2 + k]))
    for copy in copies:
        copy.start()
    copies[0].wait()
    u = jnp.zeros((ROWS, WIDTH), F32)
    for k in range(PIECES):
        copies[2 + k].wait()
        span = slice(k * DEPTH, (k + 1) * DEPTH)
        u += mm(x[:, span], w[span])
    copies[1].wait()
    write_payload(out_ref, u / lengths(u), key[...])


def lengths(u):
    return jnp.sqrt(jnp.sum(u * u, axis=1, keepdims=True) + EPSILON)


def project(x, w, keys):
    return pl.pallas_call(
        project_kernel,
        in_specs=[pl.BlockSpec(memory_space=pltpu.HBM)] * 3,
        out_specs=VMEM,
        out_shape=jax.ShapeDtypeStruct((ROWS + KEY_ROWS, WIDTH), BF16),
        scratch_shapes=[
            pltpu.VMEM((ROWS, WIDTH), BF16),
            pltpu.VMEM((WIDTH, WIDTH), BF16),
            pltpu.VMEM((1, ROWS), jnp.int32),
            pltpu.SemaphoreType.DMA((2 + PIECES,)),
        ],
        compiler_params=params(56),
        cost_estimate=cost(2 * ROWS * WIDTH * WIDTH, 4 * 2**20),
    )(x, w, keys)


def temperature(heat_log):
    return jnp.exp(jnp.full((1, 1), heat_log[0], F32))


def caption_row(block):
    digits = block[ROWS:, :LANES].astype(F32)
    return digits[0:1] * 128.0 + digits[1:2]


def add_tiles(with_stats, heat, shift, mine, key_col, pairs, total, sums):
    for block, key_row in pairs:
        vec = block[:ROWS, :]
        same = key_col == key_row
        sim = nt(mine, vec)
        logits = heat * sim + shift
        z = jnp.where(same, -logits, logits)
        t = jnp.exp(-jnp.abs(z))
        q = 1.0 / (1.0 + t)
        sig = jnp.where(z >= 0, q, t * q)
        g = jnp.where(same, -sig, sig) * (1.0 / ROWS)
        total += mm(g.astype(BF16), vec)
        if with_stats:
            new = (jnp.maximum(z, 0.0) + jnp.log1p(t), g * sim, g)
            sums = [old + add for old, add in zip(sums, new)]
    return total, sums


def pair_up(blocks, rows_ref):
    pairs = []
    for k, block in enumerate(blocks):
        key_row = caption_row(block)
        rows_ref[k] = jnp.broadcast_to(key_row, (8, LANES))
        pairs.append((block, key_row))
    return pairs


def write_payload(out_ref, unit, key):
    digit = jnp.broadcast_to(key, (KEY_ROWS, ROWS))
    row = lax.broadcasted_iota(jnp.int32, (KEY_ROWS, ROWS), 0)
    digit = jnp.where(row == 0, digit >> 7, jnp.where(row == 1, digit & 127, 0))
    out_ref[:ROWS, :] = unit.astype(BF16)
    out_ref[ROWS:, :] = jnp.zeros((KEY_ROWS, WIDTH), BF16)
    out_ref[ROWS:, :ROWS] = digit.astype(F32).astype(BF16)


def early_kernel(spot, heat_log, shift, xs, xt, ws_hbm, wt_hbm, key, *refs):
    *blocks, own, rows_ref, total_ref, unit_img, len_img, unit_txt, len_txt = refs[:-4]
    key_ref, sum_ref, w, sems = refs[-4:]
    copies = [
        pltpu.make_async_copy(ws_hbm, w.at[0], sems.at[0]),
        pltpu.make_async_copy(wt_hbm, w.at[1], sems.at[1]),
    ]
    for copy in copies:
        copy.start()
    key_col = jnp.broadcast_to(key[...].astype(F32), (ROWS, ROWS)).T
    key_ref[...] = key_col
    towers = ((xs, unit_img, len_img), (xt, unit_txt, len_txt))

    def norm(t):
        x, unit_ref, len_ref = towers[t]
        copies[t].wait()
        u = mm(x[...], w[t])
        length = lengths(u)
        unit_ref[...] = u / length
        len_ref[...] = jnp.broadcast_to(length, len_ref.shape)

    norm(0)
    own[...] = unit_img[...].astype(BF16)
    zero = jnp.zeros((ROWS, ROWS), F32)
    total, sums = add_tiles(
        True,
        temperature(heat_log),
        shift[0],
        own[...],
        key_col,
        pair_up(blocks, rows_ref),
        jnp.zeros((ROWS, WIDTH), F32),
        [zero] * 3,
    )
    total_ref[...] = total
    for k in range(3):
        sum_ref[k] = sums[k]
    norm(1)


def early(spot, scal, features, weights, keys, blocks):
    shapes = [(ROWS, WIDTH), (ROWS, LANES)]
    shapes = [(ROWS, WIDTH), *shapes, *shapes, (ROWS, ROWS), (3, ROWS, ROWS)]
    outs = [
        jax.ShapeDtypeStruct((ROWS, WIDTH), BF16),
        jax.ShapeDtypeStruct((len(blocks), 8, LANES), F32),
    ] + [jax.ShapeDtypeStruct(shape, F32) for shape in shapes]
    hbm = pl.BlockSpec(memory_space=pltpu.HBM)
    return pl.pallas_call(
        early_kernel,
        in_specs=[SMEM] * 3 + [VMEM] * 2 + [hbm] * 2 + [VMEM] * (1 + len(blocks)),
        out_specs=[VMEM] * len(outs),
        out_shape=outs,
        scratch_shapes=[pltpu.VMEM((2, WIDTH, WIDTH), BF16), pltpu.SemaphoreType.DMA((2,))],
        compiler_params=params(56),
        cost_estimate=cost(4 * 5 * ROWS * ROWS * WIDTH, 8 * 2**20),
    )(spot, *scal, *features, *weights, keys, *blocks)


def image_kernel(heat_log, shift, own, total_ref, key, acc, *refs):
    *blocks, out_ref, sum_ref, rows_ref = refs
    total, sums = add_tiles(
        True,
        temperature(heat_log),
        shift[0],
        own[...],
        key[...],
        pair_up(blocks, rows_ref),
        total_ref[...],
        [acc[k] for k in range(3)],
    )
    out_ref[...] = total
    for k in range(3):
        sum_ref[k] = sums[k]


def image_tiles(scal, own, total, key, acc, blocks):
    shapes = [(ROWS, WIDTH), (3, ROWS, ROWS), (len(blocks), 8, LANES)]
    return pl.pallas_call(
        image_kernel,
        in_specs=[SMEM] * 2 + [VMEM] * (4 + len(blocks)),
        out_specs=[VMEM] * 3,
        out_shape=[jax.ShapeDtypeStruct(shape, F32) for shape in shapes],
        compiler_params=params(56),
        cost_estimate=cost(4 * 3 * ROWS * ROWS * WIDTH, 4 * 2**20),
    )(*scal, own, total, key, acc, *blocks)


def middle_kernel(heat_log, shift, own, key, near_rows, far_rows, *refs):
    *blocks, total_ref = refs
    rows = [near_rows[0], near_rows[1], far_rows[0], far_rows[1], far_rows[2]]
    zero = jnp.zeros((ROWS, ROWS), F32)
    total, _ = add_tiles(
        False,
        temperature(heat_log),
        shift[0],
        own[:ROWS, :],
        key[...],
        [(block, row[0:1]) for block, row in zip(blocks, rows)],
        jnp.zeros((ROWS, WIDTH), F32),
        [zero] * 3,
    )
    total_ref[...] = total


def middle(scal, *arrays):
    return pl.pallas_call(
        middle_kernel,
        in_specs=[SMEM] * 2 + [VMEM] * len(arrays),
        out_specs=VMEM,
        out_shape=jax.ShapeDtypeStruct((ROWS, WIDTH), F32),
        compiler_params=params(56),
        cost_estimate=cost(4 * 5 * ROWS * ROWS * WIDTH, 4 * 2**20),
    )(*scal, *arrays)


def late_kernel(with_stats, ways, count, spot, heat_log, shift, own, *refs):
    total_ref, unit, length, key, acc, *refs = refs
    blocks, outs, held = refs[:count], refs[count:-1], refs[-1]
    heat = temperature(heat_log)
    if with_stats:
        *outs, rows_ref = outs
        pairs = pair_up(blocks, rows_ref)
    else:
        rows, block = blocks
        pairs = [(block, rows[0][0:1])]
    total, sums = add_tiles(
        with_stats,
        heat,
        shift[0],
        own[:ROWS, :],
        key[...],
        pairs,
        total_ref[...],
        [acc[k] for k in range(3)] if with_stats else [acc[...]] * 3,
    )
    total = total * heat
    u = unit[...]
    inner = jnp.sum(u * total, axis=1, keepdims=True)
    du = (total - u * inner) / length[:, :1]
    held[...] = du.T.astype(BF16).reshape(held.shape)
    if with_stats:
        def full(x):
            return jnp.sum(jnp.sum(x, axis=1, keepdims=True), axis=0, keepdims=True)

        lane = lax.broadcasted_iota(jnp.int32, (KEY_ROWS, LANES), 1)
        row = lax.broadcasted_iota(jnp.int32, (KEY_ROWS, LANES), 0)
        kind = lane % 3
        value = jnp.where(
            kind == 0,
            full(sums[0]) * (1.0 / ROWS),
            jnp.where(kind == 1, full(sums[1]) * heat, full(sums[2])),
        )
        value = jnp.where((row == 0) & (lane < 9), value, 0.0)
        high = value.astype(BF16).astype(F32)
        middle = (value - high).astype(BF16).astype(F32)
        low = value - high - middle
        parts = jnp.where(lane < 3, high, jnp.where(lane < 6, middle, low)).astype(BF16)
        for out in outs:
            out[2 * COLS :, :] = parts
    for step, out in enumerate(outs):
        w = lax.rem(spot[0] + step, ways)
        for h in range(2):
            out[h * COLS : (h + 1) * COLS, :] = held[h * ways + w]


def late(with_stats, ways, spot, scal, own, partial, blocks):
    rows = 2 * COLS + (KEY_ROWS if with_stats else 0)
    shapes = [jax.ShapeDtypeStruct((rows, ROWS), BF16)] * ways
    if with_stats:
        shapes.append(jax.ShapeDtypeStruct((len(blocks), 8, LANES), F32))
    return pl.pallas_call(
        functools.partial(late_kernel, with_stats, ways, len(blocks)),
        in_specs=[SMEM] * 3 + [VMEM] * (6 + len(blocks)),
        out_specs=[VMEM] * len(shapes),
        out_shape=shapes,
        scratch_shapes=[pltpu.VMEM((2 * ways, COLS, ROWS), BF16)],
        compiler_params=params(56),
        cost_estimate=cost(4 * 2 * ROWS * ROWS * WIDTH, 4 * 2**20),
    )(spot, *scal, own, *partial, *blocks)


def head_kernel(with_stats, spot, feat, *refs):
    spreads, (kept, given, held) = refs[:-3], refs[-3:]
    ways = len(spreads)
    total = jnp.zeros((2 * COLS, feat.shape[1]), F32)
    for step, spread in enumerate(spreads):
        source = lax.rem(spot[0] + ways - step, ways)
        rows = feat[pl.ds(pl.multiple_of(source * ROWS, ROWS), ROWS), :]
        total += mm(spread[: 2 * COLS, :], rows)
    spare = None
    if with_stats:
        parts = jnp.zeros((KEY_ROWS, LANES), F32)
        for spread in spreads:
            parts += spread[2 * COLS :, :].astype(F32)
        lane = lax.broadcasted_iota(jnp.int32, (8, LANES), 1)
        row = lax.broadcasted_iota(jnp.int32, (8, LANES), 0)
        place = lane - STATS
        summed = jnp.zeros((8, LANES), F32)
        for k in range(3):
            number = jnp.sum(
                jnp.where((lane[:1] % 3 == k) & (lane[:1] < 9), parts[0:1], 0.0),
                axis=1,
                keepdims=True,
            )
            summed = jnp.where(place % 3 == k, number, summed)
        value = jnp.where((row == spot[1]) & (place >= 0) & (place < 9), summed, 0.0)
        high = value.astype(BF16).astype(F32)
        middle = (value - high).astype(BF16).astype(F32)
        low = value - high - middle
        spare = jnp.where(place < 3, high, jnp.where(place < 6, middle, low))
    for h in range(2):
        main = total[h * COLS : h * COLS + LANES, :].T
        rest = total[h * COLS + LANES : (h + 1) * COLS, :]
        for m in range(QUADS):
            for side in range(2):
                start = (2 * m + side) * CHUNK
                target = held.at[side, 2 * m + h]
                target[:CHUNK, :] = main[start : start + CHUNK]
                target[CHUNK:SLOT, :] = jnp.zeros((SLOT - CHUNK, LANES), F32)
                target[SLOT:, :] = jnp.zeros((8, LANES), F32) if spare is None else spare
                for k in range(2):
                    target[SLOT:, 64 * k : 64 * k + CHUNK] = rest[
                        8 * k : 8 * k + 8, start : start + CHUNK
                    ]
    kept[...] = held[spot[1]]
    given[...] = held[1 - spot[1]].astype(BF16)


def heads(with_stats, spot, feat, spreads):
    shape = (2 * QUADS, SLOT + 8, LANES)
    return pl.pallas_call(
        functools.partial(head_kernel, with_stats),
        in_specs=[SMEM] + [VMEM] * (1 + len(spreads)),
        out_specs=[VMEM, VMEM],
        out_shape=[jax.ShapeDtypeStruct(shape, F32), jax.ShapeDtypeStruct(shape, BF16)],
        scratch_shapes=[pltpu.VMEM((2, *shape), F32)],
        compiler_params=params(24 if with_stats else 56),
        cost_estimate=cost(2 * 4 * ROWS * 2 * COLS * feat.shape[1], 4 * 2**20),
    )(spot, feat, *spreads)


def mix_kernel(kept_img, taken_img, kept_txt, taken_txt, out):
    out[:, :SLAB, :] = (kept_img[...] + taken_img[...].astype(F32)).astype(BF16)
    out[:, SLAB:, :] = (kept_txt[...] + taken_txt[...].astype(F32)).astype(BF16)


def mix(*arrays):
    return pl.pallas_call(
        mix_kernel,
        in_specs=[VMEM] * 4,
        out_specs=VMEM,
        out_shape=jax.ShapeDtypeStruct((2 * QUADS, 2 * SLAB, LANES), BF16),
        compiler_params=params(16),
        cost_estimate=cost(4 * QUADS * SLAB * LANES, 2**20),
    )(*arrays)


def final_kernel(count, parts, out_img, out_txt, stats):
    both = jnp.sum(parts[...].astype(F32), axis=0)
    for out, total in ((out_img, both[:SLAB]), (out_txt, both[SLAB:])):
        out[:, :LANES] = total[:CHUNK]
        rest = total[SLOT:, :].T
        out[:, LANES : LANES + 8] = rest[:CHUNK]
        out[:, LANES + 8 :] = rest[64 : 64 + CHUNK]
    place = lax.broadcasted_iota(jnp.int32, (1, LANES), 1) - STATS
    row = both[SLOT : SLOT + 1] + both[SLOT + 1 : SLOT + 2]
    for k in range(3):
        chosen = jnp.where((place % 3 == k) & (place >= 0) & (place < 9), row, 0.0)
        stats[k] = jnp.sum(chosen) * (1.0 / count)


def final(count, parts):
    grad = jax.ShapeDtypeStruct((CHUNK, COLS), F32)
    return pl.pallas_call(
        functools.partial(final_kernel, count),
        in_specs=[VMEM],
        out_specs=[VMEM, VMEM, SMEM],
        out_shape=[grad, grad, jax.ShapeDtypeStruct((3,), F32)],
        compiler_params=params(8),
        cost_estimate=cost(4 * QUADS * SLAB * LANES, 2**20),
    )(parts)


def body(pictures, sentences, keys, picture_weights, sentence_weights, heat_log, shift_value):
    ways = lax.axis_size("dx")
    spot = jnp.stack([lax.axis_index(axis) for axis in ("dx", "lc")]).astype(jnp.int32)
    scal = (heat_log, shift_value)
    txt = project(sentences[0], sentence_weights, keys)
    txt_a = exchange(txt, "lz", 1)
    txt_y2 = exchange(txt, "ly", 2)
    txt_y1 = exchange(txt, "ly", 1)
    txt_c = exchange(txt, "lc", 1)
    img_feat = lax.all_gather(after(pictures[0], txt), "dx", axis=0, tiled=True)
    txt_feat = lax.all_gather(after(sentences[0], txt), "dx", axis=0, tiled=True)

    features = (pictures[0], sentences[0])
    weights = (picture_weights, sentence_weights)
    img, near_rows, *first = early(spot, scal, features, weights, keys, [txt, txt_c])
    txt_b = exchange(after(txt_a, txt_y1, txt_y2), "lz", 3)
    img_a = exchange(img, "lz", 1)
    img_c = exchange(after(img, txt_a, txt_y1, txt_y2), "lc", 1)
    total, acc, mid_rows = image_tiles(
        scal, img, first[0], first[5], first[6], [after(txt_y1, img_c), txt_y2, txt_a]
    )
    img_part = (total, *first[1:3], first[5], acc)
    img_n = after(img, img_c, acc)
    img_y2 = exchange(img_n, "ly", 2)
    img_y1 = exchange(img_n, "ly", 1)
    img_b = exchange(img_a, "lz", 3)

    count = 2 * QUADS * lax.axis_size("dz") * ways

    def turn(array, axis, step):
        size = lax.axis_size(axis)
        return lax.ppermute(array, axis, [(i, (i + step) % size) for i in range(size)])

    def columns(outs):
        return [outs[0]] + [turn(out, "dx", step) for step, out in enumerate(outs) if step]

    last = after(txt_b, img_feat, img_a, img_c)
    *img_outs, far_rows = late(
        True, ways, spot, scal, img, img_part, [last]
    )
    img_outs = list(lax.optimization_barrier((*img_outs, img_y1, img_y2))[:-2])
    img_cols = columns(img_outs)
    txt_total = middle(
        scal, txt, first[5], near_rows, mid_rows, img, img_c, img_y1, img_y2, img_a
    )
    txt_part = (txt_total, *first[3:5], first[5], first[5])
    last = after(img_b, img_cols[1], img_cols[3], txt_total)
    outs = late(False, ways, spot, scal, txt, txt_part, [far_rows, last])
    txt_cols = columns(outs)
    img_kept, img_given = heads(True, spot, after(img_feat, outs[0], txt_feat), img_cols)
    img_taken = exchange(img_given, "lc", 1)
    txt_kept, txt_given = heads(False, spot, txt_feat, txt_cols)
    txt_taken = exchange(txt_given, "lc", 1)
    sums = mix(img_kept, img_taken, txt_kept, txt_taken)
    sums = lax.all_to_all(sums, ("ly", "lz", "dz"), 0, 0, tiled=True)
    grad_img, grad_txt, stats = final(count, sums)
    return grad_img, grad_txt, stats


def solution(mesh):
    split = Mesh(mesh.devices.reshape(4, 4, 2, 2, 4), ("ly", "lz", "lc", "dz", "dx"))
    dp = ("dz", "dx")
    return jax.shard_map(
        body,
        mesh=split,
        in_specs=(P(dp, LOSS, None), P(dp, LOSS, None), P(dp, LOSS), P(), P(), P(), P()),
        out_specs=(P(LOSS, dp), P(LOSS, dp), P()),
        check_vma=False,
    )
```
